32 devices in a mesh: expert: 8 (over z, x), hidden: 4 (over y, core).
Axes of the slice: x: 2, y: 2, z: 4, core: 2. Of those that a mesh axis runs over, the one named last changes fastest.
Arguments:
- token_ids: int32 [8, 1024], P('expert'), may hold values from 0 to 50303
- target_ids: int32 [8, 1024], P('expert'), may hold values from 0 to 50303
- doc_segments: int32 [8, 1024], P('expert'), may hold values from 0 to 7, never falling along the last dimension, each value on 1 to 512 neighbouring positions
- hash_experts: int32 [50304], replicated, may hold values from 0 to 7
- embed_table: float32 [50304, 768], P(('expert', 'hidden')), may hold values from -0.3 to 0.3
- embed_first: float32 [50304, 768], P(('expert', 'hidden')), may hold values from -3.5762787e-07 to 3.5762787e-07
- embed_second: float32 [50304, 768], P(('expert', 'hidden')), may hold values from 1.6509235e-14 to 1.4790959e-10
- attn_in: float32 [768, 3, 768], P('expert', None, 'hidden'), may hold values from -0.21875 to 0.21875
- attn_in_first: float32 [768, 3, 768], P('expert', None, 'hidden'), may hold values from -3.5762787e-07 to 3.5762787e-07
- attn_in_second: float32 [768, 3, 768], P('expert', None, 'hidden'), may hold values from 1.6509235e-14 to 6.730688e-14
- attn_out: float32 [768, 768], P('expert', 'hidden'), may hold values from -0.875 to 0.875
- attn_out_first: float32 [768, 768], P('expert', 'hidden'), may hold values from -3.5762787e-07 to 3.5762787e-07
- attn_out_second: float32 [768, 768], P('expert', 'hidden'), may hold values from 1.6509235e-14 to 6.730688e-14
- expert_in: float32 [8, 768, 3072], P('expert', None, 'hidden'), may hold values from -0.21875 to 0.21875
- expert_in_first: float32 [8, 768, 3072], P('expert', None, 'hidden'), may hold values from -3.5762787e-07 to 3.5762787e-07
- expert_in_second: float32 [8, 768, 3072], P('expert', None, 'hidden'), may hold values from 1.6509235e-14 to 6.730688e-14
- expert_out: float32 [8, 3072, 768], P('expert', 'hidden'), may hold values from -0.109375 to 0.109375
- expert_out_first: float32 [8, 3072, 768], P('expert', 'hidden'), may hold values from -3.5762787e-07 to 3.5762787e-07
- expert_out_second: float32 [8, 3072, 768], P('expert', 'hidden'), may hold values from 1.6509235e-14 to 6.730688e-14
- norm_gains: float32 [768, 3], P('expert'), may hold values from 0.5 to 1.5
- gains_first: float32 [768, 3], P('expert'), may hold values from -3.8146973e-06 to 3.8146973e-06
- gains_second: float32 [768, 3], P('expert'), may hold values from 1.6509234e-12 to 6.730688e-12
Outputs:
- loss_value: float32 [], replicated
- clip_norm: float32 [], replicated
- embed_new: float32 [50304, 768], P(('expert', 'hidden'))
- embed_first_new: float32 [50304, 768], P(('expert', 'hidden'))
- embed_second_new: float32 [50304, 768], P(('expert', 'hidden'))
- attn_in_new: float32 [768, 3, 768], P('expert', None, 'hidden')
- attn_in_first_new: float32 [768, 3, 768], P('expert', None, 'hidden')
- attn_in_second_new: float32 [768, 3, 768], P('expert', None, 'hidden')
- attn_out_new: float32 [768, 768], P('expert', 'hidden')
- attn_out_first_new: float32 [768, 768], P('expert', 'hidden')
- attn_out_second_new: float32 [768, 768], P('expert', 'hidden')
- expert_in_new: float32 [8, 768, 3072], P('expert', None, 'hidden')
- expert_in_first_new: float32 [8, 768, 3072], P('expert', None, 'hidden')
- expert_in_second_new: float32 [8, 768, 3072], P('expert', None, 'hidden')
- expert_out_new: float32 [8, 3072, 768], P('expert', 'hidden')
- expert_out_first_new: float32 [8, 3072, 768], P('expert', 'hidden')
- expert_out_second_new: float32 [8, 3072, 768], P('expert', 'hidden')
- gains_new: float32 [768, 3], P('expert')
- gains_first_new: float32 [768, 3], P('expert')
- gains_second_new: float32 [768, 3], P('expert')
The draws below stay inside these ranges and needn't reach their ends.
All inputs are finite; a program needn't handle non-finite values.
Results may differ from the reference program's by a relative error of at most 0.0025.
The reference program's roundings to bfloat16 on the way (of `normed_one`, `qkv`, `probability`, `attended`, `normed_two`, `active`, `expert_result` and `final_rows`) count: a program that leaves them out, or rounds other values in their place, can miss the bound.
Values may be sent and summed in bfloat16 or wider, within the bound.
No kernel may reach another device: no remote copies, remote signals or barrier semaphores. Data moves between devices by JAX's collectives and lax.ppermute only.
A program may use at most 256 MiB of HBM per device.

```python
import math
import jax
import jax.numpy as jnp
import numpy as np
from jax import lax

D = 768
HEADS = 12
HD = 64
FF = 3072
VOCAB = 50304
SEQ = 1024
DOCS_ROW = 8
DOC_MOST = 512
STEP = 7
EXPERTS = 8
ROWS = 8
TOKD = 1024
CAP = 192
PARAMS = 78743808
N_EXPERT = 8


def draw_embed_second(key, part):
    key = jax.random.fold_in(key, 11)
    spread = jax.random.uniform(key, (VOCAB, D), jnp.float32, 0.0, 1.0)
    level = 1.3e-06 / PARAMS * jnp.exp(spread * math.log(4.0))
    return level.astype(jnp.float32)


def place_ends(values, rng, least, top_value):
    place = [jax.random.randint(jax.random.fold_in(rng, axis), (), 0, length) for axis, length in enumerate(values.shape)]
    main_axis = values.shape.index(max(values.shape))
    neighbour = place[:main_axis] + [(place[main_axis] + 1) % values.shape[main_axis]] + place[main_axis + 1:]
    return values.at[tuple(place)].set(least).at[tuple(neighbour)].set(top_value)


def levels(key, shape, cuts, low, largest):
    level, own = 1.0, jax.random.fold_in(key, 6)
    for dim, parts in cuts:
        heights = jnp.exp(jax.random.uniform(jax.random.fold_in(own, dim), (parts,), jnp.float32, low / len(cuts), largest / len(cuts)))
        level = level * jnp.repeat(heights, shape[dim] // parts).reshape([-1 if axis == dim else 1 for axis in range(len(shape))])
    return level


def rank_bounds(number_of, skew):
    portions = [(1 << 20) // math.isqrt(standing ** skew) + 1 for standing in range(1, number_of + 1)]
    width = 1 + sum(portions) // (1 << 30)
    return np.cumsum(np.array([max(1, weight // width) for weight in portions]))


def ranked_ids(stream_key, extent, count, skew):
    listing = rank_bounds(count, skew)
    ticket = jax.random.randint(jax.random.fold_in(stream_key, 1), extent, 0, int(listing[count - 1]))
    standing = jnp.searchsorted(jnp.asarray(listing, jnp.int32), ticket, side="right")
    return jax.random.permutation(jax.random.fold_in(stream_key, 2), count)[standing].astype(jnp.int32)


def length_profile(count, total, reach, slope):
    loads = [(1 << 20) // math.isqrt(standing ** slope) + 1 for standing in range(2, count + 1)]
    spare, counts = total - reach - (count - 1), [1] * (count - 1)
    while spare > 0:
        movable = [i for i in range(count - 1) if counts[i] < reach]
        pool, remaining = sum([loads[i] for i in movable]), spare
        for i in movable:
            addition = min(reach - counts[i], max(1, remaining * loads[i] // pool), spare)
            counts[i] = counts[i] + addition
            spare = spare - addition
    return np.array([reach] + counts)


def uneven_parts(key, amount, total, reach, lean):
    if amount == 2:
        one = jax.random.randint(key, (), max(1, total - reach), min(reach, total - 1) + 1)
        return jnp.stack([one, total - one])
    tallies = jnp.asarray(length_profile(amount, total, reach, lean), jnp.int32)
    pairs = (amount - 1) // 2
    source_of, receiver = tallies[1:1 + 2 * pairs:2], tallies[2:2 + 2 * pairs:2]
    slack = jnp.minimum(source_of - 1, reach - receiver)
    passed = jax.random.randint(jax.random.fold_in(key, 1), (pairs,), 0, 1 << 20) % (slack + 1)
    tallies = tallies.at[1:1 + 2 * pairs:2].set(source_of - passed).at[2:2 + 2 * pairs:2].set(receiver + passed)
    return tallies[jax.random.permutation(jax.random.fold_in(key, 2), amount)]


def scatter_about(rng, extent, width, limit, split=(), held_as=jnp.bfloat16):
    entries = jax.random.normal(rng, extent, jnp.float32) * width
    if len(split) > 0:
        entries = levels(rng, extent, split, -0.22, 0.18) * entries
    return jnp.clip(entries, min=-limit, max=limit).astype(held_as)


def setup_inputs(seed: int = 0) -> dict:
    seeds = jax.random.split(jax.random.key(seed), 23)
    return {
        "token_ids": place_ends(ranked_ids(seeds[0], (ROWS, SEQ), VOCAB, 2), jax.random.fold_in(seeds[0], 3), 0, VOCAB - 1).astype(jnp.int32),
        "target_ids": place_ends(ranked_ids(seeds[1], (ROWS, SEQ), VOCAB, 2), jax.random.fold_in(seeds[1], 3), 0, VOCAB - 1).astype(jnp.int32),
        "doc_segments": jax.vmap(lambda own: jnp.searchsorted(jnp.cumsum(uneven_parts(own, DOCS_ROW, SEQ, DOC_MOST, 2)), jnp.arange(SEQ), side="right"))(jax.random.split(seeds[2], ROWS)).reshape((ROWS, SEQ)).astype(jnp.int32),
        "hash_experts": place_ends(jax.random.randint(seeds[3], (VOCAB,), 0, EXPERTS), jax.random.fold_in(seeds[3], 1), 0, EXPERTS - 1).astype(jnp.int32),
        "embed_table": scatter_about(seeds[4], (VOCAB, D), 0.05, 0.3, ((0, 32),), jnp.float32),
        "embed_first": scatter_about(seeds[5], (VOCAB, D), (0.000555 * PARAMS ** -0.5), 3.5762786865234375e-07, ((0, 32),), jnp.float32),
        "embed_second": draw_embed_second(jax.random.fold_in(seeds[22], 71), 0),
        "attn_in": scatter_about(seeds[7], (D, 3, HEADS * HD), D ** -0.5, 0.21875, ((0, 8), (2, 4)), jnp.float32),
        "attn_in_first": scatter_about(seeds[8], (D, 3, HEADS * HD), (0.000555 * PARAMS ** -0.5), 3.5762786865234375e-07, ((0, 8), (2, 4)), jnp.float32),
        "attn_in_second": jnp.clip(jnp.exp(math.log(6.730687784461259e-14) - 1.40534253 * jax.random.uniform(seeds[9], (D, 3, HEADS * HD), jnp.float32) ** levels(seeds[9], (D, 3, HEADS * HD), ((0, 8), (2, 4)), -0.2, 0.2)), 1.650923457186329e-14, 6.730687784461259e-14),
        "attn_out": scatter_about(seeds[10], (D, HEADS * HD), (D // 16) ** -0.5, 0.875, ((0, 8), (1, 4)), jnp.float32),
        "attn_out_first": scatter_about(seeds[11], (D, HEADS * HD), (0.000555 * PARAMS ** -0.5), 3.5762786865234375e-07, ((0, 8), (1, 4)), jnp.float32),
        "attn_out_second": jnp.clip(jnp.exp(math.log(6.730687784461259e-14) - 1.40534253 * jax.random.uniform(seeds[12], (D, HEADS * HD), jnp.float32) ** levels(seeds[12], (D, HEADS * HD), ((0, 8), (1, 4)), -0.2, 0.2)), 1.650923457186329e-14, 6.730687784461259e-14),
        "expert_in": scatter_about(seeds[13], (EXPERTS, D, FF), D ** -0.5, 0.21875, ((0, 8), (2, 4)), jnp.float32),
        "expert_in_first": scatter_about(seeds[14], (EXPERTS, D, FF), (0.000555 * PARAMS ** -0.5), 3.5762786865234375e-07, ((0, 8), (2, 4)), jnp.float32),
        "expert_in_second": jnp.clip(jnp.exp(math.log(6.730687784461259e-14) - 1.40534253 * jax.random.uniform(seeds[15], (EXPERTS, D, FF), jnp.float32) ** levels(seeds[15], (EXPERTS, D, FF), ((0, 8), (2, 4)), -0.2, 0.2)), 1.650923457186329e-14, 6.730687784461259e-14),
        "expert_out": scatter_about(seeds[16], (EXPERTS, FF, D), FF ** -0.5, 0.109375, ((0, 8), (1, 4)), jnp.float32),
        "expert_out_first": scatter_about(seeds[17], (EXPERTS, FF, D), (0.000555 * PARAMS ** -0.5), 3.5762786865234375e-07, ((0, 8), (1, 4)), jnp.float32),
        "expert_out_second": jnp.clip(jnp.exp(math.log(6.730687784461259e-14) - 1.40534253 * jax.random.uniform(seeds[18], (EXPERTS, FF, D), jnp.float32) ** levels(seeds[18], (EXPERTS, FF, D), ((0, 8), (1, 4)), -0.2, 0.2)), 1.650923457186329e-14, 6.730687784461259e-14),
        "norm_gains": jnp.clip(1.0 + 0.1 * jax.random.normal(seeds[19], (D, 3), jnp.float32), 0.5, 1.5),
        "gains_first": scatter_about(seeds[20], (D, 3), (0.00555 * PARAMS ** -0.5), 3.814697265625e-06, ((0, 8),), jnp.float32),
        "gains_second": jnp.clip(jnp.exp(math.log(6.730688055511802e-12) - 1.4053426 * jax.random.uniform(seeds[21], (D, 3), jnp.float32) ** levels(seeds[21], (D, 3), ((0, 8),), -0.2, 0.2)), 1.6509234300812747e-12, 6.730688055511802e-12),
    }


@jax.custom_vjp
def low(v):
    return lax.optimization_barrier(v.astype(jnp.bfloat16)).astype(jnp.float32)

@jax.custom_vjp
def low_back(v):
    return v

def low_keep(v):
    return (low(v), None)

def low_pass(kept, grad):
    return (grad,)

def back_keep(v):
    return (v, None)

def back_low(kept, grad):
    return (low(grad),)
low.defvjp(low_keep, low_pass)
low_back.defvjp(back_keep, back_low)
EPS_NORM = 1e-06
BETA_ONE = 0.9
BETA_TWO = 0.95
ADAM_EPS = 1e-08
RATE_MATRIX = 0.05
RATE_GAIN = 0.3
DECAY = 0.1
CLIP_AT = 0.005
HIGH = lax.Precision.HIGHEST

def both_ways(value):
    return low_back(low(value))

def rms_norm(rows_in, gain):
    return rows_in * lax.rsqrt(lax.optimization_barrier(jnp.mean(rows_in * rows_in, axis=-1, keepdims=True)) + EPS_NORM) * gain

def token_weights(doc_segments):

    def row_counts(segment):
        same_doc = (segment[:, None] == segment[None, :]).astype(jnp.float32)
        return 1.0 / lax.optimization_barrier(jnp.sum(same_doc, axis=1))
    return lax.map(row_counts, doc_segments) / (ROWS * DOCS_ROW)

def places(expert_ids):
    onehot = (expert_ids[..., None] == jnp.arange(EXPERTS, dtype=jnp.int32)).astype(jnp.int32)
    before = jnp.cumsum(onehot, axis=1) - onehot
    slot_rank = lax.optimization_barrier(jnp.sum(before * onehot, axis=-1))
    return jnp.where(slot_rank < CAP, expert_ids * CAP + slot_rank, EXPERTS * CAP).astype(jnp.int32)

def row_attention(inputs):
    queries, key_rows, value_rows, segment = inputs
    scores = jnp.einsum('qhd,khd->hqk', queries, key_rows, precision=HIGH) * HD ** (-0.5)
    scores = low_back(scores)
    position = jnp.arange(SEQ)
    allowed = (position[:, None] >= position[None, :]) & (segment[:, None] == segment[None, :])
    scores = jnp.where(allowed[None], scores, -1e+30)
    row_peak = lax.optimization_barrier(jnp.max(scores, axis=-1, keepdims=True))
    exponent = jnp.exp(scores - row_peak)
    probability = exponent / lax.optimization_barrier(jnp.sum(exponent, axis=-1, keepdims=True))
    return jnp.einsum('hqk,khd->qhd', low(probability), value_rows, precision=HIGH)

def forward(params, token_ids, target_ids, doc_segments, hash_experts):
    embed_table, attn_in, attn_out, expert_in, expert_out, norm_gains = params
    table_low = low(embed_table)
    gain_low = low(norm_gains)
    embedded = table_low[token_ids] * D ** 0.5
    normed_one = low(rms_norm(embedded, gain_low[:, 0]))
    qkv = both_ways(jnp.einsum('rsd,dcf->rscf', normed_one, low(attn_in), precision=HIGH))
    queries = qkv[:, :, 0].reshape(ROWS, SEQ, HEADS, HD)
    key_rows = qkv[:, :, 1].reshape(ROWS, SEQ, HEADS, HD)
    value_rows = qkv[:, :, 2].reshape(ROWS, SEQ, HEADS, HD)
    attended = lax.map(jax.checkpoint(row_attention), (queries, key_rows, value_rows, doc_segments))
    attended = both_ways(attended.reshape(ROWS, SEQ, HEADS * HD))
    after_attn = embedded + low_back(jnp.einsum('rsf,df->rsd', attended, low(attn_out), precision=HIGH))
    normed_two = both_ways(rms_norm(after_attn, gain_low[:, 1]))
    expert_ids = hash_experts[token_ids].reshape(N_EXPERT, TOKD)
    slot_index = places(expert_ids)

    def fill_slots(rows_in, where_to):
        return jnp.zeros((EXPERTS * CAP + 1, D), rows_in.dtype).at[where_to].set(rows_in)[:-1]
    sent = jax.vmap(fill_slots)(normed_two.reshape(N_EXPERT, TOKD, D), slot_index)
    sent = sent.reshape(N_EXPERT, EXPERTS, CAP, D).transpose(1, 0, 2, 3).reshape(EXPERTS, N_EXPERT * CAP, D)
    pre_act = low_back(jnp.einsum('erd,edf->erf', sent, low(expert_in), precision=HIGH))
    active = low(jax.nn.gelu(pre_act, approximate=False))
    expert_result = both_ways(jnp.einsum('erf,efd->erd', active, low(expert_out), precision=HIGH))
    returned = expert_result.reshape(EXPERTS, N_EXPERT, CAP, D).transpose(1, 0, 2, 3).reshape(N_EXPERT, EXPERTS * CAP, D)
    returned = jnp.concatenate([returned, jnp.zeros((N_EXPERT, 1, D), returned.dtype)], axis=1)
    moe_rows = jax.vmap(lambda buffer, where_from: buffer[where_from])(returned, slot_index).reshape(ROWS, SEQ, D)
    after_moe = after_attn + moe_rows
    final_rows = low(rms_norm(after_moe, gain_low[:, 2]))
    weights = token_weights(doc_segments)

    def row_loss(inputs):
        row_hidden, row_target, row_weight = inputs
        logits = low_back(jnp.dot(row_hidden, table_low.T, precision=HIGH))
        row_peak = lax.optimization_barrier(jnp.max(logits, axis=-1, keepdims=True))
        log_total = row_peak[:, 0] + jnp.log(lax.optimization_barrier(jnp.sum(jnp.exp(logits - row_peak), axis=-1)))
        target_logit = jnp.take_along_axis(logits, row_target[:, None], axis=1)[:, 0]
        return jnp.sum((log_total - target_logit) * row_weight)
    return jnp.sum(lax.map(jax.checkpoint(row_loss), (final_rows, target_ids, weights)))

def adam_step(weight, first_moment, second_moment, gradient, step_rate, weight_decay):
    first_moment = BETA_ONE * first_moment + (1.0 - BETA_ONE) * gradient
    second_moment = BETA_TWO * second_moment + (1.0 - BETA_TWO) * gradient * gradient
    update = first_moment / (1.0 - BETA_ONE ** STEP) / (jnp.sqrt(second_moment / (1.0 - BETA_TWO ** STEP)) + ADAM_EPS)
    return (weight - step_rate * (update + weight_decay * weight), first_moment, second_moment)

def reference(token_ids, target_ids, doc_segments, hash_experts, embed_table, embed_first, embed_second, attn_in, attn_in_first, attn_in_second, attn_out, attn_out_first, attn_out_second, expert_in, expert_in_first, expert_in_second, expert_out, expert_out_first, expert_out_second, norm_gains, gains_first, gains_second):
    params = (embed_table, attn_in, attn_out, expert_in, expert_out, norm_gains)

    def objective(weights_in):
        return forward(weights_in, token_ids, target_ids, doc_segments, hash_experts)
    loss_value, pullback = jax.vjp(objective, params)
    grads = pullback(jnp.ones_like(loss_value))[0]
    squares = jnp.zeros((), jnp.float32)
    for grad_item in grads:
        squares = squares + jnp.sum(grad_item * grad_item)
    clip_norm = jnp.sqrt(squares)
    clip_scale = jnp.minimum(1.0, CLIP_AT / clip_norm)
    firsts = (embed_first, attn_in_first, attn_out_first, expert_in_first, expert_out_first, gains_first)
    seconds = (embed_second, attn_in_second, attn_out_second, expert_in_second, expert_out_second, gains_second)
    rates = (RATE_MATRIX, RATE_MATRIX, RATE_MATRIX, RATE_MATRIX, RATE_MATRIX, RATE_GAIN)
    decays = (DECAY, DECAY, DECAY, DECAY, DECAY, 0.0)
    updated = []
    for weight_index in range(6):
        updated.append(adam_step(params[weight_index], firsts[weight_index], seconds[weight_index], grads[weight_index] * clip_scale, rates[weight_index], decays[weight_index]))
    return (loss_value, clip_norm, updated[0][0], updated[0][1], updated[0][2], updated[1][0], updated[1][1], updated[1][2], updated[2][0], updated[2][1], updated[2][2], updated[3][0], updated[3][1], updated[3][2], updated[4][0], updated[4][1], updated[4][2], updated[5][0], updated[5][1], updated[5][2])
```

```python
from functools import partial

import jax
import jax.numpy as jnp
from jax import lax
from jax.experimental import pallas as pl
from jax.experimental.pallas import tpu as pltpu
from jax.sharding import PartitionSpec as P

HD = 64
DOCS_ROW = 8
STEP = 7


EPS_NORM = 1e-06
BETA_ONE = 0.9
BETA_TWO = 0.95
ADAM_EPS = 1e-08
RATE_MATRIX = 0.05
RATE_GAIN = 0.3
DECAY = 0.1
CLIP_AT = 0.005
NEVER = -1e30
BF = jnp.bfloat16
F32 = jnp.float32
VMEM = 56 * 1024 * 1024


def flip(x, axis, k):
    return lax.ppermute(x, axis, [(j, j ^ k) for j in range(lax.axis_size(axis))])


def hidden_gather(x):
    two = jnp.stack([x, flip(x, "hidden", 2)])
    return jnp.concatenate([two, flip(two, "hidden", 1)])


def piece_of(bits):
    return (bits >> 1) + 2 * (bits & 1)


def round_up(n, m):
    return -(-n // m) * m


def rms_norm(rows_in, gain):
    return (
        rows_in * lax.rsqrt(jnp.mean(rows_in * rows_in, axis=-1, keepdims=True) + EPS_NORM) * gain
    )


def norm_back(rows_in, gain, gradient):
    normed, pullback = jax.vjp(rms_norm, rows_in, gain)
    return pullback(gradient)


def dot(a, b, ca=1, cb=0):
    return lax.dot_general(a, b, (((ca,), (cb,)), ((), ())), preferred_element_type=F32)


def hot_rows(place, count):
    return (jnp.arange(count, dtype=jnp.int32)[:, None] == place[None, :]).astype(BF)


def hot_columns(place, count):
    return (place[:, None] == jnp.arange(count, dtype=jnp.int32)[None, :]).astype(BF)


QB = 256
SPAN = 2


def mask_of(seg_a, seg_b, pos_a, pos_b):
    return (pos_a >= pos_b) & (seg_a == seg_b)


def attend_kernel(q_ref, k_ref, v_ref, segr_ref, segc_ref, o_ref):
    seq = q_ref.shape[0]
    factor = HD**-0.5
    for b in range(seq // QB):
        lo, hi = max(0, b - SPAN) * QB, (b + 1) * QB
        width = hi - lo
        seg_q = segc_ref[b * QB : hi, :]
        seg_k = segr_ref[:, lo:hi]
        pos_q = lax.broadcasted_iota(jnp.int32, (QB, width), 0) + b * QB
        pos_k = lax.broadcasted_iota(jnp.int32, (QB, width), 1) + lo
        allowed = (pos_q >= pos_k) & (seg_q == seg_k)
        for p in range(2):
            cols = slice(p * HD, (p + 1) * HD)
            q = q_ref[b * QB : hi, cols]
            k = k_ref[lo:hi, cols]
            v = v_ref[lo:hi, cols]
            s = jnp.where(allowed, dot(q, k, 1, 1) * factor, NEVER)
            e = jnp.exp(s - jnp.max(s, axis=1, keepdims=True))
            prob = (e / jnp.sum(e, axis=1, keepdims=True)).astype(BF)
            o_ref[b * QB : hi, cols] = dot(prob, v).astype(BF)


def attend(qkv, seg):
    seq, width = qkv.shape
    pairs = width // 3 // 128

    def part(c):
        return pl.BlockSpec((seq, 128), lambda i: (0, c * pairs + i))

    return pl.pallas_call(
        attend_kernel,
        grid=(pairs,),
        in_specs=[
            part(0),
            part(1),
            part(2),
            pl.BlockSpec((1, seq), lambda i: (0, 0)),
            pl.BlockSpec((seq, 1), lambda i: (0, 0)),
        ],
        out_specs=pl.BlockSpec((seq, 128), lambda i: (0, i)),
        out_shape=jax.ShapeDtypeStruct((seq, width // 3), BF),
        compiler_params=pltpu.CompilerParams(vmem_limit_bytes=VMEM),
        name="attend",
    )(qkv, qkv, qkv, seg[None, :], seg[:, None])


def attend_back_kernel(q_ref, k_ref, v_ref, g_ref, segr_ref, segc_ref, dq_ref, dk_ref, dv_ref, dk_acc, dv_acc):
    seq = q_ref.shape[0]
    factor = HD**-0.5
    dk_acc[...] = jnp.zeros_like(dk_acc)
    dv_acc[...] = jnp.zeros_like(dv_acc)
    for b in range(seq // QB):
        lo, hi = max(0, b - SPAN) * QB, (b + 1) * QB
        width = hi - lo
        seg_q = segr_ref[:, b * QB : hi]
        seg_k = segc_ref[lo:hi, :]
        pos_q = lax.broadcasted_iota(jnp.int32, (width, QB), 1) + b * QB
        pos_k = lax.broadcasted_iota(jnp.int32, (width, QB), 0) + lo
        allowed = (pos_q >= pos_k) & (seg_q == seg_k)
        for p in range(2):
            cols = slice(p * HD, (p + 1) * HD)
            q = q_ref[b * QB : hi, cols]
            k = k_ref[lo:hi, cols]
            v = v_ref[lo:hi, cols]
            g = g_ref[b * QB : hi, cols]
            s = jnp.where(allowed, dot(k, q, 1, 1) * factor, NEVER)
            e = jnp.exp(s - jnp.max(s, axis=0, keepdims=True))
            prob = e / jnp.sum(e, axis=0, keepdims=True)
            d_prob = dot(v, g, 1, 1)
            centre = jnp.sum(prob * d_prob, axis=0, keepdims=True)
            d_score = (prob * (d_prob - centre)).astype(BF)
            dq_ref[b * QB : hi, cols] = (dot(d_score, k, 0, 0) * factor).astype(BF)
            dk_acc[lo:hi, cols] += dot(d_score, q) * factor
            dv_acc[lo:hi, cols] += dot(prob.astype(BF), g)
    dk_ref[...] = dk_acc[...].astype(BF)
    dv_ref[...] = dv_acc[...].astype(BF)


def attend_back(qkv, seg, grad):
    seq, width = qkv.shape
    pairs = width // 3 // 128

    def part(c):
        return pl.BlockSpec((seq, 128), lambda i: (0, c * pairs + i))

    return pl.pallas_call(
        attend_back_kernel,
        grid=(pairs,),
        in_specs=[
            part(0),
            part(1),
            part(2),
            part(0),
            pl.BlockSpec((1, seq), lambda i: (0, 0)),
            pl.BlockSpec((seq, 1), lambda i: (0, 0)),
        ],
        out_specs=[part(0)] * 3,
        out_shape=[jax.ShapeDtypeStruct((seq, width // 3), BF)] * 3,
        scratch_shapes=[pltpu.VMEM((seq, 128), F32)] * 2,
        compiler_params=pltpu.CompilerParams(vmem_limit_bytes=VMEM),
        name="attend_back",
    )(qkv, qkv, qkv, grad, seg[None, :], seg[:, None])


def vocab_block(count):
    for parts in (5, 4, 3, 2):
        if count % (128 * parts) == 0 and count // parts >= 640:
            return count // parts
    return count


def logits_kernel(block, padded, real, table_ref, rows_ref, col_ref, out_ref, stat_ref):
    j = pl.program_id(0)
    logits = dot(table_ref[...], rows_ref[...], 1, 1)
    first = j * block
    row = lax.broadcasted_iota(jnp.int32, (block, 1), 0) + first
    pad = jnp.zeros((block, 1), F32)
    for q in range(4):
        pad = jnp.where((row >= q * padded + real) & (row < (q + 1) * padded), NEVER, pad)
    logits = logits + pad
    out_ref[...] = logits

    @pl.when(j == 0)
    def _():
        stat_ref[0:1, :] = jnp.full((1, stat_ref.shape[1]), NEVER, F32)
        stat_ref[1:8, :] = jnp.zeros((7, stat_ref.shape[1]), F32)

    before = stat_ref[0:1, :]
    peak = jnp.maximum(before, jnp.max(logits, axis=0, keepdims=True))
    total = jnp.sum(jnp.exp(logits - peak), axis=0, keepdims=True)
    rows = lax.broadcasted_iota(jnp.int32, logits.shape, 0)
    hit = rows == (col_ref[...] - first)
    stat_ref[0:1, :] = peak
    stat_ref[1:2, :] = stat_ref[1:2, :] * jnp.exp(before - peak) + total
    stat_ref[2:3, :] += jnp.sum(jnp.where(hit, logits, 0.0), axis=0, keepdims=True)


def head_logits(table, rows, col, padded, real):
    vocab, width = table.shape
    tokens = rows.shape[0]
    block = vocab_block(vocab)
    return pl.pallas_call(
        partial(logits_kernel, block, padded, real),
        grid=(vocab // block,),
        in_specs=[
            pl.BlockSpec((block, width), lambda j: (j, 0)),
            pl.BlockSpec((tokens, width), lambda j: (0, 0)),
            pl.BlockSpec((1, tokens), lambda j: (0, 0)),
        ],
        out_specs=[
            pl.BlockSpec((block, tokens), lambda j: (j, 0)),
            pl.BlockSpec((8, tokens), lambda j: (0, 0)),
        ],
        out_shape=[
            jax.ShapeDtypeStruct((vocab, tokens), F32),
            jax.ShapeDtypeStruct((8, tokens), F32),
        ],
        compiler_params=pltpu.CompilerParams(vmem_limit_bytes=VMEM),
        cost_estimate=pl.CostEstimate(
            flops=2 * vocab * tokens * width,
            bytes_accessed=4 * vocab * tokens + 2 * vocab * width,
            transcendentals=vocab * tokens,
        ),
        name="head_logits",
    )(table, rows, col)


def head_back_kernel(block, table_ref, logits_ref, col_ref, side_ref, d_ref, out_ref, acc):
    j = pl.program_id(0)
    logits = logits_ref[...]
    rows = lax.broadcasted_iota(jnp.int32, logits.shape, 0)
    hit = rows == (col_ref[...] - j * block)
    prob = jnp.exp(logits - side_ref[0:1, :])
    d = (jnp.where(hit, prob - 1.0, prob) * side_ref[1:2, :]).astype(BF)
    d_ref[...] = d
    part = dot(table_ref[...], d)

    @pl.when(j == 0)
    def _():
        acc[...] = part

    @pl.when(j > 0)
    def _():
        acc[...] += part

    @pl.when(j == pl.num_programs(0) - 1)
    def _():
        out_ref[...] = acc[...].T.astype(out_ref.dtype)


def head_back(table_t, logits, col, side):
    width, vocab = table_t.shape
    tokens = logits.shape[1]
    block = vocab_block(vocab)
    return pl.pallas_call(
        partial(head_back_kernel, block),
        grid=(vocab // block,),
        in_specs=[
            pl.BlockSpec((width, block), lambda j: (0, j)),
            pl.BlockSpec((block, tokens), lambda j: (j, 0)),
            pl.BlockSpec((1, tokens), lambda j: (0, 0)),
            pl.BlockSpec((8, tokens), lambda j: (0, 0)),
        ],
        out_specs=[
            pl.BlockSpec((block, tokens), lambda j: (j, 0)),
            pl.BlockSpec((tokens, width), lambda j: (0, 0)),
        ],
        out_shape=[
            jax.ShapeDtypeStruct((vocab, tokens), BF),
            jax.ShapeDtypeStruct((tokens, width), BF),
        ],
        scratch_shapes=[pltpu.VMEM((width, tokens), F32)],
        compiler_params=pltpu.CompilerParams(vmem_limit_bytes=VMEM),
        cost_estimate=pl.CostEstimate(
            flops=2 * vocab * tokens * width,
            bytes_accessed=6 * vocab * tokens + 2 * vocab * width,
            transcendentals=vocab * tokens,
        ),
        name="head_back",
    )(table_t, logits, col, side)


def table_grad_kernel(count, *refs):
    d_refs, row_refs, out_ref = refs[:count], refs[count : 2 * count], refs[2 * count]
    total = dot(d_refs[0][...], row_refs[0][...])
    for k in range(1, count):
        total += dot(d_refs[k][...], row_refs[k][...])
    out_ref[...] = total


def table_grad(ds, rows):
    vocab, tokens = ds[0].shape
    width = rows[0].shape[1]
    count = len(ds)
    block = vocab // 10 if vocab % 160 == 0 else vocab // 4 if vocab % 64 == 0 else vocab
    return pl.pallas_call(
        partial(table_grad_kernel, count),
        grid=(vocab // block,),
        in_specs=[pl.BlockSpec((block, tokens), lambda j: (j, 0))] * count
        + [pl.BlockSpec((tokens, width), lambda j: (0, 0))] * count,
        out_specs=pl.BlockSpec((block, width), lambda j: (j, 0)),
        out_shape=jax.ShapeDtypeStruct((vocab, width), F32),
        compiler_params=pltpu.CompilerParams(vmem_limit_bytes=VMEM),
        cost_estimate=pl.CostEstimate(
            flops=2 * vocab * tokens * width * count,
            bytes_accessed=2 * vocab * tokens * count + 4 * vocab * width,
            transcendentals=0,
        ),
        name="table_grad",
    )(*ds, *rows)


def adam_step(weight, first_moment, second_moment, gradient, step_rate, weight_decay):
    first_moment = BETA_ONE * first_moment + (1.0 - BETA_ONE) * gradient
    second_moment = BETA_TWO * second_moment + (1.0 - BETA_TWO) * gradient * gradient
    update = (
        first_moment
        / (1.0 - BETA_ONE**STEP)
        / (jnp.sqrt(second_moment / (1.0 - BETA_TWO**STEP)) + ADAM_EPS)
    )
    return (weight - step_rate * (update + weight_decay * weight), first_moment, second_moment)


def combine_stats(left, right):
    peak = jnp.maximum(left[0], right[0])
    total = left[1] * jnp.exp(left[0] - peak) + right[1] * jnp.exp(right[0] - peak)
    return jnp.stack([peak, total, left[2] + right[2]])


def on_device(
    token_ids,
    target_ids,
    doc_segments,
    hash_experts,
    embed_table,
    embed_first,
    embed_second,
    attn_in,
    attn_in_first,
    attn_in_second,
    attn_out,
    attn_out_first,
    attn_out_second,
    expert_in,
    expert_in_first,
    expert_in_second,
    expert_out,
    expert_out_first,
    expert_out_second,
    norm_gains,
    gains_first,
    gains_second,
):
    n_expert = lax.axis_size("expert")
    n_hidden = lax.axis_size("hidden")
    assert n_hidden == 4 and token_ids.shape[0] == 1
    e_index = lax.axis_index("expert")
    h_index = lax.axis_index("hidden")
    tok_count = token_ids.shape[1]
    vocab_rows, model_width = embed_table.shape
    embed_scale = model_width**0.5
    ids = token_ids[0]
    targets = target_ids[0]
    segment = doc_segments[0]
    token_at = jnp.arange(tok_count, dtype=jnp.int32)

    padded = round_up(vocab_rows, 32)
    table_own = jnp.pad(embed_table.astype(BF), ((0, padded - vocab_rows), (0, 0)))
    own_rows = attn_in.shape[0]
    head_width = attn_in.shape[2]
    packed = jnp.concatenate(
        [
            attn_in.reshape(own_rows, 3 * head_width),
            attn_out,
            jnp.pad(norm_gains, ((0, 0), (0, 125))),
        ],
        axis=1,
    ).astype(BF)
    packed = jnp.stack([packed, flip(packed, "hidden", 2)])
    packed = lax.all_gather(packed, "expert", axis=1, tiled=True)
    w_qkv = (
        packed[:, :, : 3 * head_width]
        .reshape(2, model_width, 3, head_width)
        .transpose(1, 2, 0, 3)
        .reshape(model_width, 6 * head_width)
    )
    w_proj = (
        packed[:, :, 3 * head_width : 4 * head_width]
        .transpose(1, 0, 2)
        .reshape(model_width, 2 * head_width)
    )
    gain_full = packed[0, :, 4 * head_width : 4 * head_width + 3].astype(F32)

    slots = round_up(3 * tok_count // (2 * n_expert * n_hidden), 16)
    shard = ids // vocab_rows
    shard_e, shard_h = shard // n_hidden, shard % n_hidden
    same_id = ids[:, None] == ids[None, :]
    first_at = jnp.min(jnp.where(same_id, token_at[None, :], tok_count), axis=1)
    is_first = first_at == token_at
    rank = jnp.sum(
        (
            (shard[:, None] == shard[None, :])
            & is_first[None, :]
            & (token_at[None, :] < first_at[:, None])
        ).astype(jnp.int32),
        axis=1,
    )
    overflow = jnp.max(rank) >= slots
    place_own = jnp.where(
        (shard_h == h_index) & (rank < slots), shard_e * slots + rank, -1
    )
    wanted = jnp.max(
        jnp.where(
            jnp.arange(n_expert * slots, dtype=jnp.int32)[:, None] == place_own[None, :],
            (ids % vocab_rows)[None, :],
            -1,
        ),
        axis=1,
    )
    asked = jnp.concatenate(
        [
            wanted.reshape(n_expert, slots),
            jnp.broadcast_to(overflow.astype(jnp.int32), (n_expert, 128 - slots)),
        ],
        axis=1,
    )
    asked = lax.all_to_all(asked, "expert", split_axis=0, concat_axis=0, tiled=True)
    any_overflow = jnp.max(asked[:, slots:]) > 0
    asked_rows = asked[:, :slots].reshape(n_expert * slots)
    answer = dot(hot_columns(asked_rows, padded), table_own).astype(BF)
    answer = lax.all_to_all(answer, "expert", split_axis=0, concat_axis=0, tiled=True)
    answers = hidden_gather(answer).reshape(4 * n_expert * slots, model_width)
    place_all = piece_of(shard_h ^ h_index) * (n_expert * slots) + shard_e * slots + rank
    looked_up = dot(hot_columns(place_all, 4 * n_expert * slots), answers).astype(BF)

    def look_up_all():
        table_all = lax.all_gather(embed_table.astype(BF), "expert", axis=0, tiled=True)
        is_owned = shard_h == h_index
        local = jnp.where(is_owned, shard_e * vocab_rows + ids % vocab_rows, 0)
        found = jnp.where(is_owned[:, None], table_all[local], jnp.zeros((), BF))
        return lax.psum(found, "hidden")

    looked_up = lax.cond(any_overflow, look_up_all, lambda: looked_up)
    embedded = looked_up.astype(F32) * embed_scale

    normed_one = rms_norm(embedded, gain_full[:, 0]).astype(BF)
    qkv = dot(normed_one, w_qkv).astype(BF)
    attended = attend(qkv, segment)
    attn_part = dot(attended, w_proj, 1, 1)
    after_attn = embedded + (attn_part + flip(attn_part, "hidden", 1))
    normed_two = rms_norm(after_attn, gain_full[:, 1]).astype(BF)

    capacity = 3 * tok_count // (2 * n_expert)
    quarter = capacity // n_hidden
    expert_ids = hash_experts[ids]
    onehot = (expert_ids[:, None] == jnp.arange(n_expert, dtype=jnp.int32)).astype(jnp.int32)
    before = jnp.cumsum(onehot, axis=0) - onehot
    slot_rank = jnp.sum(before * onehot, axis=1)
    kept = slot_rank < capacity
    slot_h = slot_rank // quarter
    slot_in = expert_ids * quarter + slot_rank % quarter
    rows_dev = n_expert * quarter
    fill_place = jnp.where(kept & (slot_h == h_index), slot_in, -1)
    pick_place = jnp.where(kept, piece_of(slot_h ^ h_index) * rows_dev + slot_in, -1)
    fill_hot = hot_rows(fill_place, rows_dev)
    pick_hot = hot_columns(pick_place, 4 * rows_dev)

    def to_expert(rows_in):
        block = dot(fill_hot, rows_in).astype(BF)
        return lax.all_to_all(block, "expert", split_axis=0, concat_axis=0, tiled=True)

    def from_expert(rows_in):
        block = lax.all_to_all(rows_in, "expert", split_axis=0, concat_axis=0, tiled=True)
        return dot(pick_hot, hidden_gather(block).reshape(4 * rows_dev, model_width))

    weights_own = jnp.stack([expert_in[0], expert_out[0]]).astype(BF)
    expert_w = hidden_gather(weights_own)
    received = to_expert(normed_two)
    pre_act = [dot(received, expert_w[p, 0]) for p in range(4)]
    active = [jax.nn.gelu(pre, approximate=False).astype(BF) for pre in pre_act]
    expert_result = sum(dot(active[p], expert_w[p, 1]) for p in range(4)).astype(BF)
    moe_rows = from_expert(expert_result)
    after_moe = after_attn + moe_rows
    final_rows = rms_norm(after_moe, gain_full[:, 2]).astype(BF)

    half, fourth = tok_count // 2, tok_count // 4
    own_at = (h_index & 1) * half + (h_index >> 1) * fourth
    other_at = (h_index & 1) * half + (1 - (h_index >> 1)) * fourth
    n_far = n_expert // 2

    def own_order(x):
        return jnp.concatenate(
            [
                lax.dynamic_slice_in_dim(x, own_at, fourth, x.ndim - 1),
                lax.dynamic_slice_in_dim(x, other_at, fourth, x.ndim - 1),
            ],
            axis=-1,
        )

    counts = jnp.sum((segment[:, None] == segment[None, :]).astype(F32), axis=1)
    weights = 1.0 / counts / (n_expert * DOCS_ROW)
    about = own_order(jnp.stack([targets.astype(F32), weights]))
    about_all = [about] + [flip(about, "expert", 2 * k) for k in range(1, n_far)]
    slice_two = jnp.concatenate([table_own, flip(table_own, "expert", 1)])
    table = jnp.concatenate([slice_two, flip(slice_two, "hidden", 1)])
    table_t = table.T

    own_part = lax.dynamic_slice_in_dim(final_rows, own_at, fourth, 0)
    other_part = lax.dynamic_slice_in_dim(final_rows, other_at, fourth, 0)
    head_rows = [jnp.concatenate([own_part, other_part])]
    for k in range(1, n_far):
        far = flip(own_part, "expert", 2 * k)
        head_rows.append(jnp.concatenate([far, flip(far, "hidden", 2)]))

    columns = []
    for k in range(n_far):
        target = about_all[k][0].astype(jnp.int32)
        block_of = target // vocab_rows
        away_e = (block_of // n_hidden) ^ e_index
        away_h = (block_of % n_hidden) ^ h_index
        mine = (away_e < 2) & (away_h < 2)
        column = (away_e + 2 * away_h) * padded + target % vocab_rows
        columns.append(jnp.where(mine, column, -1)[None, :])
    logits, stats = [], []
    for k in range(n_far):
        one, stat = head_logits(table, head_rows[k], columns[k], padded, vocab_rows)
        logits.append(one)
        stats.append(stat[:3])
    stat = jnp.stack(stats, axis=1)
    across = flip(stat, "hidden", 2)
    stat = combine_stats(stat, jnp.concatenate([across[..., fourth:], across[..., :fourth]], axis=2))
    far_stats = [flip(stat, "expert", 2 * k) for k in range(1, n_far)]
    for k in range(1, n_far):
        far = jnp.stack([far_stats[k - 1][:, j ^ k] for j in range(n_far)], axis=1)
        stat = combine_stats(stat, far)
    log_total = stat[0] + jnp.log(stat[1])
    loss_part = jnp.sum((log_total[0] - stat[2, 0]) * about[1])

    d_logits, d_parts = [None] * n_far, [None] * n_far
    for k in list(range(1, n_far)) + [0]:
        side = jnp.concatenate(
            [log_total[k][None, :], about_all[k][1:2], jnp.zeros((6, half), F32)]
        )
        d_logits[k], part = head_back(table_t, logits[k], columns[k], side)
        gathered = part[:fourth].astype(F32) + flip(part[fourth:], "hidden", 2).astype(F32)
        if k:
            gathered = flip(gathered.astype(BF), "expert", 2 * k).astype(F32)
        d_parts[k] = gathered
    d_quarter = sum(d_parts)
    d_four = hidden_gather(d_quarter.astype(BF))
    low_half = jnp.where(h_index & 1, d_four[2:], d_four[:2])
    high_half = jnp.where(h_index & 1, d_four[:2], d_four[2:])
    both = jnp.stack([low_half, high_half])
    both = jnp.where(h_index >> 1, both[:, ::-1], both)
    d_final = both.reshape(tok_count, model_width).astype(F32)

    d_slices = table_grad(d_logits, head_rows)
    d_after_moe, d_gain_three = norm_back(after_moe, gain_full[:, 2], d_final)

    d_slices = d_slices.reshape(2, 2, padded, model_width)
    d_two = d_slices[0] + flip(d_slices[1], "hidden", 1)
    d_table = d_two[0] + flip(d_two[1].astype(BF), "expert", 1).astype(F32)

    grad_in = to_expert(d_after_moe.astype(BF))
    d_received = 0.0
    d_w = []
    for p in range(4):
        d_active = dot(grad_in, expert_w[p, 1], 1, 1)
        gelu_pull = jax.vjp(partial(jax.nn.gelu, approximate=False), pre_act[p])[1]
        d_pre = gelu_pull(d_active)[0].astype(BF)
        d_received = d_received + dot(d_pre, expert_w[p, 0], 1, 1)
        d_w.append(jnp.stack([dot(received, d_pre, 0, 0), dot(active[p], grad_in, 0, 0)]))
    d_normed_two = from_expert(d_received.astype(BF))
    w_near = flip(jnp.stack([d_w[2], d_w[3]]), "hidden", 1)
    g_expert = (d_w[0] + w_near[0]) + flip((d_w[1] + w_near[1]).astype(BF), "hidden", 2).astype(F32)
    d_after_norm, d_gain_two = norm_back(after_attn, gain_full[:, 1], d_normed_two)
    d_after_attn = d_after_moe + d_after_norm

    d_branch = d_after_attn.astype(BF)
    d_proj = dot(d_branch, attended[:, :head_width], 0, 0)
    d_attended = dot(d_branch, w_proj).astype(BF)
    d_qkv = jnp.concatenate(attend_back(qkv, segment, d_attended), axis=1)
    d_norm_part = dot(d_qkv, w_qkv, 1, 1)
    d_own = d_qkv.reshape(tok_count, 3, 2, head_width)[:, :, 0].reshape(tok_count, 3 * head_width)
    d_in = dot(normed_one, d_own, 0, 0)
    d_normed_one = d_norm_part + flip(d_norm_part, "hidden", 1)
    d_embed_norm, d_gain_one = norm_back(embedded, gain_full[:, 0], d_normed_one)
    d_embedded = (d_after_attn + d_embed_norm) * embed_scale

    d_high = lax.reduce_precision(d_embedded, 8, 7)
    d_low = (d_embedded - d_high).astype(BF)
    row_hot = hot_rows(place_own, n_expert * slots)
    d_rows = dot(row_hot, d_high.astype(BF)) + dot(row_hot, d_low)
    d_gains = jnp.stack([d_gain_one, d_gain_two, d_gain_three], axis=1).reshape(n_expert, 1, -1)
    gains_high = lax.reduce_precision(d_gains, 8, 7)
    gains_two = jnp.concatenate([gains_high, d_gains - gains_high], axis=1).astype(BF)
    gains_two = jnp.pad(gains_two, ((0, 0), (0, 14), (0, model_width - gains_two.shape[2])))
    sent = jnp.concatenate(
        [
            d_rows.astype(BF).reshape(n_expert, slots, model_width),
            gains_two,
            jnp.concatenate([d_in, d_proj], axis=1)
            .astype(BF)
            .reshape(n_expert, own_rows, 4 * head_width),
        ],
        axis=1,
    )
    got = lax.all_to_all(sent, "expert", split_axis=0, concat_axis=0, tiled=True)
    got_rows = got[:, :slots].reshape(n_expert * slots, model_width)
    d_scattered = dot(hot_rows(asked_rows, padded), got_rows)

    def scatter_all():
        def step(k, carry):
            d_far, ids_far, total = carry
            shard_far = ids_far // vocab_rows
            is_owned = shard_far == e_index * n_hidden + h_index
            local = jnp.where(is_owned, ids_far % vocab_rows, 0)
            total = total.at[local].add(jnp.where(is_owned[:, None], d_far, 0.0))
            ring = [(j, (j + 1) % n_expert) for j in range(n_expert)]
            return lax.ppermute(d_far, "expert", ring), lax.ppermute(ids_far, "expert", ring), total

        start = (d_embedded, ids, jnp.zeros((padded, model_width), F32))
        return lax.fori_loop(0, n_expert, step, start)[2]

    d_scattered = lax.cond(any_overflow, scatter_all, lambda: d_scattered)
    g_table = (d_table + d_scattered)[:vocab_rows]
    g_attn = jnp.sum(got[:, slots + 16 :].astype(F32), axis=0)
    g_attn_in = g_attn[:, : 3 * head_width].reshape(own_rows, 3, head_width)
    g_attn_out = g_attn[:, 3 * head_width :]
    g_gains = jnp.sum(got[:, slots : slots + 2, : 3 * own_rows].astype(F32), axis=(0, 1)).reshape(
        own_rows, 3
    )
    g_expert_in = g_expert[0][None]
    g_expert_out = g_expert[1][None]

    squares = (
        jnp.sum(g_table * g_table)
        + jnp.sum(g_attn * g_attn)
        + jnp.sum(g_expert * g_expert)
        + jnp.sum(g_gains * g_gains) / n_hidden
    )
    both_sums = jnp.stack([squares, loss_part * (2.0 / n_hidden)])
    both_sums = jnp.broadcast_to(jnp.pad(both_sums, (0, 126))[None], (n_expert, 128))
    both_sums = lax.all_to_all(both_sums, "expert", split_axis=0, concat_axis=0, tiled=True)
    both_sums = lax.all_gather(jnp.sum(both_sums, axis=0), "hidden", axis=0)
    both_sums = jnp.sum(both_sums, axis=0)
    clip_norm = jnp.sqrt(both_sums[0])
    loss_value = both_sums[1]
    clip_scale = jnp.minimum(1.0, CLIP_AT / clip_norm)
    table_up = adam_step(
        embed_table, embed_first, embed_second, g_table * clip_scale, RATE_MATRIX, DECAY
    )
    attn_in_up = adam_step(
        attn_in, attn_in_first, attn_in_second, g_attn_in * clip_scale, RATE_MATRIX, DECAY
    )
    attn_out_up = adam_step(
        attn_out, attn_out_first, attn_out_second, g_attn_out * clip_scale, RATE_MATRIX, DECAY
    )
    expert_in_up = adam_step(
        expert_in, expert_in_first, expert_in_second, g_expert_in * clip_scale, RATE_MATRIX, DECAY
    )
    expert_out_up = adam_step(
        expert_out,
        expert_out_first,
        expert_out_second,
        g_expert_out * clip_scale,
        RATE_MATRIX,
        DECAY,
    )
    gains_up = adam_step(
        norm_gains, gains_first, gains_second, g_gains * clip_scale, RATE_GAIN, 0.0
    )
    return (
        loss_value,
        clip_norm,
        *table_up,
        *attn_in_up,
        *attn_out_up,
        *expert_in_up,
        *expert_out_up,
        *gains_up,
    )


def solution(mesh):
    rows = P("expert", None)
    table = P(("expert", "hidden"), None)
    wide = P("expert", None, "hidden")
    flat = P("expert", "hidden")
    tall = P("expert", "hidden", None)
    groups = (table, wide, flat, wide, tall, rows)
    each = tuple(spec for spec in groups for _ in range(3))
    return jax.shard_map(
        on_device,
        mesh=mesh,
        in_specs=(rows, rows, rows, P(), *each),
        out_specs=(P(), P(), *each),
        check_vma=False,
    )
```

```python
from functools import partial

import jax
import jax.numpy as jnp
from jax import lax
from jax.experimental import pallas as pl
from jax.experimental.pallas import tpu as pltpu
from jax.sharding import PartitionSpec as P

HD = 64
DOCS_ROW = 8
STEP = 7


EPS_NORM = 1e-06
BETA_ONE = 0.9
BETA_TWO = 0.95
ADAM_EPS = 1e-08
RATE_MATRIX = 0.05
RATE_GAIN = 0.3
DECAY = 0.1
CLIP_AT = 0.005
NEVER = -1e30
BF = jnp.bfloat16
F32 = jnp.float32
VMEM = 56 * 1024 * 1024
SHORT = pl.CostEstimate(flops=1024, bytes_accessed=1024, transcendentals=0)


def flip(x, axis, k):
    return lax.ppermute(x, axis, [(j, j ^ k) for j in range(lax.axis_size(axis))])


def behind(x, after):
    return jnp.where(after == after, x, 0)


def far_flip(x, axis, k, after=None):
    pairs = [[j, j ^ k] for j in range(lax.axis_size(axis)) if not j & k]
    both = lax.all_gather(x, axis, axis_index_groups=pairs)
    upper = (lax.axis_index(axis) // k) % 2
    if after is not None:
        upper = behind(upper, after)
    return lax.dynamic_index_in_dim(both, 1 - upper, 0, keepdims=False)


def hidden_gather(x):
    far = flip(x, "hidden", 2)
    return [x, far, flip(x, "hidden", 1), flip(far, "hidden", 1)]


def piece_of(bits):
    return (bits >> 1) + 2 * (bits & 1)


def round_up(n, m):
    return -(-n // m) * m


def dot(a, b, ca=1, cb=0):
    return lax.dot_general(a, b, (((ca,), (cb,)), ((), ())), preferred_element_type=F32)


def hot_rows(place, count):
    return (jnp.arange(count, dtype=jnp.int32)[:, None] == place[None, :]).astype(BF)


def hot_columns(place, count):
    return (place[:, None] == jnp.arange(count, dtype=jnp.int32)[None, :]).astype(BF)


QB = 256
SPAN = 2


ANY = pl.BlockSpec(memory_space=pl.ANY)
WHOLE = pl.BlockSpec(memory_space=pltpu.VMEM)


def bias_of(first, second, axis, at_first, at_second):
    shape = (first.shape[0], second.shape[1])
    pos_a = lax.broadcasted_iota(jnp.int32, shape, 0) + at_first
    pos_b = lax.broadcasted_iota(jnp.int32, shape, 1) + at_second
    seen = (pos_a >= pos_b) if axis == 0 else (pos_b >= pos_a)
    return jnp.where(seen & (first == second), 0.0, NEVER)


def pack_kernel(in_ref, out_ref, gains_ref, *rest):
    o_ref = rest[-1]
    o_ref[...] = jnp.zeros_like(o_ref)
    width = out_ref.shape[1]
    for c in range(3):
        o_ref[:, c * width : (c + 1) * width] = in_ref[c].astype(BF)
    wide = round_up(3 * width, 128)
    o_ref[:, wide : wide + width] = out_ref[...].astype(BF)
    o_ref[:, wide + width : wide + width + 3] = gains_ref[...].astype(BF)


def pack(attn_in, attn_out, gains, ready):
    rows, width = attn_out.shape
    return pl.pallas_call(
        pack_kernel,
        in_specs=[WHOLE] * 3 + [ANY] * len(ready),
        out_specs=WHOLE,
        out_shape=jax.ShapeDtypeStruct((rows, round_up(round_up(3 * width, 128) + width + 3, 128)), BF),
        name="pack",
    )(attn_in.transpose(1, 0, 2), attn_out, gains, *ready)


def attend_kernel(rows_ref, w_ref, segr_ref, segc_ref, *rest):
    qkv_ref, o_ref, part_ref = rest[-3:]
    pieces, seq, width = o_ref.shape
    wide = round_up(3 * width, 128)
    factor = jnp.asarray(HD**-0.5, BF)
    heads = [(p, c) for p in range(pieces) for c in range(0, width, HD)]
    for p in range(pieces):
        qkv_ref[p] = dot(rows_ref[...], w_ref[p, :, : 3 * width]).astype(BF)
    for b in range(seq // QB):
        lo, at, hi = max(0, b - SPAN) * QB, b * QB, (b + 1) * QB
        bias = bias_of(segc_ref[at:hi, :], segr_ref[:, lo:hi], 0, at, lo)
        scores = []
        for p, c in heads:
            q = qkv_ref[p, at:hi, c : c + HD] * factor
            scores.append(dot(q, qkv_ref[p, lo:hi, width + c : width + c + HD], 1, 1))
        probs = []
        for s in scores:
            s = s + bias
            e = jnp.exp(s - jnp.max(s, axis=1, keepdims=True))
            probs.append((e * (1.0 / jnp.sum(e, axis=1, keepdims=True))).astype(BF))
        outs = [
            dot(prob, qkv_ref[p, lo:hi, 2 * width + c : 2 * width + c + HD])
            for prob, (p, c) in zip(probs, heads, strict=True)
        ]
        for out, (p, c) in zip(outs, heads, strict=True):
            o_ref[p, at:hi, c : c + HD] = out.astype(BF)
    total = dot(o_ref[0], w_ref[0, :, wide : wide + width], 1, 1)
    for p in range(1, pieces):
        total += dot(o_ref[p], w_ref[p, :, wide : wide + width], 1, 1)
    part_ref[...] = total


def attend(rows, packed, width, seg, ready):
    seq, model = rows.shape
    pieces = packed.shape[0]
    return pl.pallas_call(
        attend_kernel,
        in_specs=[WHOLE] * 4 + [ANY] * len(ready),
        out_specs=[WHOLE] * 3,
        out_shape=[
            jax.ShapeDtypeStruct((pieces, seq, 3 * width), BF),
            jax.ShapeDtypeStruct((pieces, seq, width), BF),
            jax.ShapeDtypeStruct((seq, model), F32),
        ],
        compiler_params=pltpu.CompilerParams(vmem_limit_bytes=VMEM),
        cost_estimate=SHORT,
        name="attend",
    )(rows, packed, seg[None, :], seg[:, None], *ready)


def attend_back_kernel(branch_ref, w_ref, qkv_ref, segr_ref, segc_ref, *rest):
    d_ref, part_ref, g_ref, dk_acc, dv_acc = rest[-5:]
    pieces, seq, width = g_ref.shape
    wide = round_up(3 * width, 128)
    scale = HD**-0.5
    factor = jnp.asarray(scale, BF)
    heads = [(p, c) for p in range(pieces) for c in range(0, width, HD)]
    for p in range(pieces):
        g_ref[p] = dot(branch_ref[...], w_ref[p, :, wide : wide + width]).astype(BF)
    dk_acc[...] = jnp.zeros_like(dk_acc)
    dv_acc[...] = jnp.zeros_like(dv_acc)
    for b in range(seq // QB):
        lo, at, hi = max(0, b - SPAN) * QB, b * QB, (b + 1) * QB
        bias = bias_of(segc_ref[lo:hi, :], segr_ref[:, at:hi], 1, lo, at)
        for group in (heads[: len(heads) // 2], heads[len(heads) // 2 :]):
            qs = [qkv_ref[p, at:hi, c : c + HD] * factor for p, c in group]
            ks = [qkv_ref[p, lo:hi, width + c : width + c + HD] for p, c in group]
            gs = [g_ref[p, at:hi, c : c + HD] for p, c in group]
            scores = [dot(k, q, 1, 1) for k, q in zip(ks, qs, strict=True)]
            d_probs = [
                dot(qkv_ref[p, lo:hi, 2 * width + c : 2 * width + c + HD], g, 1, 1)
                for (p, c), g in zip(group, gs, strict=True)
            ]
            probs, d_scores = [], []
            for s, d_prob in zip(scores, d_probs, strict=True):
                s = s + bias
                e = jnp.exp(s - jnp.max(s, axis=0, keepdims=True))
                prob = e * (1.0 / jnp.sum(e, axis=0, keepdims=True))
                centre = jnp.sum(prob * d_prob, axis=0, keepdims=True)
                d_scores.append((prob * (d_prob - centre)).astype(BF))
                probs.append(prob.astype(BF))
            dqs = [dot(d, k, 0, 0) for d, k in zip(d_scores, ks, strict=True)]
            dks = [dot(d, q) for d, q in zip(d_scores, qs, strict=True)]
            dvs = [dot(prob, g) for prob, g in zip(probs, gs, strict=True)]
            for i, (p, c) in enumerate(group):
                d_ref[p, at:hi, c : c + HD] = (dqs[i] * scale).astype(BF)
                dk_acc[p, lo:hi, c : c + HD] += dks[i]
                dv_acc[p, lo:hi, c : c + HD] += dvs[i]
    d_ref[:, :, width : 2 * width] = dk_acc[...].astype(BF)
    d_ref[:, :, 2 * width :] = dv_acc[...].astype(BF)
    total = dot(d_ref[0], w_ref[0, :, : 3 * width], 1, 1)
    for p in range(1, pieces):
        total += dot(d_ref[p], w_ref[p, :, : 3 * width], 1, 1)
    part_ref[...] = total


def attend_back(branch, packed, qkv, seg, ready):
    seq, model = branch.shape
    pieces, _, width = qkv.shape
    return pl.pallas_call(
        attend_back_kernel,
        in_specs=[WHOLE] * 5 + [ANY] * len(ready),
        out_specs=[WHOLE] * 2,
        out_shape=[
            jax.ShapeDtypeStruct((pieces, seq, width), BF),
            jax.ShapeDtypeStruct((seq, model), F32),
        ],
        scratch_shapes=[
            pltpu.VMEM((pieces, seq, width // 3), BF),
            pltpu.VMEM((pieces, seq, width // 3), F32),
            pltpu.VMEM((pieces, seq, width // 3), F32),
        ],
        compiler_params=pltpu.CompilerParams(vmem_limit_bytes=VMEM),
        cost_estimate=SHORT,
        name="attend_back",
    )(branch, packed, qkv, seg[None, :], seg[:, None], *ready)


def attn_grad_kernel(rows_ref, d_ref, branch_ref, o_ref, *rest):
    out_ref = rest[-1]
    width = d_ref.shape[2]
    out_ref[:, :width] = dot(rows_ref[...], d_ref[0], 0, 0).astype(BF)
    out_ref[:, width:] = dot(branch_ref[...], o_ref[0], 0, 0).astype(BF)


def attn_grad(rows, d_qkv, branch, attended, ready):
    model = rows.shape[1]
    seq, third = attended.shape[1:]
    one = pl.BlockSpec((1, seq, 3 * third), lambda i: (0, 0, 0))
    two = pl.BlockSpec((1, seq, third), lambda i: (0, 0, 0))
    full = pl.BlockSpec((seq, model), lambda i: (0, 0))
    return pl.pallas_call(
        attn_grad_kernel,
        grid=(1,),
        in_specs=[full, one, full, two] + [ANY] * len(ready),
        out_specs=pl.BlockSpec((model, 4 * third), lambda i: (0, 0)),
        out_shape=jax.ShapeDtypeStruct((model, 4 * third), BF),
        compiler_params=pltpu.CompilerParams(vmem_limit_bytes=VMEM),
        cost_estimate=SHORT,
        name="attn_grad",
    )(rows, d_qkv, branch, attended, *ready)


def picked(place_ref, *row_refs):
    count = row_refs[0].shape[0]
    at = lax.broadcasted_iota(jnp.int32, (place_ref.shape[0], count), 1)
    total = None
    for q, ref in enumerate(row_refs):
        part = dot((at == place_ref[...] - q * count).astype(BF), ref[...])
        total = part if total is None else total + part
    return total


def pick_norm_kernel(scale, pick, parts, base, *refs):
    first_refs, refs = refs[:parts], refs[parts:]
    if base:
        base_ref, refs = refs[0], refs[1:]
    gain_ref, sum_ref, norm_ref = refs[0], refs[-2], refs[-1]
    if pick:
        x = picked(*first_refs)
    else:
        x = first_refs[0][...]
        for ref in first_refs[1:]:
            x = x + ref[...]
    if base:
        x = base_ref[...] + x
    if scale != 1.0:
        x = x * scale
    sum_ref[...] = x
    root = lax.rsqrt(jnp.mean(x * x, axis=1, keepdims=True) + EPS_NORM)
    norm_ref[...] = (x * root * gain_ref[...]).astype(BF)


def pick_norm(first, base, gain, scale=1.0, pick=True, ready=()):
    tokens = first[0].shape[0]
    width = gain.shape[1]
    block = min(tokens, 256)
    by_rows = pl.BlockSpec((block, width), lambda i: (i, 0))
    if pick:
        first = (first[0][:, None], *first[1:])
        specs = [pl.BlockSpec((block, 1), lambda i: (i, 0))]
        specs += [pl.BlockSpec(r.shape, lambda i: (0, 0)) for r in first[1:]]
    else:
        specs = [by_rows] * len(first)
    has_base = base is not None
    return pl.pallas_call(
        partial(pick_norm_kernel, scale, pick, len(first), has_base),
        grid=(tokens // block,),
        in_specs=specs
        + [by_rows] * has_base
        + [pl.BlockSpec((1, width), lambda i: (0, 0))]
        + [ANY] * len(ready),
        out_specs=[by_rows, by_rows],
        out_shape=[
            jax.ShapeDtypeStruct((tokens, width), F32),
            jax.ShapeDtypeStruct((tokens, width), BF),
        ],
        compiler_params=pltpu.CompilerParams(vmem_limit_bytes=VMEM),
        cost_estimate=SHORT,
        name="pick_norm",
    )(*first, *((base,) if has_base else ()), gain, *ready)


def norm_back_kernel(scale, parts, pick, rest, split, x_ref, gain_ref, *refs):
    g_refs, refs = refs[:parts], refs[parts:]
    if rest:
        rest_ref, refs = refs[0], refs[1:]
    gain_out, one_ref, two_ref = refs[-3:]
    x = x_ref[...]
    if pick == "rows":
        g = picked(*g_refs)
    elif pick == "blocks":
        which = g_refs[0][pl.program_id(0)]
        g = g_refs[1][...].astype(F32)
        for q, ref in enumerate(g_refs[2:], 1):
            g = jnp.where(which == q, ref[...].astype(F32), g)
    else:
        g = g_refs[0][...].astype(F32)
        for ref in g_refs[1:]:
            g = g + ref[...].astype(F32)
    root = lax.rsqrt(jnp.mean(x * x, axis=1, keepdims=True) + EPS_NORM)
    scaled = x * root
    d_gain = jnp.sum(g * scaled, axis=0, keepdims=True)
    g = g * gain_ref[...]
    dx = root * (g - scaled * jnp.mean(g * scaled, axis=1, keepdims=True))
    if rest:
        dx = rest_ref[...] + dx
    if scale != 1.0:
        dx = dx * scale
    high = dx.astype(BF)
    one_ref[...] = high
    two_ref[...] = (dx - high.astype(F32)).astype(BF) if split else dx

    @pl.when(pl.program_id(0) == 0)
    def _():
        gain_out[...] = d_gain

    @pl.when(pl.program_id(0) > 0)
    def _():
        gain_out[...] += d_gain


def norm_back(x, gain, gradients, rest=None, scale=1.0, split=False, pick="", ready=()):
    tokens, width = x.shape
    block = min(tokens, 256)
    by_rows = pl.BlockSpec((block, width), lambda i: (i, 0))
    one_row = pl.BlockSpec((1, width), lambda i: (0, 0))
    has_rest = rest is not None
    whole = [pl.BlockSpec(g.shape, lambda i: (0, 0)) for g in gradients[1:]]
    if pick == "rows":
        gradients = (gradients[0][:, None], *gradients[1:])
        specs = [pl.BlockSpec((block, 1), lambda i: (i, 0)), *whole]
    elif pick == "blocks":
        specs = [pl.BlockSpec(memory_space=pltpu.SMEM), *whole]
    else:
        specs = [by_rows] * len(gradients)
    return pl.pallas_call(
        partial(norm_back_kernel, scale, len(gradients), pick, has_rest, split),
        grid=(tokens // block,),
        in_specs=[by_rows, one_row] + specs + [by_rows] * has_rest + [ANY] * len(ready),
        out_specs=[one_row, by_rows, by_rows],
        out_shape=[
            jax.ShapeDtypeStruct((1, width), F32),
            jax.ShapeDtypeStruct((tokens, width), BF),
            jax.ShapeDtypeStruct((tokens, width), BF if split else F32),
        ],
        compiler_params=pltpu.CompilerParams(vmem_limit_bytes=VMEM),
        cost_estimate=SHORT,
        name="norm_back",
    )(x, gain, *gradients, *((rest,) if has_rest else ()), *ready)


ERFC = (
    -1.26551223,
    1.00002368,
    0.37409196,
    0.09678418,
    -0.18628806,
    0.27886807,
    -1.13520398,
    1.48851587,
    -0.82215223,
    0.17087277,
)


def gelu_and_slope(x):
    t = 1.0 / (1.0 + 0.35355339059327373 * jnp.abs(x))
    poly = jnp.full_like(t, ERFC[-1])
    for c in ERFC[-2::-1]:
        poly = poly * t + c
    square = 0.5 * x * x
    half = 0.5 * t * jnp.exp(poly - square)
    below = jnp.where(x >= 0.0, 1.0 - half, half)
    return x * below, below + x * jnp.exp(-square) * 0.3989422804014327


def expert_back_kernel(grad_ref, *refs):
    w_refs, slope_refs, refs = refs[:4], refs[4:8], refs[8:]
    out_ref, d_refs = refs[-5], refs[-4:]
    grad = grad_ref[...]
    total = None
    for w_ref, slope_ref, d_ref in zip(w_refs, slope_refs, d_refs, strict=True):
        d_pre = (dot(grad, w_ref[1], 1, 1) * slope_ref[...]).astype(BF)
        d_ref[...] = d_pre
        product = dot(d_pre, w_ref[0], 1, 1)
        total = product if total is None else total + product
    out_ref[...] = total.astype(BF)


def expert_back(grad, weights, slopes, ready):
    return pl.pallas_call(
        expert_back_kernel,
        in_specs=[WHOLE] * 9 + [ANY] * len(ready),
        out_specs=[WHOLE] * 5,
        out_shape=[jax.ShapeDtypeStruct(grad.shape, BF)]
        + [jax.ShapeDtypeStruct(slope.shape, BF) for slope in slopes],
        compiler_params=pltpu.CompilerParams(vmem_limit_bytes=VMEM),
        cost_estimate=SHORT,
        name="expert_back",
    )(grad, *weights, *slopes, *ready)


def part_rows(padded):
    return max(r for r in range(32, 385, 32) if padded % r == 0)


def cast_pick_kernel(real, place_ref, x_ref, table_ref, o_ref, acc):
    j = pl.program_id(0)
    rows = x_ref.shape[0]
    at = lax.broadcasted_iota(jnp.int32, x_ref.shape, 0) + j * rows
    table_ref[...] = jnp.where(at < real, x_ref[...], 0.0).astype(BF)
    column = lax.broadcasted_iota(jnp.int32, (place_ref.shape[0], rows), 1) + j * rows
    found = dot((column == place_ref[...]).astype(BF), table_ref[...])

    @pl.when(j == 0)
    def _():
        acc[...] = found

    @pl.when(j > 0)
    def _():
        acc[...] += found

    @pl.when(j == pl.num_programs(0) - 1)
    def _():
        o_ref[...] = acc[...].astype(BF)


def cast_pick(place, x, padded):
    real, width = x.shape
    rows = part_rows(padded)
    count = place.shape[0]
    return pl.pallas_call(
        partial(cast_pick_kernel, real),
        grid=(padded // rows,),
        in_specs=[
            pl.BlockSpec((count, 1), lambda j: (0, 0)),
            pl.BlockSpec((rows, width), lambda j: (j, 0)),
        ],
        out_specs=[
            pl.BlockSpec((rows, width), lambda j: (j, 0)),
            pl.BlockSpec((count, width), lambda j: (0, 0)),
        ],
        out_shape=[
            jax.ShapeDtypeStruct((padded, width), BF),
            jax.ShapeDtypeStruct((count, width), BF),
        ],
        scratch_shapes=[pltpu.VMEM((count, width), F32)],
        compiler_params=pltpu.CompilerParams(vmem_limit_bytes=VMEM),
        cost_estimate=SHORT,
        name="cast_pick",
    )(place[:, None], x)


def turn_kernel(a_ref, b_ref, c_ref, d_ref, o_ref):
    o_ref[...] = jnp.concatenate([a_ref[...], b_ref[...], c_ref[...], d_ref[...]], axis=0).T


def turned(slices):
    padded, width = slices[0].shape
    rows = part_rows(padded)
    return pl.pallas_call(
        turn_kernel,
        grid=(padded // rows,),
        in_specs=[pl.BlockSpec((rows, width), lambda j: (j, 0))] * 4,
        out_specs=pl.BlockSpec((width, 4 * rows), lambda j: (0, j)),
        out_shape=jax.ShapeDtypeStruct((width, 4 * padded), BF),
        compiler_params=pltpu.CompilerParams(vmem_limit_bytes=VMEM),
        cost_estimate=pl.CostEstimate(flops=0, bytes_accessed=24 * padded * width, transcendentals=0),
        name="turned",
    )(*slices)


def logits_kernel(
    real, a_ref, b_ref, c_ref, d_ref, rows_ref, col_ref, *rest
):
    out_ref, peak_ref, stat_ref, peak_s, sum_s, hit_s = rest[-6:]
    j = pl.program_id(0)
    tokens = rows_ref.shape[0]
    part = a_ref.shape[0]

    @pl.when(j == 0)
    def _():
        peak_s[...] = jnp.full((8, tokens), NEVER, F32)
        sum_s[...] = jnp.zeros((8, tokens), F32)
        hit_s[...] = jnp.zeros((8, tokens), F32)

    away = col_ref[...] - j * (4 * part) - lax.broadcasted_iota(jnp.int32, (8, tokens), 0)
    peak, total, hit = peak_s[...], sum_s[...], hit_s[...]
    rows = rows_ref[...]
    tail = round_up(part * (-(-real // part)) - real, 8)
    for q, ref in enumerate((a_ref, b_ref, c_ref, d_ref)):
        logits = dot(ref[...], rows, 1, 1)
        if tail:
            at = lax.broadcasted_iota(jnp.int32, (tail, tokens), 0) + (j + 1) * part - tail
            end = jnp.where(at < real, logits[part - tail :], NEVER)
            logits = jnp.concatenate([logits[: part - tail], end], axis=0)
        tiles = logits.reshape(part // 8, 8, tokens)
        new = jnp.maximum(peak, jnp.max(tiles, axis=0))
        powers = jnp.exp(tiles - new[None])
        out_ref[q * part : (q + 1) * part, :] = powers.reshape(part, tokens)
        peak_ref[q * 8 : (q + 1) * 8, :] = new
        total = total * jnp.exp(peak - new) + jnp.sum(powers, axis=0)
        for i in range(part // 8):
            hit = hit + jnp.where(away == q * part + 8 * i, tiles[i], 0.0)
        peak = new
    peak_s[...], sum_s[...], hit_s[...] = peak, total, hit

    @pl.when(j == pl.num_programs(0) - 1)
    def _():
        top = jnp.max(peak, axis=0, keepdims=True)
        stat_ref[0:1, :] = top
        stat_ref[1:2, :] = jnp.sum(total * jnp.exp(peak - top), axis=0, keepdims=True)
        stat_ref[2:3, :] = jnp.sum(hit, axis=0, keepdims=True)
        stat_ref[3:8, :] = jnp.zeros((5, tokens), F32)


def head_logits(slices, rows, col, real, ready=()):
    padded, width = slices[0].shape
    tokens = rows.shape[0]
    part = part_rows(padded)
    steps = padded // part
    return pl.pallas_call(
        partial(logits_kernel, real),
        grid=(steps,),
        in_specs=[pl.BlockSpec((part, width), lambda j: (j, 0))] * 4
        + [
            pl.BlockSpec((tokens, width), lambda j: (0, 0)),
            pl.BlockSpec((1, tokens), lambda j: (0, 0)),
        ]
        + [ANY] * len(ready),
        out_specs=[
            pl.BlockSpec((4 * part, tokens), lambda j: (j, 0)),
            pl.BlockSpec((32, tokens), lambda j: (j, 0)),
            pl.BlockSpec((8, tokens), lambda j: (0, 0)),
        ],
        out_shape=[
            jax.ShapeDtypeStruct((4 * padded, tokens), F32),
            jax.ShapeDtypeStruct((32 * steps, tokens), F32),
            jax.ShapeDtypeStruct((8, tokens), F32),
        ],
        scratch_shapes=[pltpu.VMEM((8, tokens), F32)] * 3,
        compiler_params=pltpu.CompilerParams(vmem_limit_bytes=VMEM),
        cost_estimate=pl.CostEstimate(flops=16 * padded * tokens * width, bytes_accessed=16 * padded * tokens, transcendentals=0),
        name="head_logits",
    )(*slices, rows, col, *ready)


def head_back_kernel(table_ref, power_ref, peak_ref, col_ref, side_ref, *rest):
    d_ref, out_ref, acc = rest[-3:]
    j = pl.program_id(0)
    block, tokens = power_ref.shape
    part = block // 4
    away = col_ref[...] - j * block - lax.broadcasted_iota(jnp.int32, (8, tokens), 0)
    log_total, weight = side_ref[0:1, :], side_ref[1:2, :]
    pieces = []
    for q in range(4):
        factor = jnp.exp(peak_ref[q * 8 : (q + 1) * 8, :] - log_total) * weight
        for i in range(part // 8):
            at = q * part + 8 * i
            less = jnp.where(away == at, weight, 0.0)
            pieces.append(power_ref[at : at + 8, :] * factor - less)
    d = jnp.concatenate(pieces, axis=0).astype(BF)
    d_ref[...] = d
    product = dot(table_ref[...], d)

    @pl.when(j == 0)
    def _():
        acc[...] = product

    @pl.when(j > 0)
    def _():
        acc[...] += product

    @pl.when(j == pl.num_programs(0) - 1)
    def _():
        out_ref[...] = acc[...].T.astype(out_ref.dtype)


def head_back(table_t, powers, peaks, at, col, side, ready=()):
    width, vocab = table_t.shape
    tokens = col.shape[1]
    steps = peaks.shape[0] // 32
    block = vocab // steps
    return pl.pallas_call(
        head_back_kernel,
        grid=(steps,),
        in_specs=[
            pl.BlockSpec((width, block), lambda j: (0, j)),
            pl.BlockSpec((block, tokens), lambda j: (j, at)),
            pl.BlockSpec((32, tokens), lambda j: (j, at)),
            pl.BlockSpec((1, tokens), lambda j: (0, 0)),
            pl.BlockSpec((8, tokens), lambda j: (0, 0)),
        ]
        + [ANY] * len(ready),
        out_specs=[
            pl.BlockSpec((block, tokens), lambda j: (j, 0)),
            pl.BlockSpec((tokens, width), lambda j: (0, 0)),
        ],
        out_shape=[
            jax.ShapeDtypeStruct((vocab, tokens), BF),
            jax.ShapeDtypeStruct((tokens, width), BF),
        ],
        scratch_shapes=[pltpu.VMEM((width, tokens), F32)],
        compiler_params=pltpu.CompilerParams(vmem_limit_bytes=VMEM),
        cost_estimate=pl.CostEstimate(flops=4 * vocab * tokens * width, bytes_accessed=6 * vocab * tokens, transcendentals=0),
        name="head_back",
    )(table_t, powers, peaks, col, side, *ready)


def table_grad_kernel(count, *refs):
    d_refs, row_refs, out_refs = refs[: 2 * count], refs[2 * count : 3 * count], refs[-2:]
    total = None
    for k in range(count):
        both = jnp.concatenate([d_refs[2 * k][...], d_refs[2 * k + 1][...]], axis=0)
        product = dot(both, row_refs[k][...])
        total = product if total is None else total + product
    part = out_refs[0].shape[0]
    for q in range(2):
        out_refs[q][...] = total[q * part : (q + 1) * part]


def table_grad(ds, rows, padded, which, ready):
    width = rows[0].shape[1]
    part = part_rows(padded)

    def spec(tokens, q):
        return pl.BlockSpec((part, tokens), lambda j: (4 * j + q, 0))

    return pl.pallas_call(
        partial(table_grad_kernel, len(ds)),
        grid=(padded // part,),
        in_specs=[spec(d.shape[1], q) for d in ds for q in which]
        + [pl.BlockSpec(r.shape, lambda j: (0, 0)) for r in rows]
        + [ANY] * len(ready),
        out_specs=[pl.BlockSpec((part, width), lambda j: (j, 0))] * 2,
        out_shape=[jax.ShapeDtypeStruct((padded, width), F32)] * 2,
        compiler_params=pltpu.CompilerParams(vmem_limit_bytes=VMEM),
        cost_estimate=pl.CostEstimate(
            flops=4 * padded * width * sum(d.shape[1] for d in ds),
            bytes_accessed=8 * padded * width,
            transcendentals=0,
        ),
        name="table_grad",
    )(*[d for d in ds for _ in which], *rows, *ready)


def finish_kernel(real, base_ref, place_ref, rows_ref, out_ref, square_ref):
    rows = base_ref.shape[0]
    first = pl.program_id(0) * rows
    at = lax.broadcasted_iota(jnp.int32, (rows, place_ref.shape[1]), 0) + first
    spread = dot((at == place_ref[...]).astype(BF), rows_ref[...])
    g = base_ref[...] + spread
    out_ref[...] = g
    inside = lax.broadcasted_iota(jnp.int32, g.shape, 0) + first < real
    g = jnp.where(inside, g, 0.0)
    squares = jnp.sum(g * g, axis=0, keepdims=True)

    @pl.when(pl.program_id(0) == 0)
    def _():
        square_ref[...] = squares

    @pl.when(pl.program_id(0) > 0)
    def _():
        square_ref[...] += squares


def finish(base, place, rows, real):
    padded, width = base.shape
    part = part_rows(padded)
    block = pl.BlockSpec((part, width), lambda j: (j, 0))
    return pl.pallas_call(
        partial(finish_kernel, real),
        grid=(padded // part,),
        in_specs=[
            block,
            pl.BlockSpec((1, place.shape[0]), lambda j: (0, 0)),
            pl.BlockSpec(rows.shape, lambda j: (0, 0)),
        ],
        out_specs=[block, pl.BlockSpec((1, width), lambda j: (0, 0))],
        out_shape=[
            jax.ShapeDtypeStruct((real, width), F32),
            jax.ShapeDtypeStruct((1, width), F32),
        ],
        compiler_params=pltpu.CompilerParams(vmem_limit_bytes=VMEM),
        cost_estimate=SHORT,
        name="finish",
    )(base, place[None, :], rows)


def adam_step(weight, first_moment, second_moment, gradient, step_rate, weight_decay):
    first_moment = BETA_ONE * first_moment + (1.0 - BETA_ONE) * gradient
    second_moment = BETA_TWO * second_moment + (1.0 - BETA_TWO) * gradient * gradient
    update = (
        first_moment
        / (1.0 - BETA_ONE**STEP)
        / (jnp.sqrt(second_moment / (1.0 - BETA_TWO**STEP)) + ADAM_EPS)
    )
    return (weight - step_rate * (update + weight_decay * weight), first_moment, second_moment)


def combine_stats(left, right):
    peak = jnp.maximum(left[0], right[0])
    total = left[1] * jnp.exp(left[0] - peak) + right[1] * jnp.exp(right[0] - peak)
    return jnp.stack([peak, total, left[2] + right[2]])


def on_device(
    token_ids,
    target_ids,
    doc_segments,
    hash_experts,
    embed_table,
    embed_first,
    embed_second,
    attn_in,
    attn_in_first,
    attn_in_second,
    attn_out,
    attn_out_first,
    attn_out_second,
    expert_in,
    expert_in_first,
    expert_in_second,
    expert_out,
    expert_out_first,
    expert_out_second,
    norm_gains,
    gains_first,
    gains_second,
):
    n_expert = lax.axis_size("expert")
    n_hidden = lax.axis_size("hidden")
    assert n_hidden == 4 and token_ids.shape[0] == 1
    e_index = lax.axis_index("expert")
    h_index = lax.axis_index("hidden")
    tok_count = token_ids.shape[1]
    vocab_rows, model_width = embed_table.shape
    embed_scale = model_width**0.5
    ids = token_ids[0]
    targets = target_ids[0]
    segment = doc_segments[0]
    token_at = jnp.arange(tok_count, dtype=jnp.int32)

    padded = round_up(vocab_rows, 32)
    own_rows = attn_in.shape[0]
    head_width = attn_in.shape[2]

    slots = round_up(5 * tok_count // (4 * n_expert * n_hidden), 8)
    shard = ids // vocab_rows
    shard_e, shard_h = shard // n_hidden, shard % n_hidden
    same_id = ids[:, None] == ids[None, :]
    first_at = jnp.min(jnp.where(same_id, token_at[None, :], tok_count), axis=1)
    is_first = first_at == token_at
    rank = jnp.sum(
        (
            (shard[:, None] == shard[None, :])
            & is_first[None, :]
            & (token_at[None, :] < first_at[:, None])
        ).astype(jnp.int32),
        axis=1,
    )
    overflow = jnp.max(rank) >= slots
    place_own = jnp.where(
        (shard_h == h_index) & (rank < slots), shard_e * slots + rank, -1
    )
    wanted = jnp.max(
        jnp.where(
            jnp.arange(n_expert * slots, dtype=jnp.int32)[:, None] == place_own[None, :],
            (ids % vocab_rows)[None, :],
            -1,
        ),
        axis=1,
    )
    asked = jnp.concatenate(
        [
            wanted.reshape(n_expert, slots),
            jnp.broadcast_to(overflow.astype(jnp.int32), (n_expert, 128 - slots)),
        ],
        axis=1,
    )

    asked = lax.all_to_all(asked, "expert", split_axis=0, concat_axis=0, tiled=True)
    any_overflow = jnp.max(asked[:, slots:]) > 0
    asked_rows = asked[:, :slots].reshape(n_expert * slots)

    capacity = 3 * tok_count // (2 * n_expert)
    quarter = capacity // n_hidden
    expert_ids = hash_experts[ids]
    onehot = (expert_ids[:, None] == jnp.arange(n_expert, dtype=jnp.int32)).astype(jnp.int32)
    before = jnp.cumsum(onehot, axis=0) - onehot
    slot_rank = jnp.sum(before * onehot, axis=1)
    kept = slot_rank < capacity
    slot_h = slot_rank // quarter
    slot_in = expert_ids * quarter + slot_rank % quarter
    rows_dev = n_expert * quarter
    fill_place = jnp.where(kept & (slot_h == h_index), slot_in, -1)
    pick_place = jnp.where(kept, piece_of(slot_h ^ h_index) * rows_dev + slot_in, -1)

    asked_rows = jnp.where(any_overflow, -1, asked_rows)
    table_own, answer = cast_pick(asked_rows, embed_table, padded)
    wide = round_up(3 * head_width, 128)
    packed = pack(attn_in, attn_out, norm_gains, (asked_rows,))
    packed = jnp.stack([packed, flip(packed, "hidden", 2)])
    packed = lax.all_gather(packed, "expert", axis=1, tiled=True)
    gain_full = packed[0, :, wide + head_width : wide + head_width + 3].astype(F32).T
    weights_own = jnp.stack([expert_in[0], expert_out[0]]).astype(BF)
    weights_y = far_flip(weights_own, "hidden", 2)

    n_all = n_expert * n_hidden
    own_shard = e_index * n_hidden + h_index
    everyone = [(j, (j + 1) % n_all) for j in range(n_all)]

    answer = lax.all_to_all(
        answer.reshape(n_expert, slots, model_width),
        "expert",
        split_axis=0,
        concat_axis=0,
        tiled=True,
    )
    answers = hidden_gather(answer.reshape(n_expert * slots, model_width))
    place_all = piece_of(shard_h ^ h_index) * (n_expert * slots) + shard_e * slots + rank

    def look_up_step(k, carry):
        table_far, found = carry
        here = (own_shard - k + n_all) % n_all
        place = jnp.where(shard == here, ids % vocab_rows, -1)
        row = dot(hot_columns(place, padded), table_far).astype(BF)
        row = jnp.pad(row, ((0, 4 * n_expert * slots - tok_count), (0, 0)))
        parts = row.reshape(4, n_expert * slots, model_width)
        found = [jnp.where(k == 0, 0, found[q]) + parts[q] for q in range(4)]
        return lax.ppermute(table_far, ("expert", "hidden"), everyone), found

    answers = lax.fori_loop(
        0, jnp.where(any_overflow, n_all, 0), look_up_step, (table_own, answers)
    )[1]
    place_all = jnp.where(any_overflow, token_at, place_all)
    embedded, normed_one = pick_norm(
        (place_all, *answers), None, gain_full[0:1], embed_scale, ready=(fill_place, pick_place)
    )

    qkv, attended, attn_part = attend(normed_one, packed, head_width, segment, ())
    after_attn, normed_two = pick_norm(
        (attn_part, flip(attn_part, "hidden", 1)),
        embedded,
        gain_full[1:2],
        pick=False,
    )

    fill_hot = hot_rows(fill_place, rows_dev)

    def to_expert(rows_in):
        block = dot(fill_hot, rows_in).astype(BF)
        return lax.all_to_all(block, "expert", split_axis=0, concat_axis=0, tiled=True)

    def from_expert(rows_in):
        block = lax.all_to_all(rows_in, "expert", split_axis=0, concat_axis=0, tiled=True)
        return hidden_gather(block.reshape(rows_dev, model_width))

    expert_w = [
        weights_own,
        weights_y,
        flip(weights_own, "hidden", 1),
        flip(weights_y, "hidden", 1),
    ]
    received = to_expert(normed_two)
    active, slope = [None] * 4, [None] * 4
    expert_sum = 0.0
    for p in (0, 2, 1, 3):
        value, slope[p] = gelu_and_slope(dot(received, expert_w[p][0]))
        active[p] = value.astype(BF)
        expert_sum = expert_sum + dot(active[p], expert_w[p][1])
    after_moe, final_rows = pick_norm(
        (pick_place, *from_expert(expert_sum.astype(BF))),
        after_attn,
        gain_full[2:3],
    )

    slice_x = far_flip(table_own, "expert", 1, final_rows[0, 0])
    slices = [table_own, slice_x, flip(table_own, "hidden", 1), flip(slice_x, "hidden", 1)]
    table_t = turned(slices)
    part = part_rows(padded)

    half, fourth = tok_count // 2, tok_count // 4
    own_at = (h_index & 1) * half + (h_index >> 1) * fourth
    other_at = (h_index & 1) * half + (1 - (h_index >> 1)) * fourth
    n_far = n_expert // 2

    def own_order(x):
        return jnp.concatenate(
            [
                lax.dynamic_slice_in_dim(x, own_at, fourth, x.ndim - 1),
                lax.dynamic_slice_in_dim(x, other_at, fourth, x.ndim - 1),
            ],
            axis=-1,
        )

    counts = jnp.sum((segment[:, None] == segment[None, :]).astype(F32), axis=1)
    weights = 1.0 / counts / (n_expert * DOCS_ROW)
    about = own_order(jnp.stack([targets.astype(F32), weights]))
    about_all = [about] + [flip(about, "expert", 2 * k) for k in range(1, n_far)]
    own_part = lax.dynamic_slice_in_dim(final_rows, own_at, fourth, 0)
    other_part = lax.dynamic_slice_in_dim(final_rows, other_at, fourth, 0)
    far_rows = [flip(own_part, "expert", 2 * k) for k in range(1, n_far)]

    columns = []
    for k in range(n_far):
        target = about_all[k][0].astype(jnp.int32)
        block_of = target // vocab_rows
        away_e = (block_of // n_hidden) ^ e_index
        away_h = (block_of % n_hidden) ^ h_index
        mine = (away_e < 2) & (away_h < 2)
        row_of = target % vocab_rows
        column = (row_of // part) * (4 * part) + (away_e + 2 * away_h) * part + row_of % part
        columns.append(jnp.where(mine, column, -1)[None, :])
    head_rows = [jnp.concatenate([own_part, other_part])]
    powers, stats = [], []
    for k in range(0, n_far, 2):
        for far in far_rows[max(k - 1, 0) : k + 1]:
            far = behind(far, stats[-1][0, 0]) if stats else far
            head_rows.append(jnp.concatenate([far, flip(far, "hidden", 2)]))
        one, two, stat = head_logits(
            slices,
            jnp.concatenate(head_rows[k : k + 2]),
            jnp.concatenate(columns[k : k + 2], axis=1),
            vocab_rows,
            () if k else (table_t,),
        )
        powers.append((one, two))
        stats += [stat[:3, :half], stat[:3, half:]]
    stat = jnp.stack(stats, axis=1)
    across = flip(stat, "hidden", 2)
    stat = combine_stats(stat, jnp.concatenate([across[..., fourth:], across[..., :fourth]], axis=2))
    far_stats = [flip(stat, "expert", 2 * k) for k in range(1, n_far)]
    for k in range(1, n_far):
        far = jnp.stack([far_stats[k - 1][:, j ^ k] for j in range(n_far)], axis=1)
        stat = combine_stats(stat, far)
    log_total = stat[0] + jnp.log(stat[1])
    loss_part = jnp.sum((log_total[0] - stat[2, 0]) * about[1])

    groups = [[0], [1]] + [[k, k + 1] for k in range(2, n_far, 2)]
    group_rows = [jnp.concatenate([head_rows[k] for k in group]) for group in groups]
    d_logits, d_parts, on_y = [None] * len(groups), [None] * n_far, []
    for i in range(len(groups) - 1, -1, -1):
        group = groups[i]
        wide_weights = jnp.concatenate([about_all[k][1] for k in group])
        wide_totals = jnp.concatenate([log_total[k] for k in group])
        side = jnp.stack([wide_totals, wide_weights] + [jnp.zeros_like(wide_totals)] * 6)
        d_logits[i], product = head_back(
            table_t,
            *powers[group[0] // 2],
            group[0] % 2,
            jnp.concatenate([columns[k] for k in group], axis=1),
            side,
            on_y[-3:-2] if i == 0 else (),
        )
        for g in reversed(range(len(group))):
            k, one = group[g], product[g * half : (g + 1) * half]
            gathered = one[:fourth].astype(F32) + flip(one[fourth:], "hidden", 2).astype(F32)
            if k:
                on_y.append(gathered.astype(BF))
                gathered = flip(on_y[-1], "expert", 2 * k).astype(F32)
            d_parts[k] = gathered
    d_quarter = sum(d_parts)
    d_four = hidden_gather(d_quarter.astype(BF))
    quarter_h = jnp.array([0, 2, 1, 3], jnp.int32)

    d_gain_three, d_result, d_after_moe = norm_back(
        after_moe,
        gain_full[2:3],
        (piece_of(quarter_h ^ h_index), *d_four),
        pick="blocks",
    )
    d_across = table_grad(d_logits, group_rows, padded, (1, 3), (d_result,))
    across_x = (d_across[0] + flip(d_across[1], "hidden", 1)).astype(BF)
    grad_in = to_expert(d_result)
    d_received, *d_pre = expert_back(grad_in, expert_w, slope, (across_x,))
    d_w = [
        jnp.stack([dot(received, d_pre[p], 0, 0), dot(active[p], grad_in, 0, 0)]) for p in range(4)
    ]
    d_same = table_grad(d_logits, group_rows, padded, (0, 2), (d_received,))

    d_base = (
        d_same[0] + flip(d_same[1], "hidden", 1) + far_flip(across_x, "expert", 1).astype(F32)
    )

    w_near = flip(d_w[3], "hidden", 1), flip(d_w[2], "hidden", 1)
    w_sent = (d_w[1] + w_near[0]).astype(BF)
    w_far = far_flip(w_sent, "hidden", 2)
    d_gain_two, d_branch, d_after_attn = norm_back(
        after_attn,
        gain_full[1:2],
        (pick_place, *from_expert(d_received)),
        d_after_moe,
        pick="rows",
    )

    d_qkv, d_norm_part = attend_back(d_branch, packed, qkv, segment, (w_sent,))
    d_gain_one, d_high, d_low = norm_back(
        embedded,
        gain_full[0:1],
        [d_norm_part, flip(d_norm_part, "hidden", 1)],
        d_after_attn,
        scale=embed_scale,
        split=True,
    )

    attn_sent = attn_grad(normed_one, d_qkv, d_branch, attended, (d_high,))

    row_hot = hot_rows(place_own, n_expert * slots)
    d_rows = dot(row_hot, d_high) + dot(row_hot, d_low)
    d_gains = jnp.concatenate([d_gain_one, d_gain_two, d_gain_three])
    d_gains = d_gains.reshape(3, n_expert, own_rows).transpose(1, 0, 2).reshape(n_expert, 1, -1)
    gains_high = lax.reduce_precision(d_gains, 8, 7)
    gains_two = jnp.concatenate([gains_high, d_gains - gains_high], axis=1).astype(BF)
    gains_two = jnp.pad(gains_two, ((0, 0), (0, 14), (0, model_width - gains_two.shape[2])))
    attn_got = lax.all_to_all(
        attn_sent.reshape(n_expert, own_rows, 4 * head_width),
        "expert",
        split_axis=0,
        concat_axis=0,
        tiled=True,
    )
    sent = jnp.concatenate(
        [d_rows.astype(BF).reshape(n_expert, slots, model_width), gains_two], axis=1
    )
    got = lax.all_to_all(sent, "expert", split_axis=0, concat_axis=0, tiled=True)
    got_rows = got[:, :slots].reshape(n_expert * slots, model_width)

    def scatter_step(k, carry):
        d_far, ids_far, total = carry
        here = ids_far // vocab_rows == own_shard
        local = jnp.where(here, ids_far % vocab_rows, 0)
        d_sum = d_far[0].astype(F32) + d_far[1].astype(F32)
        total = total.at[local].add(jnp.where(here[:, None], d_sum, 0.0))
        ring = [(j, (j + 1) % n_expert) for j in range(n_expert)]
        return lax.ppermute(d_far, "expert", ring), lax.ppermute(ids_far, "expert", ring), total

    d_base = lax.fori_loop(
        0,
        jnp.where(any_overflow, n_expert, 0),
        scatter_step,
        ((d_high, d_low), ids, d_base),
    )[2]
    g_table, table_squares = finish(d_base, asked_rows, got_rows, vocab_rows)
    g_attn = jnp.sum(attn_got.astype(F32), axis=0)
    g_attn_in = g_attn[:, : 3 * head_width].reshape(own_rows, 3, head_width)
    g_attn_out = g_attn[:, 3 * head_width :]
    g_gains = jnp.sum(got[:, slots : slots + 2, : 3 * own_rows].astype(F32), axis=(0, 1))
    g_gains = g_gains.reshape(3, own_rows).T
    g_expert = d_w[0] + w_near[1] + w_far.astype(F32)
    g_expert_in = g_expert[0][None]
    g_expert_out = g_expert[1][None]

    squares = (
        jnp.sum(table_squares)
        + jnp.sum(g_attn * g_attn)
        + jnp.sum(g_expert * g_expert)
        + jnp.sum(g_gains * g_gains) / n_hidden
    )
    both_sums = jnp.stack([squares, loss_part * (2.0 / n_hidden)])
    both_sums = jnp.broadcast_to(jnp.pad(both_sums, (0, 126))[None], (n_expert, 128))
    both_sums = lax.all_to_all(both_sums, "expert", split_axis=0, concat_axis=0, tiled=True)
    both_sums = lax.all_gather(jnp.sum(both_sums, axis=0), "hidden", axis=0)
    both_sums = jnp.sum(both_sums, axis=0)
    clip_norm = jnp.sqrt(both_sums[0])
    loss_value = both_sums[1]
    clip_scale = jnp.minimum(1.0, CLIP_AT / clip_norm)
    table_up = adam_step(
        embed_table, embed_first, embed_second, g_table * clip_scale, RATE_MATRIX, DECAY
    )
    attn_in_up = adam_step(
        attn_in, attn_in_first, attn_in_second, g_attn_in * clip_scale, RATE_MATRIX, DECAY
    )
    attn_out_up = adam_step(
        attn_out, attn_out_first, attn_out_second, g_attn_out * clip_scale, RATE_MATRIX, DECAY
    )
    expert_in_up = adam_step(
        expert_in, expert_in_first, expert_in_second, g_expert_in * clip_scale, RATE_MATRIX, DECAY
    )
    expert_out_up = adam_step(
        expert_out,
        expert_out_first,
        expert_out_second,
        g_expert_out * clip_scale,
        RATE_MATRIX,
        DECAY,
    )
    gains_up = adam_step(
        norm_gains, gains_first, gains_second, g_gains * clip_scale, RATE_GAIN, 0.0
    )
    return (
        loss_value,
        clip_norm,
        *table_up,
        *attn_in_up,
        *attn_out_up,
        *expert_in_up,
        *expert_out_up,
        *gains_up,
    )


def solution(mesh):
    rows = P("expert", None)
    table = P(("expert", "hidden"), None)
    wide = P("expert", None, "hidden")
    flat = P("expert", "hidden")
    tall = P("expert", "hidden", None)
    groups = (table, wide, flat, wide, tall, rows)
    each = tuple(spec for spec in groups for _ in range(3))
    return jax.shard_map(
        on_device,
        mesh=mesh,
        in_specs=(rows, rows, rows, P(), *each),
        out_specs=(P(), P(), *each),
        check_vma=False,
    )
```

```python
from functools import partial

import jax
import jax.numpy as jnp
from jax import lax
from jax.experimental import pallas as pl
from jax.experimental.pallas import tpu as pltpu
from jax.sharding import PartitionSpec as P

HD = 64
DOCS_ROW = 8
STEP = 7


EPS_NORM = 1e-06
BETA_ONE = 0.9
BETA_TWO = 0.95
ADAM_EPS = 1e-08
RATE_MATRIX = 0.05
RATE_GAIN = 0.3
DECAY = 0.1
CLIP_AT = 0.005
NEVER = -1e30
BF = jnp.bfloat16
F32 = jnp.float32
VMEM = 56 * 1024 * 1024
SHORT = pl.CostEstimate(flops=1024, bytes_accessed=1024, transcendentals=0)


def flip(x, axis, k):
    return lax.ppermute(x, axis, [(j, j ^ k) for j in range(lax.axis_size(axis))])


def behind(x, after):
    return jnp.where(after == after, x, 0)


def far_flip(x, axis, k, after=None):
    pairs = [[j, j ^ k] for j in range(lax.axis_size(axis)) if not j & k]
    both = lax.all_gather(x, axis, axis_index_groups=pairs)
    upper = (lax.axis_index(axis) // k) % 2
    if after is not None:
        upper = behind(upper, after)
    return lax.dynamic_index_in_dim(both, 1 - upper, 0, keepdims=False), both


def hidden_gather(x, after=None):
    far = flip(x, "hidden", 2)
    if after is not None:
        far = behind(far, after)
    return [x, far, flip(x, "hidden", 1), flip(far, "hidden", 1)]


def piece_of(bits):
    return (bits >> 1) + 2 * (bits & 1)


def round_up(n, m):
    return -(-n // m) * m


def dot(a, b, ca=1, cb=0):
    return lax.dot_general(a, b, (((ca,), (cb,)), ((), ())), preferred_element_type=F32)


def hot_rows(place, count):
    return (jnp.arange(count, dtype=jnp.int32)[:, None] == place[None, :]).astype(BF)


def hot_columns(place, count):
    return (place[:, None] == jnp.arange(count, dtype=jnp.int32)[None, :]).astype(BF)


QB = 256
SPAN = 2


ANY = pl.BlockSpec(memory_space=pl.ANY)
WHOLE = pl.BlockSpec(memory_space=pltpu.VMEM)


def bias_of(first, second, axis, at_first, at_second):
    shape = (first.shape[0], second.shape[1])
    pos_a = lax.broadcasted_iota(jnp.int32, shape, 0) + at_first
    pos_b = lax.broadcasted_iota(jnp.int32, shape, 1) + at_second
    seen = (pos_a >= pos_b) if axis == 0 else (pos_b >= pos_a)
    return jnp.where(seen & (first == second), 0.0, NEVER)


def pack_kernel(in_ref, out_ref, *rest):
    o_ref = rest[-1]
    width = out_ref.shape[1]
    for c in range(3):
        o_ref[:, c * width : (c + 1) * width] = in_ref[c].astype(BF)
    o_ref[:, 3 * width :] = out_ref[...].astype(BF)


def pack(attn_in, attn_out, ready):
    rows, width = attn_out.shape
    return pl.pallas_call(
        pack_kernel,
        in_specs=[WHOLE] * 2 + [ANY] * len(ready),
        out_specs=WHOLE,
        out_shape=jax.ShapeDtypeStruct((rows, 4 * width), BF),
        name="pack",
    )(attn_in.transpose(1, 0, 2), attn_out, *ready)


def attend_kernel(rows_ref, w_ref, segr_ref, segc_ref, *rest):
    qkv_ref, o_ref, part_ref = rest[-3:]
    pieces, seq, width = o_ref.shape
    wide = 3 * width
    factor = jnp.asarray(HD**-0.5, BF)
    heads = [(p, c) for p in range(pieces) for c in range(0, width, HD)]
    for p in range(pieces):
        qkv_ref[p] = dot(rows_ref[...], w_ref[p, :, : 3 * width]).astype(BF)
    for b in range(seq // QB):
        lo, at, hi = max(0, b - SPAN) * QB, b * QB, (b + 1) * QB
        bias = bias_of(segc_ref[at:hi, :], segr_ref[:, lo:hi], 0, at, lo)
        scores = []
        for p, c in heads:
            q = qkv_ref[p, at:hi, c : c + HD] * factor
            scores.append(dot(q, qkv_ref[p, lo:hi, width + c : width + c + HD], 1, 1))
        probs = []
        for s in scores:
            s = s + bias
            e = jnp.exp(s - jnp.max(s, axis=1, keepdims=True))
            probs.append((e * (1.0 / jnp.sum(e, axis=1, keepdims=True))).astype(BF))
        outs = [
            dot(prob, qkv_ref[p, lo:hi, 2 * width + c : 2 * width + c + HD])
            for prob, (p, c) in zip(probs, heads, strict=True)
        ]
        for out, (p, c) in zip(outs, heads, strict=True):
            o_ref[p, at:hi, c : c + HD] = out.astype(BF)
    total = dot(o_ref[0], w_ref[0, :, wide : wide + width], 1, 1)
    for p in range(1, pieces):
        total += dot(o_ref[p], w_ref[p, :, wide : wide + width], 1, 1)
    part_ref[...] = total


def attend(rows, packed, width, seg, ready):
    seq, model = rows.shape
    pieces = packed.shape[0]
    return pl.pallas_call(
        attend_kernel,
        in_specs=[WHOLE] * 4 + [ANY] * len(ready),
        out_specs=[WHOLE] * 3,
        out_shape=[
            jax.ShapeDtypeStruct((pieces, seq, 3 * width), BF),
            jax.ShapeDtypeStruct((pieces, seq, width), BF),
            jax.ShapeDtypeStruct((seq, model), F32),
        ],
        compiler_params=pltpu.CompilerParams(vmem_limit_bytes=VMEM),
        cost_estimate=SHORT,
        name="attend",
    )(rows, packed, seg[None, :], seg[:, None], *ready)


def attend_back_kernel(branch_ref, w_ref, qkv_ref, segr_ref, segc_ref, *rest):
    d_ref, part_ref, g_ref, dk_acc, dv_acc = rest[-5:]
    pieces, seq, width = g_ref.shape
    wide = 3 * width
    scale = HD**-0.5
    factor = jnp.asarray(scale, BF)
    heads = [(p, c) for p in range(pieces) for c in range(0, width, HD)]
    for p in range(pieces):
        g_ref[p] = dot(branch_ref[...], w_ref[p, :, wide : wide + width]).astype(BF)
    dk_acc[...] = jnp.zeros_like(dk_acc)
    dv_acc[...] = jnp.zeros_like(dv_acc)
    for b in range(seq // QB):
        lo, at, hi = max(0, b - SPAN) * QB, b * QB, (b + 1) * QB
        bias = bias_of(segc_ref[lo:hi, :], segr_ref[:, at:hi], 1, lo, at)
        for group in (heads[: len(heads) // 2], heads[len(heads) // 2 :]):
            qs = [qkv_ref[p, at:hi, c : c + HD] * factor for p, c in group]
            ks = [qkv_ref[p, lo:hi, width + c : width + c + HD] for p, c in group]
            gs = [g_ref[p, at:hi, c : c + HD] for p, c in group]
            scores = [dot(k, q, 1, 1) for k, q in zip(ks, qs, strict=True)]
            d_probs = [
                dot(qkv_ref[p, lo:hi, 2 * width + c : 2 * width + c + HD], g, 1, 1)
                for (p, c), g in zip(group, gs, strict=True)
            ]
            probs, d_scores = [], []
            for s, d_prob in zip(scores, d_probs, strict=True):
                s = s + bias
                e = jnp.exp(s - jnp.max(s, axis=0, keepdims=True))
                prob = e * (1.0 / jnp.sum(e, axis=0, keepdims=True))
                centre = jnp.sum(prob * d_prob, axis=0, keepdims=True)
                d_scores.append((prob * (d_prob - centre)).astype(BF))
                probs.append(prob.astype(BF))
            dqs = [dot(d, k, 0, 0) for d, k in zip(d_scores, ks, strict=True)]
            dks = [dot(d, q) for d, q in zip(d_scores, qs, strict=True)]
            dvs = [dot(prob, g) for prob, g in zip(probs, gs, strict=True)]
            for i, (p, c) in enumerate(group):
                d_ref[p, at:hi, c : c + HD] = (dqs[i] * scale).astype(BF)
                dk_acc[p, lo:hi, c : c + HD] += dks[i]
                dv_acc[p, lo:hi, c : c + HD] += dvs[i]
    d_ref[:, :, width : 2 * width] = dk_acc[...].astype(BF)
    d_ref[:, :, 2 * width :] = dv_acc[...].astype(BF)
    total = dot(d_ref[0], w_ref[0, :, : 3 * width], 1, 1)
    for p in range(1, pieces):
        total += dot(d_ref[p], w_ref[p, :, : 3 * width], 1, 1)
    part_ref[...] = total


def attend_back(branch, packed, qkv, seg, ready):
    seq, model = branch.shape
    pieces, _, width = qkv.shape
    return pl.pallas_call(
        attend_back_kernel,
        in_specs=[WHOLE] * 5 + [ANY] * len(ready),
        out_specs=[WHOLE] * 2,
        out_shape=[
            jax.ShapeDtypeStruct((pieces, seq, width), BF),
            jax.ShapeDtypeStruct((seq, model), F32),
        ],
        scratch_shapes=[
            pltpu.VMEM((pieces, seq, width // 3), BF),
            pltpu.VMEM((pieces, seq, width // 3), F32),
            pltpu.VMEM((pieces, seq, width // 3), F32),
        ],
        compiler_params=pltpu.CompilerParams(vmem_limit_bytes=VMEM),
        cost_estimate=SHORT,
        name="attend_back",
    )(branch, packed, qkv, seg[None, :], seg[:, None], *ready)


def attn_grad_kernel(rows_ref, d_ref, branch_ref, o_ref, *rest):
    out_ref = rest[-1]
    width = d_ref.shape[2]
    out_ref[:, :width] = dot(rows_ref[...], d_ref[0], 0, 0).astype(BF)
    out_ref[:, width:] = dot(branch_ref[...], o_ref[0], 0, 0).astype(BF)


def attn_grad(rows, d_qkv, branch, attended, ready):
    model = rows.shape[1]
    seq, third = attended.shape[1:]
    one = pl.BlockSpec((1, seq, 3 * third), lambda i: (0, 0, 0))
    two = pl.BlockSpec((1, seq, third), lambda i: (0, 0, 0))
    full = pl.BlockSpec((seq, model), lambda i: (0, 0))
    return pl.pallas_call(
        attn_grad_kernel,
        grid=(1,),
        in_specs=[full, one, full, two] + [ANY] * len(ready),
        out_specs=pl.BlockSpec((model, 4 * third), lambda i: (0, 0)),
        out_shape=jax.ShapeDtypeStruct((model, 4 * third), BF),
        compiler_params=pltpu.CompilerParams(vmem_limit_bytes=VMEM),
        cost_estimate=SHORT,
        name="attn_grad",
    )(rows, d_qkv, branch, attended, *ready)


def picked(place_ref, *row_refs):
    count = row_refs[0].shape[0]
    at = lax.broadcasted_iota(jnp.int32, (place_ref.shape[0], count), 1)
    total = None
    for q, ref in enumerate(row_refs):
        part = dot((at == place_ref[...] - q * count).astype(BF), ref[...])
        total = part if total is None else total + part
    return total


def pick_norm_kernel(scale, pick, parts, base, *refs):
    first_refs, refs = refs[:parts], refs[parts:]
    if base:
        base_ref, refs = refs[0], refs[1:]
    gain_ref, sum_ref, norm_ref = refs[0], refs[-2], refs[-1]
    if pick:
        x = picked(*first_refs)
    else:
        x = first_refs[0][...]
        for ref in first_refs[1:]:
            x = x + ref[...]
    if base:
        x = base_ref[...] + x
    if scale != 1.0:
        x = x * scale
    sum_ref[...] = x
    root = lax.rsqrt(jnp.mean(x * x, axis=1, keepdims=True) + EPS_NORM)
    norm_ref[...] = (x * root * gain_ref[...]).astype(BF)


def pick_norm(first, base, gain, scale=1.0, pick=True, ready=()):
    tokens = first[0].shape[0]
    width = gain.shape[1]
    block = min(tokens, 256)
    by_rows = pl.BlockSpec((block, width), lambda i: (i, 0))
    if pick:
        first = (first[0][:, None], *first[1:])
        specs = [pl.BlockSpec((block, 1), lambda i: (i, 0))]
        specs += [pl.BlockSpec(r.shape, lambda i: (0, 0)) for r in first[1:]]
    else:
        specs = [by_rows] * len(first)
    has_base = base is not None
    return pl.pallas_call(
        partial(pick_norm_kernel, scale, pick, len(first), has_base),
        grid=(tokens // block,),
        in_specs=specs
        + [by_rows] * has_base
        + [pl.BlockSpec((1, width), lambda i: (0, 0))]
        + [ANY] * len(ready),
        out_specs=[by_rows, by_rows],
        out_shape=[
            jax.ShapeDtypeStruct((tokens, width), F32),
            jax.ShapeDtypeStruct((tokens, width), BF),
        ],
        compiler_params=pltpu.CompilerParams(vmem_limit_bytes=VMEM),
        cost_estimate=SHORT,
        name="pick_norm",
    )(*first, *((base,) if has_base else ()), gain, *ready)


def norm_back_kernel(scale, parts, pick, rest, split, x_ref, gain_ref, *refs):
    g_refs, refs = refs[:parts], refs[parts:]
    if rest:
        rest_ref, refs = refs[0], refs[1:]
    gain_out, one_ref, two_ref = refs[-3:]
    x = x_ref[...]
    if pick == "rows":
        g = picked(*g_refs)
    elif pick == "blocks":
        which = g_refs[0][pl.program_id(0)]
        g = g_refs[1][...].astype(F32)
        for q, ref in enumerate(g_refs[2:], 1):
            g = jnp.where(which == q, ref[...].astype(F32), g)
    else:
        g = g_refs[0][...].astype(F32)
        for ref in g_refs[1:]:
            g = g + ref[...].astype(F32)
    root = lax.rsqrt(jnp.mean(x * x, axis=1, keepdims=True) + EPS_NORM)
    scaled = x * root
    d_gain = jnp.sum(g * scaled, axis=0, keepdims=True)
    g = g * gain_ref[...]
    dx = root * (g - scaled * jnp.mean(g * scaled, axis=1, keepdims=True))
    if rest:
        dx = rest_ref[...] + dx
    if scale != 1.0:
        dx = dx * scale
    high = dx.astype(BF)
    one_ref[...] = high
    two_ref[...] = (dx - high.astype(F32)).astype(BF) if split else dx

    @pl.when(pl.program_id(0) == 0)
    def _():
        gain_out[...] = d_gain

    @pl.when(pl.program_id(0) > 0)
    def _():
        gain_out[...] += d_gain


def norm_back(x, gain, gradients, rest=None, scale=1.0, split=False, pick="", ready=()):
    tokens, width = x.shape
    block = min(tokens, 256)
    by_rows = pl.BlockSpec((block, width), lambda i: (i, 0))
    one_row = pl.BlockSpec((1, width), lambda i: (0, 0))
    has_rest = rest is not None
    whole = [pl.BlockSpec(g.shape, lambda i: (0, 0)) for g in gradients[1:]]
    if pick == "rows":
        gradients = (gradients[0][:, None], *gradients[1:])
        specs = [pl.BlockSpec((block, 1), lambda i: (i, 0)), *whole]
    elif pick == "blocks":
        specs = [pl.BlockSpec(memory_space=pltpu.SMEM), *whole]
    else:
        specs = [by_rows] * len(gradients)
    return pl.pallas_call(
        partial(norm_back_kernel, scale, len(gradients), pick, has_rest, split),
        grid=(tokens // block,),
        in_specs=[by_rows, one_row] + specs + [by_rows] * has_rest + [ANY] * len(ready),
        out_specs=[one_row, by_rows, by_rows],
        out_shape=[
            jax.ShapeDtypeStruct((1, width), F32),
            jax.ShapeDtypeStruct((tokens, width), BF),
            jax.ShapeDtypeStruct((tokens, width), BF if split else F32),
        ],
        compiler_params=pltpu.CompilerParams(vmem_limit_bytes=VMEM),
        cost_estimate=SHORT,
        name="norm_back",
    )(x, gain, *gradients, *((rest,) if has_rest else ()), *ready)


ERFC = (
    -1.26551223,
    1.00002368,
    0.37409196,
    0.09678418,
    -0.18628806,
    0.27886807,
    -1.13520398,
    1.48851587,
    -0.82215223,
    0.17087277,
)


def gelu_and_slope(x):
    t = 1.0 / (1.0 + 0.35355339059327373 * jnp.abs(x))
    poly = jnp.full_like(t, ERFC[-1])
    for c in ERFC[-2::-1]:
        poly = poly * t + c
    square = 0.5 * x * x
    half = 0.5 * t * jnp.exp(poly - square)
    below = jnp.where(x >= 0.0, 1.0 - half, half)
    return x * below, below + x * jnp.exp(-square) * 0.3989422804014327


def expert_kernel(rows_ref, *refs):
    w_refs, out_ref, active_refs, slope_refs = refs[:4], refs[4], refs[5:9], refs[9:]
    rows = rows_ref[...]
    total = None
    for w_ref, active_ref, slope_ref in zip(w_refs, active_refs, slope_refs, strict=True):
        value, slope_ref[...] = gelu_and_slope(dot(rows, w_ref[0]))
        active = value.astype(BF)
        active_ref[...] = active
        product = dot(active, w_ref[1])
        total = product if total is None else total + product
    out_ref[...] = total.astype(BF)


def expert(rows, weights):
    hidden = jax.ShapeDtypeStruct((rows.shape[0], weights[0].shape[2]), BF)
    slope = jax.ShapeDtypeStruct(hidden.shape, F32)
    out, *rest = pl.pallas_call(
        expert_kernel,
        in_specs=[WHOLE] * 5,
        out_specs=[WHOLE] * 9,
        out_shape=[jax.ShapeDtypeStruct(rows.shape, BF)] + [hidden] * 4 + [slope] * 4,
        compiler_params=pltpu.CompilerParams(vmem_limit_bytes=VMEM),
        cost_estimate=SHORT,
        name="expert",
    )(rows, *weights)
    return out, rest[:4], rest[4:]


def expert_back_kernel(grad_ref, *refs):
    w_refs, slope_refs, refs = refs[:4], refs[4:8], refs[8:]
    out_ref, d_refs = refs[-5], refs[-4:]
    grad = grad_ref[...]
    total = None
    for w_ref, slope_ref, d_ref in zip(w_refs, slope_refs, d_refs, strict=True):
        d_pre = (dot(grad, w_ref[1], 1, 1) * slope_ref[...]).astype(BF)
        d_ref[...] = d_pre
        product = dot(d_pre, w_ref[0], 1, 1)
        total = product if total is None else total + product
    out_ref[...] = total.astype(BF)


def expert_back(grad, weights, slopes, ready):
    return pl.pallas_call(
        expert_back_kernel,
        in_specs=[WHOLE] * 9 + [ANY] * len(ready),
        out_specs=[WHOLE] * 5,
        out_shape=[jax.ShapeDtypeStruct(grad.shape, BF)]
        + [jax.ShapeDtypeStruct(slope.shape, BF) for slope in slopes],
        compiler_params=pltpu.CompilerParams(vmem_limit_bytes=VMEM),
        cost_estimate=SHORT,
        name="expert_back",
    )(grad, *weights, *slopes, *ready)


def part_rows(padded):
    return max(r for r in range(32, 385, 32) if padded % r == 0)


def cast_pick_kernel(real, place_ref, x_ref, table_ref, o_ref, acc):
    j = pl.program_id(0)
    rows = x_ref.shape[0]
    at = lax.broadcasted_iota(jnp.int32, x_ref.shape, 0) + j * rows
    table_ref[...] = jnp.where(at < real, x_ref[...], 0.0).astype(BF)
    column = lax.broadcasted_iota(jnp.int32, (place_ref.shape[0], rows), 1) + j * rows
    found = dot((column == place_ref[...]).astype(BF), table_ref[...])

    @pl.when(j == 0)
    def _():
        acc[...] = found

    @pl.when(j > 0)
    def _():
        acc[...] += found

    @pl.when(j == pl.num_programs(0) - 1)
    def _():
        o_ref[...] = acc[...].astype(BF)


def cast_pick(place, x, padded):
    real, width = x.shape
    rows = part_rows(padded)
    count = place.shape[0]
    return pl.pallas_call(
        partial(cast_pick_kernel, real),
        grid=(padded // rows,),
        in_specs=[
            pl.BlockSpec((count, 1), lambda j: (0, 0)),
            pl.BlockSpec((rows, width), lambda j: (j, 0)),
        ],
        out_specs=[
            pl.BlockSpec((rows, width), lambda j: (j, 0)),
            pl.BlockSpec((count, width), lambda j: (0, 0)),
        ],
        out_shape=[
            jax.ShapeDtypeStruct((padded, width), BF),
            jax.ShapeDtypeStruct((count, width), BF),
        ],
        scratch_shapes=[pltpu.VMEM((count, width), F32)],
        compiler_params=pltpu.CompilerParams(vmem_limit_bytes=VMEM),
        cost_estimate=SHORT,
        name="cast_pick",
    )(place[:, None], x)


def turn_kernel(a_ref, b_ref, c_ref, d_ref, o_ref):
    o_ref[...] = jnp.concatenate([a_ref[...], b_ref[...], c_ref[...], d_ref[...]], axis=0).T


def turned(slices):
    padded, width = slices[0].shape
    rows = part_rows(padded)
    return pl.pallas_call(
        turn_kernel,
        grid=(padded // rows,),
        in_specs=[pl.BlockSpec((rows, width), lambda j: (j, 0))] * 4,
        out_specs=pl.BlockSpec((width, 4 * rows), lambda j: (0, j)),
        out_shape=jax.ShapeDtypeStruct((width, 4 * padded), BF),
        compiler_params=pltpu.CompilerParams(vmem_limit_bytes=VMEM),
        cost_estimate=pl.CostEstimate(flops=0, bytes_accessed=24 * padded * width, transcendentals=0),
        name="turned",
    )(*slices)


def logits_kernel(
    real, a_ref, b_ref, c_ref, d_ref, rows_ref, col_ref, *rest
):
    out_ref, peak_ref, stat_ref, peak_s, sum_s, hit_s = rest[-6:]
    j = pl.program_id(0)
    tokens = rows_ref.shape[0]
    part = a_ref.shape[0]

    @pl.when(j == 0)
    def _():
        peak_s[...] = jnp.full((8, tokens), NEVER, F32)
        sum_s[...] = jnp.zeros((8, tokens), F32)
        hit_s[...] = jnp.zeros((8, tokens), F32)

    away = col_ref[...] - j * (4 * part) - lax.broadcasted_iota(jnp.int32, (8, tokens), 0)
    peak, total, hit = peak_s[...], sum_s[...], hit_s[...]
    rows = rows_ref[...]
    tail = round_up(part * (-(-real // part)) - real, 8)
    for q, ref in enumerate((a_ref, b_ref, c_ref, d_ref)):
        logits = dot(ref[...], rows, 1, 1)
        if tail:
            at = lax.broadcasted_iota(jnp.int32, (tail, tokens), 0) + (j + 1) * part - tail
            end = jnp.where(at < real, logits[part - tail :], NEVER)
            logits = jnp.concatenate([logits[: part - tail], end], axis=0)
        tiles = logits.reshape(part // 8, 8, tokens)
        new = jnp.maximum(peak, jnp.max(tiles, axis=0))
        powers = jnp.exp(tiles - new[None])
        out_ref[q * part : (q + 1) * part, :] = powers.reshape(part, tokens)
        peak_ref[q * 8 : (q + 1) * 8, :] = new
        total = total * jnp.exp(peak - new) + jnp.sum(powers, axis=0)
        for i in range(part // 8):
            hit = hit + jnp.where(away == q * part + 8 * i, tiles[i], 0.0)
        peak = new
    peak_s[...], sum_s[...], hit_s[...] = peak, total, hit

    @pl.when(j == pl.num_programs(0) - 1)
    def _():
        top = jnp.max(peak, axis=0, keepdims=True)
        stat_ref[0:1, :] = top
        stat_ref[1:2, :] = jnp.sum(total * jnp.exp(peak - top), axis=0, keepdims=True)
        stat_ref[2:3, :] = jnp.sum(hit, axis=0, keepdims=True)
        stat_ref[3:8, :] = jnp.zeros((5, tokens), F32)


def head_logits(slices, rows, col, real, ready=()):
    padded, width = slices[0].shape
    tokens = rows.shape[0]
    part = part_rows(padded)
    steps = padded // part
    return pl.pallas_call(
        partial(logits_kernel, real),
        grid=(steps,),
        in_specs=[pl.BlockSpec((part, width), lambda j: (j, 0))] * 4
        + [
            pl.BlockSpec((tokens, width), lambda j: (0, 0)),
            pl.BlockSpec((1, tokens), lambda j: (0, 0)),
        ]
        + [ANY] * len(ready),
        out_specs=[
            pl.BlockSpec((4 * part, tokens), lambda j: (j, 0)),
            pl.BlockSpec((32, tokens), lambda j: (j, 0)),
            pl.BlockSpec((8, tokens), lambda j: (0, 0)),
        ],
        out_shape=[
            jax.ShapeDtypeStruct((4 * padded, tokens), F32),
            jax.ShapeDtypeStruct((32 * steps, tokens), F32),
            jax.ShapeDtypeStruct((8, tokens), F32),
        ],
        scratch_shapes=[pltpu.VMEM((8, tokens), F32)] * 3,
        compiler_params=pltpu.CompilerParams(vmem_limit_bytes=VMEM),
        cost_estimate=pl.CostEstimate(flops=16 * padded * tokens * width, bytes_accessed=16 * padded * tokens, transcendentals=0),
        name="head_logits",
    )(*slices, rows, col, *ready)


def head_back_kernel(table_ref, power_ref, peak_ref, col_ref, side_ref, *rest):
    d_ref, out_ref, acc = rest[-3:]
    j = pl.program_id(0)
    block, tokens = power_ref.shape
    part = block // 4
    away = col_ref[...] - j * block - lax.broadcasted_iota(jnp.int32, (8, tokens), 0)
    log_total, weight = side_ref[0:1, :], side_ref[1:2, :]
    pieces = []
    for q in range(4):
        factor = jnp.exp(peak_ref[q * 8 : (q + 1) * 8, :] - log_total) * weight
        for i in range(part // 8):
            at = q * part + 8 * i
            less = jnp.where(away == at, weight, 0.0)
            pieces.append(power_ref[at : at + 8, :] * factor - less)
    d = jnp.concatenate(pieces, axis=0).astype(BF)
    d_ref[...] = d
    product = dot(table_ref[...], d)

    @pl.when(j == 0)
    def _():
        acc[...] = product

    @pl.when(j > 0)
    def _():
        acc[...] += product

    @pl.when(j == pl.num_programs(0) - 1)
    def _():
        out_ref[...] = acc[...].T.astype(out_ref.dtype)


def head_back(table_t, powers, peaks, at, col, side, ready=()):
    width, vocab = table_t.shape
    tokens = col.shape[1]
    steps = peaks.shape[0] // 32
    block = vocab // steps
    return pl.pallas_call(
        head_back_kernel,
        grid=(steps,),
        in_specs=[
            pl.BlockSpec((width, block), lambda j: (0, j)),
            pl.BlockSpec((block, tokens), lambda j: (j, at)),
            pl.BlockSpec((32, tokens), lambda j: (j, at)),
            pl.BlockSpec((1, tokens), lambda j: (0, 0)),
            pl.BlockSpec((8, tokens), lambda j: (0, 0)),
        ]
        + [ANY] * len(ready),
        out_specs=[
            pl.BlockSpec((block, tokens), lambda j: (j, 0)),
            pl.BlockSpec((tokens, width), lambda j: (0, 0)),
        ],
        out_shape=[
            jax.ShapeDtypeStruct((vocab, tokens), BF),
            jax.ShapeDtypeStruct((tokens, width), BF),
        ],
        scratch_shapes=[pltpu.VMEM((width, tokens), F32)],
        compiler_params=pltpu.CompilerParams(vmem_limit_bytes=VMEM),
        cost_estimate=pl.CostEstimate(flops=4 * vocab * tokens * width, bytes_accessed=6 * vocab * tokens, transcendentals=0),
        name="head_back",
    )(table_t, powers, peaks, col, side, *ready)


def table_grad_kernel(count, *refs):
    d_refs, row_refs, out_refs = refs[: 2 * count], refs[2 * count : 3 * count], refs[-2:]
    total = None
    for k in range(count):
        both = jnp.concatenate([d_refs[2 * k][...], d_refs[2 * k + 1][...]], axis=0)
        product = dot(both, row_refs[k][...])
        total = product if total is None else total + product
    part = out_refs[0].shape[0]
    for q in range(2):
        out_refs[q][...] = total[q * part : (q + 1) * part].astype(out_refs[q].dtype)


def table_grad(ds, rows, padded, which, ready):
    width = rows[0].shape[1]
    part = part_rows(padded)

    def spec(tokens, q):
        return pl.BlockSpec((part, tokens), lambda j: (4 * j + q, 0))

    return pl.pallas_call(
        partial(table_grad_kernel, len(ds)),
        grid=(padded // part,),
        in_specs=[spec(d.shape[1], q) for d in ds for q in which]
        + [pl.BlockSpec(r.shape, lambda j: (0, 0)) for r in rows]
        + [ANY] * len(ready),
        out_specs=[pl.BlockSpec((part, width), lambda j: (j, 0))] * 2,
        out_shape=[jax.ShapeDtypeStruct((padded, width), t) for t in (F32, BF)],
        compiler_params=pltpu.CompilerParams(vmem_limit_bytes=VMEM),
        cost_estimate=pl.CostEstimate(
            flops=4 * padded * width * sum(d.shape[1] for d in ds),
            bytes_accessed=8 * padded * width,
            transcendentals=0,
        ),
        name="table_grad",
    )(*[d for d in ds for _ in which], *rows, *ready)


def finish_kernel(real, base_ref, place_ref, rows_ref, out_ref, square_ref):
    rows = base_ref.shape[0]
    first = pl.program_id(0) * rows
    at = lax.broadcasted_iota(jnp.int32, (rows, place_ref.shape[1]), 0) + first
    spread = dot((at == place_ref[...]).astype(BF), rows_ref[...])
    g = base_ref[...] + spread
    out_ref[...] = g
    inside = lax.broadcasted_iota(jnp.int32, g.shape, 0) + first < real
    g = jnp.where(inside, g, 0.0)
    squares = jnp.sum(g * g, axis=0, keepdims=True)

    @pl.when(pl.program_id(0) == 0)
    def _():
        square_ref[...] = squares

    @pl.when(pl.program_id(0) > 0)
    def _():
        square_ref[...] += squares


def finish(base, place, rows, real):
    padded, width = base.shape
    part = part_rows(padded)
    block = pl.BlockSpec((part, width), lambda j: (j, 0))
    return pl.pallas_call(
        partial(finish_kernel, real),
        grid=(padded // part,),
        in_specs=[
            block,
            pl.BlockSpec((1, place.shape[0]), lambda j: (0, 0)),
            pl.BlockSpec(rows.shape, lambda j: (0, 0)),
        ],
        out_specs=[block, pl.BlockSpec((1, width), lambda j: (0, 0))],
        out_shape=[
            jax.ShapeDtypeStruct((real, width), F32),
            jax.ShapeDtypeStruct((1, width), F32),
        ],
        compiler_params=pltpu.CompilerParams(vmem_limit_bytes=VMEM),
        cost_estimate=SHORT,
        name="finish",
    )(base, place[None, :], rows)


def adam_step(weight, first_moment, second_moment, gradient, step_rate, weight_decay):
    first_moment = BETA_ONE * first_moment + (1.0 - BETA_ONE) * gradient
    second_moment = BETA_TWO * second_moment + (1.0 - BETA_TWO) * gradient * gradient
    update = (
        first_moment
        / (1.0 - BETA_ONE**STEP)
        / (jnp.sqrt(second_moment / (1.0 - BETA_TWO**STEP)) + ADAM_EPS)
    )
    return (weight - step_rate * (update + weight_decay * weight), first_moment, second_moment)


def combine_stats(left, right):
    peak = jnp.maximum(left[0], right[0])
    total = left[1] * jnp.exp(left[0] - peak) + right[1] * jnp.exp(right[0] - peak)
    return jnp.stack([peak, total, left[2] + right[2]])


def on_device(
    token_ids,
    target_ids,
    doc_segments,
    hash_experts,
    embed_table,
    embed_first,
    embed_second,
    attn_in,
    attn_in_first,
    attn_in_second,
    attn_out,
    attn_out_first,
    attn_out_second,
    expert_in,
    expert_in_first,
    expert_in_second,
    expert_out,
    expert_out_first,
    expert_out_second,
    norm_gains,
    gains_first,
    gains_second,
):
    n_expert = lax.axis_size("expert")
    n_hidden = lax.axis_size("hidden")
    assert n_hidden == 4 and token_ids.shape[0] == 1
    e_index = lax.axis_index("expert")
    h_index = lax.axis_index("hidden")
    tok_count = token_ids.shape[1]
    vocab_rows, model_width = embed_table.shape
    embed_scale = model_width**0.5
    ids = token_ids[0]
    targets = target_ids[0]
    segment = doc_segments[0]
    token_at = jnp.arange(tok_count, dtype=jnp.int32)

    padded = round_up(vocab_rows, 32)
    own_rows = attn_in.shape[0]
    head_width = attn_in.shape[2]

    slots = round_up(5 * tok_count // (4 * n_expert * n_hidden), 8)
    shard = ids // vocab_rows
    shard_e, shard_h = shard // n_hidden, shard % n_hidden
    same_id = ids[:, None] == ids[None, :]
    first_at = jnp.min(jnp.where(same_id, token_at[None, :], tok_count), axis=1)
    is_first = first_at == token_at
    rank = jnp.sum(
        (
            (shard[:, None] == shard[None, :])
            & is_first[None, :]
            & (token_at[None, :] < first_at[:, None])
        ).astype(jnp.int32),
        axis=1,
    )
    overflow = jnp.max(rank) >= slots
    place_own = jnp.where(
        (shard_h == h_index) & (rank < slots), shard_e * slots + rank, -1
    )
    wanted = jnp.max(
        jnp.where(
            jnp.arange(n_expert * slots, dtype=jnp.int32)[:, None] == place_own[None, :],
            (ids % vocab_rows)[None, :],
            -1,
        ),
        axis=1,
    )
    own_gains = norm_gains.astype(BF).astype(F32).T.reshape(1, 3 * own_rows)
    own_gains = jnp.pad(own_gains, ((0, 0), (0, round_up(3 * own_rows, 128) - 3 * own_rows)))
    asked = jnp.concatenate(
        [
            wanted.reshape(n_expert, slots).astype(F32),
            jnp.broadcast_to(overflow.astype(F32), (n_expert, 128 - slots)),
            jnp.broadcast_to(own_gains, (n_expert, own_gains.shape[1])),
        ],
        axis=1,
    )

    asked = lax.all_to_all(asked, "expert", split_axis=0, concat_axis=0, tiled=True)
    any_overflow = jnp.max(asked[:, slots:128]) > 0
    asked_rows = asked[:, :slots].astype(jnp.int32).reshape(n_expert * slots)
    gain_full = asked[:, 128 : 128 + 3 * own_rows].reshape(n_expert, 3, own_rows)
    gain_full = gain_full.transpose(1, 0, 2).reshape(3, model_width)

    capacity = 3 * tok_count // (2 * n_expert)
    quarter = capacity // n_hidden
    expert_ids = hash_experts[ids]
    onehot = (expert_ids[:, None] == jnp.arange(n_expert, dtype=jnp.int32)).astype(jnp.int32)
    before = jnp.cumsum(onehot, axis=0) - onehot
    slot_rank = jnp.sum(before * onehot, axis=1)
    kept = slot_rank < capacity
    slot_h = slot_rank // quarter
    slot_in = expert_ids * quarter + slot_rank % quarter
    rows_dev = n_expert * quarter
    fill_place = jnp.where(kept & (slot_h == h_index), slot_in, -1)
    pick_place = jnp.where(kept, piece_of(slot_h ^ h_index) * rows_dev + slot_in, -1)

    asked_rows = jnp.where(any_overflow, -1, asked_rows)
    table_own, answer = cast_pick(asked_rows, embed_table, padded)
    packed = pack(attn_in, attn_out, (asked_rows,))
    packed = jnp.stack([packed, flip(packed, "hidden", 2)])
    packed = lax.all_gather(packed, "expert", axis=1, tiled=True)
    weights_own = jnp.stack([expert_in[0], expert_out[0]]).astype(BF)

    n_all = n_expert * n_hidden
    own_shard = e_index * n_hidden + h_index
    everyone = [(j, (j + 1) % n_all) for j in range(n_all)]

    answer = lax.all_to_all(
        answer.reshape(n_expert, slots, model_width),
        "expert",
        split_axis=0,
        concat_axis=0,
        tiled=True,
    )
    answers = hidden_gather(answer.reshape(n_expert * slots, model_width))
    place_all = piece_of(shard_h ^ h_index) * (n_expert * slots) + shard_e * slots + rank

    def look_up_step(k, carry):
        table_far, found = carry
        here = (own_shard - k + n_all) % n_all
        place = jnp.where(shard == here, ids % vocab_rows, -1)
        row = dot(hot_columns(place, padded), table_far).astype(BF)
        row = jnp.pad(row, ((0, 4 * n_expert * slots - tok_count), (0, 0)))
        parts = row.reshape(4, n_expert * slots, model_width)
        found = [jnp.where(k == 0, 0, found[q]) + parts[q] for q in range(4)]
        return lax.ppermute(table_far, ("expert", "hidden"), everyone), found

    answers = lax.fori_loop(
        0, jnp.where(any_overflow, n_all, 0), look_up_step, (table_own, answers)
    )[1]
    place_all = jnp.where(any_overflow, token_at, place_all)
    embedded, normed_one = pick_norm(
        (place_all, *answers), None, gain_full[0:1], embed_scale, ready=(fill_place, pick_place)
    )

    qkv, attended, attn_part = attend(normed_one, packed, head_width, segment, ())
    after_attn, normed_two = pick_norm(
        (attn_part, flip(attn_part, "hidden", 1)),
        embedded,
        gain_full[1:2],
        pick=False,
    )

    fill_hot = hot_rows(fill_place, rows_dev)

    def to_expert(rows_in, after=None):
        block = dot(fill_hot, rows_in).astype(BF)
        if after is not None:
            block = behind(block, after)
        return lax.all_to_all(block, "expert", split_axis=0, concat_axis=0, tiled=True)

    def from_expert(rows_in, after=None):
        block = lax.all_to_all(rows_in, "expert", split_axis=0, concat_axis=0, tiled=True)
        return hidden_gather(block.reshape(rows_dev, model_width), after)

    received = to_expert(normed_two)
    weights_y, _ = far_flip(weights_own, "hidden", 2, received[0, 0])
    expert_w = [
        weights_own,
        weights_y,
        flip(weights_own, "hidden", 1),
        flip(weights_y, "hidden", 1),
    ]
    expert_result, active, slope = expert(received, expert_w)
    after_moe, final_rows = pick_norm(
        (pick_place, *from_expert(expert_result)),
        after_attn,
        gain_full[2:3],
    )

    slice_x, _ = far_flip(table_own, "expert", 1, final_rows[0, 0])
    slices = [table_own, slice_x, flip(table_own, "hidden", 1), flip(slice_x, "hidden", 1)]
    table_t = turned(slices)
    part = part_rows(padded)

    half, fourth = tok_count // 2, tok_count // 4
    own_at = (h_index & 1) * half + (h_index >> 1) * fourth
    other_at = (h_index & 1) * half + (1 - (h_index >> 1)) * fourth
    n_far = n_expert // 2

    def own_order(x):
        return jnp.concatenate(
            [
                lax.dynamic_slice_in_dim(x, own_at, fourth, x.ndim - 1),
                lax.dynamic_slice_in_dim(x, other_at, fourth, x.ndim - 1),
            ],
            axis=-1,
        )

    counts = jnp.sum((segment[:, None] == segment[None, :]).astype(F32), axis=1)
    weights = 1.0 / counts / (n_expert * DOCS_ROW)
    about = own_order(jnp.stack([targets.astype(F32), weights]))
    about_all = [about] + [flip(about, "expert", 2 * k) for k in range(1, n_far)]
    own_part = lax.dynamic_slice_in_dim(final_rows, own_at, fourth, 0)
    other_part = lax.dynamic_slice_in_dim(final_rows, other_at, fourth, 0)
    far_rows = [flip(own_part, "expert", 2 * k) for k in range(1, n_far)]

    columns = []
    for k in range(n_far):
        target = about_all[k][0].astype(jnp.int32)
        block_of = target // vocab_rows
        away_e = (block_of // n_hidden) ^ e_index
        away_h = (block_of % n_hidden) ^ h_index
        mine = (away_e < 2) & (away_h < 2)
        row_of = target % vocab_rows
        column = (row_of // part) * (4 * part) + (away_e + 2 * away_h) * part + row_of % part
        columns.append(jnp.where(mine, column, -1)[None, :])
    head_rows, onward = [jnp.concatenate([own_part, other_part])], []
    powers, stats = [], []
    for k, far in enumerate(far_rows, 1):
        onward.append(behind(far, table_t[0, 0].astype(F32)) if k > 1 else far)
        head_rows.append(jnp.concatenate([onward[-1], flip(onward[-1], "hidden", 2)]))
    for k in range(0, n_far, 2):
        one, two, stat = head_logits(
            slices,
            jnp.concatenate(head_rows[k : k + 2]),
            jnp.concatenate(columns[k : k + 2], axis=1),
            vocab_rows,
            () if k else (table_t, *onward[1:]),
        )
        powers.append((one, two))
        stats += [stat[:3, :half], stat[:3, half:]]
    stat = jnp.stack(stats, axis=1)
    across = flip(stat, "hidden", 2)
    stat = combine_stats(stat, jnp.concatenate([across[..., fourth:], across[..., :fourth]], axis=2))
    far_stats = [flip(stat, "expert", 2 * k) for k in range(1, n_far)]
    for k in range(1, n_far):
        far = jnp.stack([far_stats[k - 1][:, j ^ k] for j in range(n_far)], axis=1)
        stat = combine_stats(stat, far)
    log_total = stat[0] + jnp.log(stat[1])
    loss_part = jnp.sum((log_total[0] - stat[2, 0]) * about[1])

    groups = [[0], [1]] + [[k, k + 1] for k in range(2, n_far, 2)]
    group_rows = [jnp.concatenate([head_rows[k] for k in group]) for group in groups]
    d_logits, d_parts, on_y = [None] * len(groups), [None] * n_far, []
    for i in range(len(groups) - 1, -1, -1):
        group = groups[i]
        wide_weights = jnp.concatenate([about_all[k][1] for k in group])
        wide_totals = jnp.concatenate([log_total[k] for k in group])
        side = jnp.stack([wide_totals, wide_weights] + [jnp.zeros_like(wide_totals)] * 6)
        d_logits[i], product = head_back(
            table_t,
            *powers[group[0] // 2],
            group[0] % 2,
            jnp.concatenate([columns[k] for k in group], axis=1),
            side,
            on_y[-3:-2] if i == 0 else (),
        )
        for g in reversed(range(len(group))):
            k, one = group[g], product[g * half : (g + 1) * half]
            gathered = one[:fourth].astype(F32) + flip(one[fourth:], "hidden", 2).astype(F32)
            if k:
                on_y.append(gathered.astype(BF))
                gathered = flip(on_y[-1], "expert", 2 * k).astype(F32)
            d_parts[k] = gathered
    d_quarter = sum(d_parts)
    d_quarter = d_quarter.astype(BF)
    d_four = hidden_gather(d_quarter)
    quarter_h = jnp.array([0, 2, 1, 3], jnp.int32)

    d_gain_three, d_result, d_after_moe = norm_back(
        after_moe,
        gain_full[2:3],
        (piece_of(quarter_h ^ h_index), *d_four),
        pick="blocks",
    )
    d_across = table_grad(d_logits, group_rows, padded, (1, 3), (d_result,))
    across_x = (d_across[0] + flip(d_across[1], "hidden", 1).astype(F32)).astype(BF)
    grad_in = to_expert(d_result, across_x[0, 0].astype(F32))
    d_received, *d_pre = expert_back(grad_in, expert_w, slope, ())
    d_w = [
        jnp.stack([dot(received, d_pre[p], 0, 0), dot(active[p], grad_in, 0, 0)]) for p in range(4)
    ]
    d_same = table_grad(d_logits, group_rows, padded, (0, 2), (d_received,))

    base_x, both_x = far_flip(across_x, "expert", 1)
    d_base = d_same[0] + flip(d_same[1], "hidden", 1).astype(F32) + base_x.astype(F32)

    w_near = flip(d_w[3], "hidden", 1), flip(d_w[2], "hidden", 1)
    w_sent = (d_w[1] + w_near[0]).astype(BF)
    w_far, _ = far_flip(w_sent, "hidden", 2)
    d_gain_two, d_branch, d_after_attn = norm_back(
        after_attn,
        gain_full[1:2],
        (pick_place, *from_expert(d_received, d_same[0][0, 0])),
        d_after_moe,
        pick="rows",
        ready=(w_sent,),
    )

    d_qkv, d_norm_part = attend_back(d_branch, packed, qkv, segment, (both_x,))
    d_gain_one, d_high, d_low = norm_back(
        embedded,
        gain_full[0:1],
        [d_norm_part, flip(d_norm_part, "hidden", 1)],
        d_after_attn,
        scale=embed_scale,
        split=True,
    )

    attn_sent = attn_grad(normed_one, d_qkv, d_branch, attended, (d_high,))

    row_hot = hot_rows(place_own, n_expert * slots)
    d_rows = dot(row_hot, d_high) + dot(row_hot, d_low)
    d_gains = jnp.concatenate([d_gain_one, d_gain_two, d_gain_three])
    d_gains = d_gains.reshape(3, n_expert, own_rows).transpose(1, 0, 2).reshape(n_expert, 1, -1)
    gains_high = lax.reduce_precision(d_gains, 8, 7)
    gains_two = jnp.concatenate([gains_high, d_gains - gains_high], axis=1).astype(BF)
    gains_two = jnp.pad(gains_two, ((0, 0), (0, 14), (0, model_width - gains_two.shape[2])))
    attn_got = lax.all_to_all(
        attn_sent.reshape(n_expert, own_rows, 4 * head_width),
        "expert",
        split_axis=0,
        concat_axis=0,
        tiled=True,
    )
    sent = jnp.concatenate(
        [d_rows.astype(BF).reshape(n_expert, slots, model_width), gains_two], axis=1
    )
    got = lax.all_to_all(sent, "expert", split_axis=0, concat_axis=0, tiled=True)
    got_rows = got[:, :slots].reshape(n_expert * slots, model_width)

    def scatter_step(k, carry):
        d_far, ids_far, total = carry
        here = ids_far // vocab_rows == own_shard
        local = jnp.where(here, ids_far % vocab_rows, 0)
        d_sum = d_far[0].astype(F32) + d_far[1].astype(F32)
        total = total.at[local].add(jnp.where(here[:, None], d_sum, 0.0))
        ring = [(j, (j + 1) % n_expert) for j in range(n_expert)]
        return lax.ppermute(d_far, "expert", ring), lax.ppermute(ids_far, "expert", ring), total

    d_base = lax.fori_loop(
        0,
        jnp.where(any_overflow, n_expert, 0),
        scatter_step,
        ((d_high, d_low), ids, d_base),
    )[2]
    g_table, table_squares = finish(d_base, asked_rows, got_rows, vocab_rows)
    g_attn = jnp.sum(attn_got.astype(F32), axis=0)
    g_attn_in = g_attn[:, : 3 * head_width].reshape(own_rows, 3, head_width)
    g_attn_out = g_attn[:, 3 * head_width :]
    g_gains = jnp.sum(got[:, slots : slots + 2, : 3 * own_rows].astype(F32), axis=(0, 1))
    g_gains = g_gains.reshape(3, own_rows).T
    g_expert = d_w[0] + w_near[1] + w_far.astype(F32)
    g_expert_in = g_expert[0][None]
    g_expert_out = g_expert[1][None]

    squares = (
        jnp.sum(table_squares)
        + jnp.sum(g_attn * g_attn)
        + jnp.sum(g_expert * g_expert)
        + jnp.sum(g_gains * g_gains) / n_hidden
    )
    both_sums = jnp.stack([squares, loss_part * (2.0 / n_hidden)])
    both_sums = jnp.broadcast_to(jnp.pad(both_sums, (0, 126))[None], (n_expert, 128))
    both_sums = lax.all_to_all(both_sums, "expert", split_axis=0, concat_axis=0, tiled=True)
    both_sums = lax.all_gather(jnp.sum(both_sums, axis=0), "hidden", axis=0)
    both_sums = jnp.sum(both_sums, axis=0)
    clip_norm = jnp.sqrt(both_sums[0])
    loss_value = both_sums[1]
    clip_scale = jnp.minimum(1.0, CLIP_AT / clip_norm)
    table_up = adam_step(
        embed_table, embed_first, embed_second, g_table * clip_scale, RATE_MATRIX, DECAY
    )
    attn_in_up = adam_step(
        attn_in, attn_in_first, attn_in_second, g_attn_in * clip_scale, RATE_MATRIX, DECAY
    )
    attn_out_up = adam_step(
        attn_out, attn_out_first, attn_out_second, g_attn_out * clip_scale, RATE_MATRIX, DECAY
    )
    expert_in_up = adam_step(
        expert_in,
        expert_in_first,
        expert_in_second,
        g_expert_in * clip_scale,
        RATE_MATRIX,
        DECAY,
    )
    expert_out_up = adam_step(
        expert_out,
        expert_out_first,
        expert_out_second,
        g_expert_out * clip_scale,
        RATE_MATRIX,
        DECAY,
    )
    gains_up = adam_step(
        norm_gains, gains_first, gains_second, g_gains * clip_scale, RATE_GAIN, 0.0
    )
    return (
        loss_value,
        clip_norm,
        *table_up,
        *attn_in_up,
        *attn_out_up,
        *expert_in_up,
        *expert_out_up,
        *gains_up,
    )


def solution(mesh):
    rows = P("expert", None)
    table = P(("expert", "hidden"), None)
    wide = P("expert", None, "hidden")
    flat = P("expert", "hidden")
    tall = P("expert", "hidden", None)
    groups = (table, wide, flat, wide, tall, rows)
    each = tuple(spec for spec in groups for _ in range(3))
    return jax.shard_map(
        on_device,
        mesh=mesh,
        in_specs=(rows, rows, rows, P(), *each),
        out_specs=(P(), P(), *each),
        check_vma=False,
    )
```

```python
from functools import partial

import jax
import jax.numpy as jnp
from jax import lax
from jax.experimental import pallas as pl
from jax.experimental.pallas import tpu as pltpu
from jax.sharding import PartitionSpec as P

HD = 64
DOCS_ROW = 8
STEP = 7


EPS_NORM = 1e-06
BETA_ONE = 0.9
BETA_TWO = 0.95
ADAM_EPS = 1e-08
RATE_MATRIX = 0.05
RATE_GAIN = 0.3
DECAY = 0.1
CLIP_AT = 0.005
NEVER = -1e30
BF = jnp.bfloat16
F32 = jnp.float32
VMEM = 56 * 1024 * 1024
SHORT = pl.CostEstimate(flops=1024, bytes_accessed=1024, transcendentals=0)


def flip(x, axis, k):
    return lax.ppermute(x, axis, [(j, j ^ k) for j in range(lax.axis_size(axis))])


def behind(x, after):
    return jnp.where(after == after, x, 0)


def far_flip(x, axis, k, after=None):
    pairs = [[j, j ^ k] for j in range(lax.axis_size(axis)) if not j & k]
    both = lax.all_gather(x, axis, axis_index_groups=pairs)
    upper = (lax.axis_index(axis) // k) % 2
    if after is not None:
        upper = behind(upper, after)
    return lax.dynamic_index_in_dim(both, 1 - upper, 0, keepdims=False), both


def hidden_gather(x, after=None):
    far = flip(x, "hidden", 2)
    if after is not None:
        far = behind(far, after)
    return [x, far, flip(x, "hidden", 1), flip(far, "hidden", 1)]


def piece_of(bits):
    return (bits >> 1) + 2 * (bits & 1)


def round_up(n, m):
    return -(-n // m) * m


def dot(a, b, ca=1, cb=0):
    return lax.dot_general(a, b, (((ca,), (cb,)), ((), ())), preferred_element_type=F32)


def hot_rows(place, count):
    return (jnp.arange(count, dtype=jnp.int32)[:, None] == place[None, :]).astype(BF)


def hot_columns(place, count):
    return (place[:, None] == jnp.arange(count, dtype=jnp.int32)[None, :]).astype(BF)


QB = 256
SPAN = 2


ANY = pl.BlockSpec(memory_space=pl.ANY)
WHOLE = pl.BlockSpec(memory_space=pltpu.VMEM)


def bias_of(first, second, axis, at_first, at_second):
    shape = (first.shape[0], second.shape[1])
    pos_a = lax.broadcasted_iota(jnp.int32, shape, 0) + at_first
    pos_b = lax.broadcasted_iota(jnp.int32, shape, 1) + at_second
    seen = (pos_a >= pos_b) if axis == 0 else (pos_b >= pos_a)
    return jnp.where(seen & (first == second), 0.0, NEVER)


def pack_kernel(in_ref, out_ref, *rest):
    o_ref = rest[-1]
    width = out_ref.shape[1]
    for c in range(3):
        o_ref[:, c * width : (c + 1) * width] = in_ref[c].astype(BF)
    o_ref[:, 3 * width :] = out_ref[...].astype(BF)


def pack(attn_in, attn_out, ready):
    rows, width = attn_out.shape
    return pl.pallas_call(
        pack_kernel,
        in_specs=[WHOLE] * 2 + [ANY] * len(ready),
        out_specs=WHOLE,
        out_shape=jax.ShapeDtypeStruct((rows, 4 * width), BF),
        name="pack",
    )(attn_in.transpose(1, 0, 2), attn_out, *ready)


def attend_kernel(rows_ref, w_ref, segr_ref, segc_ref, *rest):
    qkv_ref, o_ref, part_ref = rest[-3:]
    pieces, seq, width = o_ref.shape
    wide = 3 * width
    factor = jnp.asarray(HD**-0.5, BF)
    heads = [(p, c) for p in range(pieces) for c in range(0, width, HD)]
    for p in range(pieces):
        qkv_ref[p] = dot(rows_ref[...], w_ref[p, :, : 3 * width]).astype(BF)
    for b in range(seq // QB):
        lo, at, hi = max(0, b - SPAN) * QB, b * QB, (b + 1) * QB
        bias = bias_of(segc_ref[at:hi, :], segr_ref[:, lo:hi], 0, at, lo)
        scores = []
        for p, c in heads:
            q = qkv_ref[p, at:hi, c : c + HD] * factor
            scores.append(dot(q, qkv_ref[p, lo:hi, width + c : width + c + HD], 1, 1))
        probs = []
        for s in scores:
            s = s + bias
            e = jnp.exp(s - jnp.max(s, axis=1, keepdims=True))
            probs.append((e * (1.0 / jnp.sum(e, axis=1, keepdims=True))).astype(BF))
        outs = [
            dot(prob, qkv_ref[p, lo:hi, 2 * width + c : 2 * width + c + HD])
            for prob, (p, c) in zip(probs, heads, strict=True)
        ]
        for out, (p, c) in zip(outs, heads, strict=True):
            o_ref[p, at:hi, c : c + HD] = out.astype(BF)
    total = dot(o_ref[0], w_ref[0, :, wide : wide + width], 1, 1)
    for p in range(1, pieces):
        total += dot(o_ref[p], w_ref[p, :, wide : wide + width], 1, 1)
    part_ref[...] = total


def attend(rows, packed, width, seg, ready):
    seq, model = rows.shape
    pieces = packed.shape[0]
    return pl.pallas_call(
        attend_kernel,
        in_specs=[WHOLE] * 4 + [ANY] * len(ready),
        out_specs=[WHOLE] * 3,
        out_shape=[
            jax.ShapeDtypeStruct((pieces, seq, 3 * width), BF),
            jax.ShapeDtypeStruct((pieces, seq, width), BF),
            jax.ShapeDtypeStruct((seq, model), F32),
        ],
        compiler_params=pltpu.CompilerParams(vmem_limit_bytes=VMEM),
        cost_estimate=SHORT,
        name="attend",
    )(rows, packed, seg[None, :], seg[:, None], *ready)


def attend_back_kernel(branch_ref, w_ref, qkv_ref, segr_ref, segc_ref, *rest):
    d_ref, part_ref, g_ref, dk_acc, dv_acc = rest[-5:]
    pieces, seq, width = g_ref.shape
    wide = 3 * width
    scale = HD**-0.5
    factor = jnp.asarray(scale, BF)
    heads = [(p, c) for p in range(pieces) for c in range(0, width, HD)]
    for p in range(pieces):
        g_ref[p] = dot(branch_ref[...], w_ref[p, :, wide : wide + width]).astype(BF)
    dk_acc[...] = jnp.zeros_like(dk_acc)
    dv_acc[...] = jnp.zeros_like(dv_acc)
    for b in range(seq // QB):
        lo, at, hi = max(0, b - SPAN) * QB, b * QB, (b + 1) * QB
        bias = bias_of(segc_ref[lo:hi, :], segr_ref[:, at:hi], 1, lo, at)
        for group in (heads[: len(heads) // 2], heads[len(heads) // 2 :]):
            qs = [qkv_ref[p, at:hi, c : c + HD] * factor for p, c in group]
            ks = [qkv_ref[p, lo:hi, width + c : width + c + HD] for p, c in group]
            gs = [g_ref[p, at:hi, c : c + HD] for p, c in group]
            scores = [dot(k, q, 1, 1) for k, q in zip(ks, qs, strict=True)]
            d_probs = [
                dot(qkv_ref[p, lo:hi, 2 * width + c : 2 * width + c + HD], g, 1, 1)
                for (p, c), g in zip(group, gs, strict=True)
            ]
            probs, d_scores = [], []
            for s, d_prob in zip(scores, d_probs, strict=True):
                s = s + bias
                e = jnp.exp(s - jnp.max(s, axis=0, keepdims=True))
                prob = e * (1.0 / jnp.sum(e, axis=0, keepdims=True))
                centre = jnp.sum(prob * d_prob, axis=0, keepdims=True)
                d_scores.append((prob * (d_prob - centre)).astype(BF))
                probs.append(prob.astype(BF))
            dqs = [dot(d, k, 0, 0) for d, k in zip(d_scores, ks, strict=True)]
            dks = [dot(d, q) for d, q in zip(d_scores, qs, strict=True)]
            dvs = [dot(prob, g) for prob, g in zip(probs, gs, strict=True)]
            for i, (p, c) in enumerate(group):
                d_ref[p, at:hi, c : c + HD] = (dqs[i] * scale).astype(BF)
                dk_acc[p, lo:hi, c : c + HD] += dks[i]
                dv_acc[p, lo:hi, c : c + HD] += dvs[i]
    d_ref[:, :, width : 2 * width] = dk_acc[...].astype(BF)
    d_ref[:, :, 2 * width :] = dv_acc[...].astype(BF)
    total = dot(d_ref[0], w_ref[0, :, : 3 * width], 1, 1)
    for p in range(1, pieces):
        total += dot(d_ref[p], w_ref[p, :, : 3 * width], 1, 1)
    part_ref[...] = total


def attend_back(branch, packed, qkv, seg, ready):
    seq, model = branch.shape
    pieces, _, width = qkv.shape
    return pl.pallas_call(
        attend_back_kernel,
        in_specs=[WHOLE] * 5 + [ANY] * len(ready),
        out_specs=[WHOLE] * 2,
        out_shape=[
            jax.ShapeDtypeStruct((pieces, seq, width), BF),
            jax.ShapeDtypeStruct((seq, model), F32),
        ],
        scratch_shapes=[
            pltpu.VMEM((pieces, seq, width // 3), BF),
            pltpu.VMEM((pieces, seq, width // 3), F32),
            pltpu.VMEM((pieces, seq, width // 3), F32),
        ],
        compiler_params=pltpu.CompilerParams(vmem_limit_bytes=VMEM),
        cost_estimate=SHORT,
        name="attend_back",
    )(branch, packed, qkv, seg[None, :], seg[:, None], *ready)


def attn_grad_kernel(rows_ref, d_ref, branch_ref, o_ref, *rest):
    out_ref = rest[-1]
    width = d_ref.shape[2]
    out_ref[:, :width] = dot(rows_ref[...], d_ref[0], 0, 0).astype(BF)
    out_ref[:, width:] = dot(branch_ref[...], o_ref[0], 0, 0).astype(BF)


def attn_grad(rows, d_qkv, branch, attended, ready):
    model = rows.shape[1]
    seq, third = attended.shape[1:]
    one = pl.BlockSpec((1, seq, 3 * third), lambda i: (0, 0, 0))
    two = pl.BlockSpec((1, seq, third), lambda i: (0, 0, 0))
    full = pl.BlockSpec((seq, model), lambda i: (0, 0))
    return pl.pallas_call(
        attn_grad_kernel,
        grid=(1,),
        in_specs=[full, one, full, two] + [ANY] * len(ready),
        out_specs=pl.BlockSpec((model, 4 * third), lambda i: (0, 0)),
        out_shape=jax.ShapeDtypeStruct((model, 4 * third), BF),
        compiler_params=pltpu.CompilerParams(vmem_limit_bytes=VMEM),
        cost_estimate=SHORT,
        name="attn_grad",
    )(rows, d_qkv, branch, attended, *ready)


def picked(place_ref, *row_refs):
    count = row_refs[0].shape[0]
    at = lax.broadcasted_iota(jnp.int32, (place_ref.shape[0], count), 1)
    total = None
    for q, ref in enumerate(row_refs):
        part = dot((at == place_ref[...] - q * count).astype(BF), ref[...])
        total = part if total is None else total + part
    return total


def pick_norm_kernel(scale, pick, parts, base, *refs):
    first_refs, refs = refs[:parts], refs[parts:]
    if base:
        base_ref, refs = refs[0], refs[1:]
    gain_ref, sum_ref, norm_ref = refs[0], refs[-2], refs[-1]
    if pick:
        x = picked(*first_refs)
    else:
        x = first_refs[0][...]
        for ref in first_refs[1:]:
            x = x + ref[...]
    if base:
        x = base_ref[...] + x
    if scale != 1.0:
        x = x * scale
    sum_ref[...] = x
    root = lax.rsqrt(jnp.mean(x * x, axis=1, keepdims=True) + EPS_NORM)
    norm_ref[...] = (x * root * gain_ref[...]).astype(BF)


def pick_norm(first, base, gain, scale=1.0, pick=True, ready=()):
    tokens = first[0].shape[0]
    width = gain.shape[1]
    block = min(tokens, 256)
    by_rows = pl.BlockSpec((block, width), lambda i: (i, 0))
    if pick:
        first = (first[0][:, None], *first[1:])
        specs = [pl.BlockSpec((block, 1), lambda i: (i, 0))]
        specs += [pl.BlockSpec(r.shape, lambda i: (0, 0)) for r in first[1:]]
    else:
        specs = [by_rows] * len(first)
    has_base = base is not None
    return pl.pallas_call(
        partial(pick_norm_kernel, scale, pick, len(first), has_base),
        grid=(tokens // block,),
        in_specs=specs
        + [by_rows] * has_base
        + [pl.BlockSpec((1, width), lambda i: (0, 0))]
        + [ANY] * len(ready),
        out_specs=[by_rows, by_rows],
        out_shape=[
            jax.ShapeDtypeStruct((tokens, width), F32),
            jax.ShapeDtypeStruct((tokens, width), BF),
        ],
        compiler_params=pltpu.CompilerParams(vmem_limit_bytes=VMEM),
        cost_estimate=SHORT,
        name="pick_norm",
    )(*first, *((base,) if has_base else ()), gain, *ready)


def norm_back_kernel(scale, parts, pick, rest, split, x_ref, gain_ref, *refs):
    g_refs, refs = refs[:parts], refs[parts:]
    if rest:
        rest_ref, refs = refs[0], refs[1:]
    gain_out, one_ref, two_ref = refs[-3:]
    x = x_ref[...]
    if pick == "rows":
        g = picked(*g_refs)
    elif pick == "blocks":
        which = g_refs[0][pl.program_id(0)]
        g = g_refs[1][...].astype(F32)
        for q, ref in enumerate(g_refs[2:], 1):
            g = jnp.where(which == q, ref[...].astype(F32), g)
    else:
        g = g_refs[0][...].astype(F32)
        for ref in g_refs[1:]:
            g = g + ref[...].astype(F32)
    root = lax.rsqrt(jnp.mean(x * x, axis=1, keepdims=True) + EPS_NORM)
    scaled = x * root
    d_gain = jnp.sum(g * scaled, axis=0, keepdims=True)
    g = g * gain_ref[...]
    dx = root * (g - scaled * jnp.mean(g * scaled, axis=1, keepdims=True))
    if rest:
        dx = rest_ref[...] + dx
    if scale != 1.0:
        dx = dx * scale
    high = dx.astype(BF)
    one_ref[...] = high
    two_ref[...] = (dx - high.astype(F32)).astype(BF) if split else dx

    @pl.when(pl.program_id(0) == 0)
    def _():
        gain_out[...] = d_gain

    @pl.when(pl.program_id(0) > 0)
    def _():
        gain_out[...] += d_gain


def norm_back(x, gain, gradients, rest=None, scale=1.0, split=False, pick="", ready=()):
    tokens, width = x.shape
    block = min(tokens, 256)
    by_rows = pl.BlockSpec((block, width), lambda i: (i, 0))
    one_row = pl.BlockSpec((1, width), lambda i: (0, 0))
    has_rest = rest is not None
    whole = [pl.BlockSpec(g.shape, lambda i: (0, 0)) for g in gradients[1:]]
    if pick == "rows":
        gradients = (gradients[0][:, None], *gradients[1:])
        specs = [pl.BlockSpec((block, 1), lambda i: (i, 0)), *whole]
    elif pick == "blocks":
        specs = [pl.BlockSpec(memory_space=pltpu.SMEM), *whole]
    else:
        specs = [by_rows] * len(gradients)
    return pl.pallas_call(
        partial(norm_back_kernel, scale, len(gradients), pick, has_rest, split),
        grid=(tokens // block,),
        in_specs=[by_rows, one_row] + specs + [by_rows] * has_rest + [ANY] * len(ready),
        out_specs=[one_row, by_rows, by_rows],
        out_shape=[
            jax.ShapeDtypeStruct((1, width), F32),
            jax.ShapeDtypeStruct((tokens, width), BF),
            jax.ShapeDtypeStruct((tokens, width), BF if split else F32),
        ],
        compiler_params=pltpu.CompilerParams(vmem_limit_bytes=VMEM),
        cost_estimate=SHORT,
        name="norm_back",
    )(x, gain, *gradients, *((rest,) if has_rest else ()), *ready)


ERFC = (
    -1.26551223,
    1.00002368,
    0.37409196,
    0.09678418,
    -0.18628806,
    0.27886807,
    -1.13520398,
    1.48851587,
    -0.82215223,
    0.17087277,
)


def gelu_and_slope(x):
    t = 1.0 / (1.0 + 0.35355339059327373 * jnp.abs(x))
    poly = jnp.full_like(t, ERFC[-1])
    for c in ERFC[-2::-1]:
        poly = poly * t + c
    square = 0.5 * x * x
    half = 0.5 * t * jnp.exp(poly - square)
    below = jnp.where(x >= 0.0, 1.0 - half, half)
    return x * below, below + x * jnp.exp(-square) * 0.3989422804014327


def expert_kernel(rows_ref, *refs):
    w_refs, out_ref, active_refs, slope_refs = refs[:4], refs[4], refs[5:9], refs[9:]
    rows = rows_ref[...]
    total = None
    for w_ref, active_ref, slope_ref in zip(w_refs, active_refs, slope_refs, strict=True):
        value, slope_ref[...] = gelu_and_slope(dot(rows, w_ref[0]))
        active = value.astype(BF)
        active_ref[...] = active
        product = dot(active, w_ref[1])
        total = product if total is None else total + product
    out_ref[...] = total.astype(BF)


def expert(rows, weights):
    hidden = jax.ShapeDtypeStruct((rows.shape[0], weights[0].shape[2]), BF)
    slope = jax.ShapeDtypeStruct(hidden.shape, F32)
    out, *rest = pl.pallas_call(
        expert_kernel,
        in_specs=[WHOLE] * 5,
        out_specs=[WHOLE] * 9,
        out_shape=[jax.ShapeDtypeStruct(rows.shape, BF)] + [hidden] * 4 + [slope] * 4,
        compiler_params=pltpu.CompilerParams(vmem_limit_bytes=VMEM),
        cost_estimate=SHORT,
        name="expert",
    )(rows, *weights)
    return out, rest[:4], rest[4:]


def expert_back_kernel(grad_ref, *refs):
    w_refs, slope_refs, refs = refs[:4], refs[4:8], refs[8:]
    out_ref, d_refs = refs[-5], refs[-4:]
    grad = grad_ref[...]
    total = None
    for w_ref, slope_ref, d_ref in zip(w_refs, slope_refs, d_refs, strict=True):
        d_pre = (dot(grad, w_ref[1], 1, 1) * slope_ref[...]).astype(BF)
        d_ref[...] = d_pre
        product = dot(d_pre, w_ref[0], 1, 1)
        total = product if total is None else total + product
    out_ref[...] = total.astype(BF)


def expert_back(grad, weights, slopes, ready):
    return pl.pallas_call(
        expert_back_kernel,
        in_specs=[WHOLE] * 9 + [ANY] * len(ready),
        out_specs=[WHOLE] * 5,
        out_shape=[jax.ShapeDtypeStruct(grad.shape, BF)]
        + [jax.ShapeDtypeStruct(slope.shape, BF) for slope in slopes],
        compiler_params=pltpu.CompilerParams(vmem_limit_bytes=VMEM),
        cost_estimate=SHORT,
        name="expert_back",
    )(grad, *weights, *slopes, *ready)


def part_rows(padded):
    return max(r for r in range(32, 385, 32) if padded % r == 0)


def cast_pick_kernel(real, place_ref, x_ref, table_ref, o_ref, acc):
    j = pl.program_id(0)
    rows = x_ref.shape[0]
    at = lax.broadcasted_iota(jnp.int32, x_ref.shape, 0) + j * rows
    table_ref[...] = jnp.where(at < real, x_ref[...], 0.0).astype(BF)
    column = lax.broadcasted_iota(jnp.int32, (place_ref.shape[0], rows), 1) + j * rows
    found = dot((column == place_ref[...]).astype(BF), table_ref[...])

    @pl.when(j == 0)
    def _():
        acc[...] = found

    @pl.when(j > 0)
    def _():
        acc[...] += found

    @pl.when(j == pl.num_programs(0) - 1)
    def _():
        o_ref[...] = acc[...].astype(BF)


def cast_pick(place, x, padded):
    real, width = x.shape
    rows = part_rows(padded)
    count = place.shape[0]
    return pl.pallas_call(
        partial(cast_pick_kernel, real),
        grid=(padded // rows,),
        in_specs=[
            pl.BlockSpec((count, 1), lambda j: (0, 0)),
            pl.BlockSpec((rows, width), lambda j: (j, 0)),
        ],
        out_specs=[
            pl.BlockSpec((rows, width), lambda j: (j, 0)),
            pl.BlockSpec((count, width), lambda j: (0, 0)),
        ],
        out_shape=[
            jax.ShapeDtypeStruct((padded, width), BF),
            jax.ShapeDtypeStruct((count, width), BF),
        ],
        scratch_shapes=[pltpu.VMEM((count, width), F32)],
        compiler_params=pltpu.CompilerParams(vmem_limit_bytes=VMEM),
        cost_estimate=SHORT,
        name="cast_pick",
    )(place[:, None], x)


def turn_kernel(a_ref, b_ref, c_ref, d_ref, o_ref):
    o_ref[...] = jnp.concatenate([a_ref[...], b_ref[...], c_ref[...], d_ref[...]], axis=0).T


def turned(slices):
    padded, width = slices[0].shape
    rows = part_rows(padded)
    return pl.pallas_call(
        turn_kernel,
        grid=(padded // rows,),
        in_specs=[pl.BlockSpec((rows, width), lambda j: (j, 0))] * 4,
        out_specs=pl.BlockSpec((width, 4 * rows), lambda j: (0, j)),
        out_shape=jax.ShapeDtypeStruct((width, 4 * padded), BF),
        compiler_params=pltpu.CompilerParams(vmem_limit_bytes=VMEM),
        cost_estimate=pl.CostEstimate(flops=0, bytes_accessed=24 * padded * width, transcendentals=0),
        name="turned",
    )(*slices)


def logits_kernel(
    real, a_ref, b_ref, c_ref, d_ref, rows_ref, col_ref, *rest
):
    out_ref, peak_ref, stat_ref, peak_s, sum_s, hit_s = rest[-6:]
    j = pl.program_id(0)
    tokens = rows_ref.shape[0]
    part = a_ref.shape[0]

    @pl.when(j == 0)
    def _():
        peak_s[...] = jnp.full((8, tokens), NEVER, F32)
        sum_s[...] = jnp.zeros((8, tokens), F32)
        hit_s[...] = jnp.zeros((8, tokens), F32)

    away = col_ref[...] - j * (4 * part) - lax.broadcasted_iota(jnp.int32, (8, tokens), 0)
    peak, total, hit = peak_s[...], sum_s[...], hit_s[...]
    rows = rows_ref[...]
    tail = round_up(part * (-(-real // part)) - real, 8)
    for q, ref in enumerate((a_ref, b_ref, c_ref, d_ref)):
        logits = dot(ref[...], rows, 1, 1)
        if tail:
            at = lax.broadcasted_iota(jnp.int32, (tail, tokens), 0) + (j + 1) * part - tail
            end = jnp.where(at < real, logits[part - tail :], NEVER)
            logits = jnp.concatenate([logits[: part - tail], end], axis=0)
        tiles = logits.reshape(part // 8, 8, tokens)
        new = jnp.maximum(peak, jnp.max(tiles, axis=0))
        powers = jnp.exp(tiles - new[None])
        out_ref[q * part : (q + 1) * part, :] = powers.reshape(part, tokens)
        peak_ref[q * 8 : (q + 1) * 8, :] = new
        total = total * jnp.exp(peak - new) + jnp.sum(powers, axis=0)
        for i in range(part // 8):
            hit = hit + jnp.where(away == q * part + 8 * i, tiles[i], 0.0)
        peak = new
    peak_s[...], sum_s[...], hit_s[...] = peak, total, hit

    @pl.when(j == pl.num_programs(0) - 1)
    def _():
        top = jnp.max(peak, axis=0, keepdims=True)
        stat_ref[0:1, :] = top
        stat_ref[1:2, :] = jnp.sum(total * jnp.exp(peak - top), axis=0, keepdims=True)
        stat_ref[2:3, :] = jnp.sum(hit, axis=0, keepdims=True)
        stat_ref[3:8, :] = jnp.zeros((5, tokens), F32)


def head_logits(slices, rows, col, real, ready=()):
    padded, width = slices[0].shape
    tokens = rows.shape[0]
    part = part_rows(padded)
    steps = padded // part
    return pl.pallas_call(
        partial(logits_kernel, real),
        grid=(steps,),
        in_specs=[pl.BlockSpec((part, width), lambda j: (j, 0))] * 4
        + [
            pl.BlockSpec((tokens, width), lambda j: (0, 0)),
            pl.BlockSpec((1, tokens), lambda j: (0, 0)),
        ]
        + [ANY] * len(ready),
        out_specs=[
            pl.BlockSpec((4 * part, tokens), lambda j: (j, 0)),
            pl.BlockSpec((32, tokens), lambda j: (j, 0)),
            pl.BlockSpec((8, tokens), lambda j: (0, 0)),
        ],
        out_shape=[
            jax.ShapeDtypeStruct((4 * padded, tokens), F32),
            jax.ShapeDtypeStruct((32 * steps, tokens), F32),
            jax.ShapeDtypeStruct((8, tokens), F32),
        ],
        scratch_shapes=[pltpu.VMEM((8, tokens), F32)] * 3,
        compiler_params=pltpu.CompilerParams(vmem_limit_bytes=VMEM),
        cost_estimate=pl.CostEstimate(flops=16 * padded * tokens * width, bytes_accessed=16 * padded * tokens, transcendentals=0),
        name="head_logits",
    )(*slices, rows, col, *ready)


def head_back_kernel(table_ref, power_ref, peak_ref, col_ref, side_ref, *rest):
    d_ref, out_ref, acc = rest[-3:]
    j = pl.program_id(0)
    block, tokens = power_ref.shape
    part = block // 4
    away = col_ref[...] - j * block - lax.broadcasted_iota(jnp.int32, (8, tokens), 0)
    log_total, weight = side_ref[0:1, :], side_ref[1:2, :]
    pieces = []
    for q in range(4):
        factor = jnp.exp(peak_ref[q * 8 : (q + 1) * 8, :] - log_total) * weight
        for i in range(part // 8):
            at = q * part + 8 * i
            less = jnp.where(away == at, weight, 0.0)
            pieces.append(power_ref[at : at + 8, :] * factor - less)
    d = jnp.concatenate(pieces, axis=0).astype(BF)
    d_ref[...] = d
    product = dot(table_ref[...], d)

    @pl.when(j == 0)
    def _():
        acc[...] = product

    @pl.when(j > 0)
    def _():
        acc[...] += product

    @pl.when(j == pl.num_programs(0) - 1)
    def _():
        out_ref[...] = acc[...].T.astype(out_ref.dtype)


def head_back(table_t, powers, peaks, at, col, side, ready=()):
    width, vocab = table_t.shape
    tokens = col.shape[1]
    steps = peaks.shape[0] // 32
    block = vocab // steps
    return pl.pallas_call(
        head_back_kernel,
        grid=(steps,),
        in_specs=[
            pl.BlockSpec((width, block), lambda j: (0, j)),
            pl.BlockSpec((block, tokens), lambda j: (j, at)),
            pl.BlockSpec((32, tokens), lambda j: (j, at)),
            pl.BlockSpec((1, tokens), lambda j: (0, 0)),
            pl.BlockSpec((8, tokens), lambda j: (0, 0)),
        ]
        + [ANY] * len(ready),
        out_specs=[
            pl.BlockSpec((block, tokens), lambda j: (j, 0)),
            pl.BlockSpec((tokens, width), lambda j: (0, 0)),
        ],
        out_shape=[
            jax.ShapeDtypeStruct((vocab, tokens), BF),
            jax.ShapeDtypeStruct((tokens, width), BF),
        ],
        scratch_shapes=[pltpu.VMEM((width, tokens), F32)],
        compiler_params=pltpu.CompilerParams(vmem_limit_bytes=VMEM),
        cost_estimate=pl.CostEstimate(flops=4 * vocab * tokens * width, bytes_accessed=6 * vocab * tokens, transcendentals=0),
        name="head_back",
    )(table_t, powers, peaks, col, side, *ready)


def table_grad_kernel(count, *refs):
    d_refs, row_refs, out_refs = refs[: 2 * count], refs[2 * count : 3 * count], refs[-2:]
    total = None
    for k in range(count):
        both = jnp.concatenate([d_refs[2 * k][...], d_refs[2 * k + 1][...]], axis=0)
        product = dot(both, row_refs[k][...])
        total = product if total is None else total + product
    part = out_refs[0].shape[0]
    for q in range(2):
        out_refs[q][...] = total[q * part : (q + 1) * part].astype(out_refs[q].dtype)


def table_grad(ds, rows, padded, which, ready):
    width = rows[0].shape[1]
    part = part_rows(padded)

    def spec(tokens, q):
        return pl.BlockSpec((part, tokens), lambda j: (4 * j + q, 0))

    return pl.pallas_call(
        partial(table_grad_kernel, len(ds)),
        grid=(padded // part,),
        in_specs=[spec(d.shape[1], q) for d in ds for q in which]
        + [pl.BlockSpec(r.shape, lambda j: (0, 0)) for r in rows]
        + [ANY] * len(ready),
        out_specs=[pl.BlockSpec((part, width), lambda j: (j, 0))] * 2,
        out_shape=[jax.ShapeDtypeStruct((padded, width), t) for t in (F32, BF)],
        compiler_params=pltpu.CompilerParams(vmem_limit_bytes=VMEM),
        cost_estimate=pl.CostEstimate(
            flops=4 * padded * width * sum(d.shape[1] for d in ds),
            bytes_accessed=8 * padded * width,
            transcendentals=0,
        ),
        name="table_grad",
    )(*[d for d in ds for _ in which], *rows, *ready)


def finish_kernel(real, base_ref, place_ref, rows_ref, out_ref, square_ref):
    rows = base_ref.shape[0]
    first = pl.program_id(0) * rows
    at = lax.broadcasted_iota(jnp.int32, (rows, place_ref.shape[1]), 0) + first
    spread = dot((at == place_ref[...]).astype(BF), rows_ref[...])
    g = base_ref[...] + spread
    out_ref[...] = g
    inside = lax.broadcasted_iota(jnp.int32, g.shape, 0) + first < real
    g = jnp.where(inside, g, 0.0)
    squares = jnp.sum(g * g, axis=0, keepdims=True)

    @pl.when(pl.program_id(0) == 0)
    def _():
        square_ref[...] = squares

    @pl.when(pl.program_id(0) > 0)
    def _():
        square_ref[...] += squares


def finish(base, place, rows, real):
    padded, width = base.shape
    part = part_rows(padded)
    block = pl.BlockSpec((part, width), lambda j: (j, 0))
    return pl.pallas_call(
        partial(finish_kernel, real),
        grid=(padded // part,),
        in_specs=[
            block,
            pl.BlockSpec((1, place.shape[0]), lambda j: (0, 0)),
            pl.BlockSpec(rows.shape, lambda j: (0, 0)),
        ],
        out_specs=[block, pl.BlockSpec((1, width), lambda j: (0, 0))],
        out_shape=[
            jax.ShapeDtypeStruct((real, width), F32),
            jax.ShapeDtypeStruct((1, width), F32),
        ],
        compiler_params=pltpu.CompilerParams(vmem_limit_bytes=VMEM),
        cost_estimate=SHORT,
        name="finish",
    )(base, place[None, :], rows)


def adam_step(weight, first_moment, second_moment, gradient, step_rate, weight_decay):
    first_moment = BETA_ONE * first_moment + (1.0 - BETA_ONE) * gradient
    second_moment = BETA_TWO * second_moment + (1.0 - BETA_TWO) * gradient * gradient
    update = (
        first_moment
        / (1.0 - BETA_ONE**STEP)
        / (jnp.sqrt(second_moment / (1.0 - BETA_TWO**STEP)) + ADAM_EPS)
    )
    return (weight - step_rate * (update + weight_decay * weight), first_moment, second_moment)


def combine_stats(left, right):
    peak = jnp.maximum(left[0], right[0])
    total = left[1] * jnp.exp(left[0] - peak) + right[1] * jnp.exp(right[0] - peak)
    return jnp.stack([peak, total, left[2] + right[2]])


def on_device(
    token_ids,
    target_ids,
    doc_segments,
    hash_experts,
    embed_table,
    embed_first,
    embed_second,
    attn_in,
    attn_in_first,
    attn_in_second,
    attn_out,
    attn_out_first,
    attn_out_second,
    expert_in,
    expert_in_first,
    expert_in_second,
    expert_out,
    expert_out_first,
    expert_out_second,
    norm_gains,
    gains_first,
    gains_second,
):
    n_expert = lax.axis_size("expert")
    n_hidden = lax.axis_size("hidden")
    assert n_hidden == 4 and token_ids.shape[0] == 1
    e_index = lax.axis_index("expert")
    h_index = lax.axis_index("hidden")
    tok_count = token_ids.shape[1]
    vocab_rows, model_width = embed_table.shape
    embed_scale = model_width**0.5
    ids = token_ids[0]
    targets = target_ids[0]
    segment = doc_segments[0]
    token_at = jnp.arange(tok_count, dtype=jnp.int32)

    padded = round_up(vocab_rows, 32)
    own_rows = attn_in.shape[0]
    head_width = attn_in.shape[2]

    slots = round_up(5 * tok_count // (4 * n_expert * n_hidden), 8)
    shard = ids // vocab_rows
    shard_e, shard_h = shard // n_hidden, shard % n_hidden
    same_id = ids[:, None] == ids[None, :]
    first_at = jnp.min(jnp.where(same_id, token_at[None, :], tok_count), axis=1)
    is_first = first_at == token_at
    rank = jnp.sum(
        (
            (shard[:, None] == shard[None, :])
            & is_first[None, :]
            & (token_at[None, :] < first_at[:, None])
        ).astype(jnp.int32),
        axis=1,
    )
    overflow = jnp.max(rank) >= slots
    place_own = jnp.where(
        (shard_h == h_index) & (rank < slots), shard_e * slots + rank, -1
    )
    wanted = jnp.max(
        jnp.where(
            jnp.arange(n_expert * slots, dtype=jnp.int32)[:, None] == place_own[None, :],
            (ids % vocab_rows)[None, :],
            -1,
        ),
        axis=1,
    )
    own_gains = norm_gains.astype(BF).astype(F32).T.reshape(1, 3 * own_rows)
    own_gains = jnp.pad(own_gains, ((0, 0), (0, round_up(3 * own_rows, 128) - 3 * own_rows)))
    asked = jnp.concatenate(
        [
            wanted.reshape(n_expert, slots).astype(F32),
            jnp.broadcast_to(overflow.astype(F32), (n_expert, 128 - slots)),
            jnp.broadcast_to(own_gains, (n_expert, own_gains.shape[1])),
        ],
        axis=1,
    )

    asked = lax.all_to_all(asked, "expert", split_axis=0, concat_axis=0, tiled=True)
    any_overflow = jnp.max(asked[:, slots:128]) > 0
    asked_rows = asked[:, :slots].astype(jnp.int32).reshape(n_expert * slots)
    gain_full = asked[:, 128 : 128 + 3 * own_rows].reshape(n_expert, 3, own_rows)
    gain_full = gain_full.transpose(1, 0, 2).reshape(3, model_width)

    capacity = 3 * tok_count // (2 * n_expert)
    quarter = capacity // n_hidden
    expert_ids = hash_experts[ids]
    onehot = (expert_ids[:, None] == jnp.arange(n_expert, dtype=jnp.int32)).astype(jnp.int32)
    before = jnp.cumsum(onehot, axis=0) - onehot
    slot_rank = jnp.sum(before * onehot, axis=1)
    kept = slot_rank < capacity
    slot_h = slot_rank // quarter
    slot_in = expert_ids * quarter + slot_rank % quarter
    rows_dev = n_expert * quarter
    fill_place = jnp.where(kept & (slot_h == h_index), slot_in, -1)
    pick_place = jnp.where(kept, piece_of(slot_h ^ h_index) * rows_dev + slot_in, -1)

    asked_rows = jnp.where(any_overflow, -1, asked_rows)
    table_own, answer = cast_pick(asked_rows, embed_table, padded)
    packed = pack(attn_in, attn_out, (asked_rows,))
    packed = jnp.stack([packed, flip(packed, "hidden", 2)])
    packed = lax.all_gather(packed, "expert", axis=1, tiled=True)
    weights_own = jnp.stack([expert_in[0], expert_out[0]]).astype(BF)

    n_all = n_expert * n_hidden
    own_shard = e_index * n_hidden + h_index
    everyone = [(j, (j + 1) % n_all) for j in range(n_all)]

    answer = lax.all_to_all(
        answer.reshape(n_expert, slots, model_width),
        "expert",
        split_axis=0,
        concat_axis=0,
        tiled=True,
    )
    answers = hidden_gather(answer.reshape(n_expert * slots, model_width))
    place_all = piece_of(shard_h ^ h_index) * (n_expert * slots) + shard_e * slots + rank

    def look_up_step(k, carry):
        table_far, found = carry
        here = (own_shard - k + n_all) % n_all
        place = jnp.where(shard == here, ids % vocab_rows, -1)
        row = dot(hot_columns(place, padded), table_far).astype(BF)
        row = jnp.pad(row, ((0, 4 * n_expert * slots - tok_count), (0, 0)))
        parts = row.reshape(4, n_expert * slots, model_width)
        found = [jnp.where(k == 0, 0, found[q]) + parts[q] for q in range(4)]
        return lax.ppermute(table_far, ("expert", "hidden"), everyone), found

    answers = lax.fori_loop(
        0, jnp.where(any_overflow, n_all, 0), look_up_step, (table_own, answers)
    )[1]
    place_all = jnp.where(any_overflow, token_at, place_all)
    embedded, normed_one = pick_norm(
        (place_all, *answers), None, gain_full[0:1], embed_scale, ready=(fill_place, pick_place)
    )

    qkv, attended, attn_part = attend(normed_one, packed, head_width, segment, ())
    after_attn, normed_two = pick_norm(
        (attn_part, flip(attn_part, "hidden", 1)),
        embedded,
        gain_full[1:2],
        pick=False,
    )

    fill_hot = hot_rows(fill_place, rows_dev)

    def to_expert(rows_in, after=None):
        block = dot(fill_hot, rows_in).astype(BF)
        if after is not None:
            block = behind(block, after)
        return lax.all_to_all(block, "expert", split_axis=0, concat_axis=0, tiled=True)

    def from_expert(rows_in, after=None):
        block = lax.all_to_all(rows_in, "expert", split_axis=0, concat_axis=0, tiled=True)
        return hidden_gather(block.reshape(rows_dev, model_width), after)

    received = to_expert(normed_two)
    weights_y, _ = far_flip(weights_own, "hidden", 2, received[0, 0])
    expert_w = [
        weights_own,
        weights_y,
        flip(weights_own, "hidden", 1),
        flip(weights_y, "hidden", 1),
    ]
    expert_result, active, slope = expert(received, expert_w)
    after_moe, final_rows = pick_norm(
        (pick_place, *from_expert(expert_result)),
        after_attn,
        gain_full[2:3],
    )

    slice_x, _ = far_flip(table_own, "expert", 1, final_rows[0, 0])
    slices = [table_own, slice_x, flip(table_own, "hidden", 1), flip(slice_x, "hidden", 1)]
    table_t = turned(slices)
    part = part_rows(padded)

    half, fourth = tok_count // 2, tok_count // 4
    own_at = (h_index & 1) * half + (h_index >> 1) * fourth
    other_at = (h_index & 1) * half + (1 - (h_index >> 1)) * fourth
    n_far = n_expert // 2

    def own_order(x):
        return jnp.concatenate(
            [
                lax.dynamic_slice_in_dim(x, own_at, fourth, x.ndim - 1),
                lax.dynamic_slice_in_dim(x, other_at, fourth, x.ndim - 1),
            ],
            axis=-1,
        )

    counts = jnp.sum((segment[:, None] == segment[None, :]).astype(F32), axis=1)
    weights = 1.0 / counts / (n_expert * DOCS_ROW)
    about = own_order(jnp.stack([targets.astype(F32), weights]))
    about_all = [about] + [flip(about, "expert", 2 * k) for k in range(1, n_far)]
    own_part = lax.dynamic_slice_in_dim(final_rows, own_at, fourth, 0)
    other_part = lax.dynamic_slice_in_dim(final_rows, other_at, fourth, 0)
    far_rows = [flip(own_part, "expert", 2 * k) for k in range(1, n_far)]

    columns = []
    for k in range(n_far):
        target = about_all[k][0].astype(jnp.int32)
        block_of = target // vocab_rows
        away_e = (block_of // n_hidden) ^ e_index
        away_h = (block_of % n_hidden) ^ h_index
        mine = (away_e < 2) & (away_h < 2)
        row_of = target % vocab_rows
        column = (row_of // part) * (4 * part) + (away_e + 2 * away_h) * part + row_of % part
        columns.append(jnp.where(mine, column, -1)[None, :])
    head_rows, onward = [jnp.concatenate([own_part, other_part])], []
    powers, stats = [], []
    for k, far in enumerate(far_rows, 1):
        onward.append(behind(far, table_t[0, 0].astype(F32)) if k > 1 else far)
        head_rows.append(jnp.concatenate([onward[-1], flip(onward[-1], "hidden", 2)]))
    for k in range(0, n_far, 2):
        one, two, stat = head_logits(
            slices,
            jnp.concatenate(head_rows[k : k + 2]),
            jnp.concatenate(columns[k : k + 2], axis=1),
            vocab_rows,
            () if k else (table_t, *onward[1:]),
        )
        powers.append((one, two))
        stats += [stat[:3, :half], stat[:3, half:]]
    stat = jnp.stack(stats, axis=1)
    across = flip(stat, "hidden", 2)
    stat = combine_stats(stat, jnp.concatenate([across[..., fourth:], across[..., :fourth]], axis=2))
    far_stats = [flip(stat, "expert", 2 * k) for k in range(1, n_far)]
    for k in range(1, n_far):
        far = jnp.stack([far_stats[k - 1][:, j ^ k] for j in range(n_far)], axis=1)
        stat = combine_stats(stat, far)
    log_total = stat[0] + jnp.log(stat[1])
    loss_part = jnp.sum((log_total[0] - stat[2, 0]) * about[1])

    groups = [[0], [1]] + [[k, k + 1] for k in range(2, n_far, 2)]
    group_rows = [jnp.concatenate([head_rows[k] for k in group]) for group in groups]
    d_logits, d_parts, on_y = [None] * len(groups), [None] * n_far, []
    for i in range(len(groups) - 1, -1, -1):
        group = groups[i]
        wide_weights = jnp.concatenate([about_all[k][1] for k in group])
        wide_totals = jnp.concatenate([log_total[k] for k in group])
        side = jnp.stack([wide_totals, wide_weights] + [jnp.zeros_like(wide_totals)] * 6)
        d_logits[i], product = head_back(
            table_t,
            *powers[group[0] // 2],
            group[0] % 2,
            jnp.concatenate([columns[k] for k in group], axis=1),
            side,
            on_y[-3:-2] if i == 0 else (),
        )
        for g in reversed(range(len(group))):
            k, one = group[g], product[g * half : (g + 1) * half]
            gathered = one[:fourth].astype(F32) + flip(one[fourth:], "hidden", 2).astype(F32)
            if k:
                on_y.append(gathered.astype(BF))
                gathered = flip(on_y[-1], "expert", 2 * k).astype(F32)
            d_parts[k] = gathered
    d_quarter = sum(d_parts)
    d_quarter = d_quarter.astype(BF)
    d_four = hidden_gather(d_quarter)
    quarter_h = jnp.array([0, 2, 1, 3], jnp.int32)

    d_gain_three, d_result, d_after_moe = norm_back(
        after_moe,
        gain_full[2:3],
        (piece_of(quarter_h ^ h_index), *d_four),
        pick="blocks",
    )
    d_across = table_grad(d_logits, group_rows, padded, (1, 3), (d_result,))
    across_x = (d_across[0] + flip(d_across[1], "hidden", 1).astype(F32)).astype(BF)
    grad_in = to_expert(d_result, across_x[0, 0].astype(F32))
    d_received, *d_pre = expert_back(grad_in, expert_w, slope, ())
    d_w = [
        (dot(received, d_pre[p], 0, 0), dot(active[p], grad_in, 0, 0)) for p in range(4)
    ]
    d_same = table_grad(d_logits, group_rows, padded, (0, 2), (d_received,))

    base_x, both_x = far_flip(across_x, "expert", 1)
    d_base = d_same[0] + flip(d_same[1], "hidden", 1).astype(F32) + base_x.astype(F32)

    w_near = flip(d_w[3], "hidden", 1), flip(jnp.stack(d_w[2]), "hidden", 1)
    w_sent = jnp.stack([d_w[1][i] + w_near[0][i] for i in range(2)]).astype(BF)
    d_gain_two, d_branch, d_after_attn = norm_back(
        after_attn,
        gain_full[1:2],
        (pick_place, *from_expert(d_received, d_same[0][0, 0])),
        d_after_moe,
        pick="rows",
        ready=(w_sent,),
    )

    d_qkv, d_norm_part = attend_back(d_branch, packed, qkv, segment, (both_x,))
    d_gain_one, d_high, d_low = norm_back(
        embedded,
        gain_full[0:1],
        [d_norm_part, flip(d_norm_part, "hidden", 1)],
        d_after_attn,
        scale=embed_scale,
        split=True,
    )

    attn_sent = attn_grad(normed_one, d_qkv, d_branch, attended, (d_high,))

    row_hot = hot_rows(place_own, n_expert * slots)
    d_rows = dot(row_hot, d_high) + dot(row_hot, d_low)
    d_gains = jnp.concatenate([d_gain_one, d_gain_two, d_gain_three])
    d_gains = d_gains.reshape(3, n_expert, own_rows).transpose(1, 0, 2).reshape(n_expert, 1, -1)
    gains_high = lax.reduce_precision(d_gains, 8, 7)
    gains_two = jnp.concatenate([gains_high, d_gains - gains_high], axis=1).astype(BF)
    gains_two = jnp.pad(gains_two, ((0, 0), (0, 14), (0, model_width - gains_two.shape[2])))
    attn_got = lax.all_to_all(
        attn_sent.reshape(n_expert, own_rows, 4 * head_width),
        "expert",
        split_axis=0,
        concat_axis=0,
        tiled=True,
    )
    sent = jnp.concatenate(
        [d_rows.astype(BF).reshape(n_expert, slots, model_width), gains_two], axis=1
    )
    got = lax.all_to_all(sent, "expert", split_axis=0, concat_axis=0, tiled=True)
    got_rows = got[:, :slots].reshape(n_expert * slots, model_width)

    def scatter_step(k, carry):
        d_far, ids_far, total = carry
        here = ids_far // vocab_rows == own_shard
        local = jnp.where(here, ids_far % vocab_rows, 0)
        d_sum = d_far[0].astype(F32) + d_far[1].astype(F32)
        total = total.at[local].add(jnp.where(here[:, None], d_sum, 0.0))
        ring = [(j, (j + 1) % n_expert) for j in range(n_expert)]
        return lax.ppermute(d_far, "expert", ring), lax.ppermute(ids_far, "expert", ring), total

    d_base = lax.fori_loop(
        0,
        jnp.where(any_overflow, n_expert, 0),
        scatter_step,
        ((d_high, d_low), ids, d_base),
    )[2]
    g_table, table_squares = finish(d_base, asked_rows, got_rows, vocab_rows)
    g_attn = jnp.sum(attn_got.astype(F32), axis=0)
    g_attn_in = g_attn[:, : 3 * head_width].reshape(own_rows, 3, head_width)
    g_attn_out = g_attn[:, 3 * head_width :]
    g_gains = jnp.sum(got[:, slots : slots + 2, : 3 * own_rows].astype(F32), axis=(0, 1))
    g_gains = g_gains.reshape(3, own_rows).T
    w_far, _ = far_flip(w_sent, "hidden", 2, table_squares[0, 0])
    g_expert = jnp.stack(d_w[0]) + w_near[1] + w_far.astype(F32)
    g_expert_in = g_expert[0][None]
    g_expert_out = g_expert[1][None]

    squares = (
        jnp.sum(table_squares)
        + jnp.sum(g_attn * g_attn)
        + jnp.sum(g_expert * g_expert)
        + jnp.sum(g_gains * g_gains) / n_hidden
    )
    both_sums = jnp.stack([squares, loss_part * (2.0 / n_hidden)])
    both_sums = jnp.broadcast_to(jnp.pad(both_sums, (0, 126))[None], (n_expert, 128))
    both_sums = lax.all_to_all(both_sums, "expert", split_axis=0, concat_axis=0, tiled=True)
    both_sums = lax.all_gather(jnp.sum(both_sums, axis=0), "hidden", axis=0)
    both_sums = jnp.sum(both_sums, axis=0)
    clip_norm = jnp.sqrt(both_sums[0])
    loss_value = both_sums[1]
    clip_scale = jnp.minimum(1.0, CLIP_AT / clip_norm)
    table_up = adam_step(
        embed_table, embed_first, embed_second, g_table * clip_scale, RATE_MATRIX, DECAY
    )
    attn_in_up = adam_step(
        attn_in, attn_in_first, attn_in_second, g_attn_in * clip_scale, RATE_MATRIX, DECAY
    )
    attn_out_up = adam_step(
        attn_out, attn_out_first, attn_out_second, g_attn_out * clip_scale, RATE_MATRIX, DECAY
    )
    expert_in_up = adam_step(
        expert_in,
        expert_in_first,
        expert_in_second,
        g_expert_in * clip_scale,
        RATE_MATRIX,
        DECAY,
    )
    expert_out_up = adam_step(
        expert_out,
        expert_out_first,
        expert_out_second,
        g_expert_out * clip_scale,
        RATE_MATRIX,
        DECAY,
    )
    gains_up = adam_step(
        norm_gains, gains_first, gains_second, g_gains * clip_scale, RATE_GAIN, 0.0
    )
    return (
        loss_value,
        clip_norm,
        *table_up,
        *attn_in_up,
        *attn_out_up,
        *expert_in_up,
        *expert_out_up,
        *gains_up,
    )


def solution(mesh):
    rows = P("expert", None)
    table = P(("expert", "hidden"), None)
    wide = P("expert", None, "hidden")
    flat = P("expert", "hidden")
    tall = P("expert", "hidden", None)
    groups = (table, wide, flat, wide, tall, rows)
    each = tuple(spec for spec in groups for _ in range(3))
    return jax.shard_map(
        on_device,
        mesh=mesh,
        in_specs=(rows, rows, rows, P(), *each),
        out_specs=(P(), P(), *each),
        check_vma=False,
    )
```

```python
from functools import partial

import jax
import jax.numpy as jnp
from jax import lax
from jax.experimental import pallas as pl
from jax.experimental.pallas import tpu as pltpu
from jax.sharding import PartitionSpec as P

HD = 64
DOCS_ROW = 8
STEP = 7


EPS_NORM = 1e-06
BETA_ONE = 0.9
BETA_TWO = 0.95
ADAM_EPS = 1e-08
RATE_MATRIX = 0.05
RATE_GAIN = 0.3
DECAY = 0.1
CLIP_AT = 0.005
NEVER = -1e30
BF = jnp.bfloat16
F32 = jnp.float32
VMEM = 56 * 1024 * 1024
SHORT = pl.CostEstimate(flops=1024, bytes_accessed=1024, transcendentals=0)


def flip(x, axis, k):
    return lax.ppermute(x, axis, [(j, j ^ k) for j in range(lax.axis_size(axis))])


def behind(x, after):
    return jnp.where(after == after, x, 0)


def far_flip(x, axis, k, after=None):
    pairs = [[j, j ^ k] for j in range(lax.axis_size(axis)) if not j & k]
    both = lax.all_gather(x, axis, axis_index_groups=pairs)
    upper = (lax.axis_index(axis) // k) % 2
    if after is not None:
        upper = behind(upper, after)
    return lax.dynamic_index_in_dim(both, 1 - upper, 0, keepdims=False), both


def hidden_gather(x, after=None):
    far = flip(x, "hidden", 2)
    if after is not None:
        far = behind(far, after)
    return [x, far, flip(x, "hidden", 1), flip(far, "hidden", 1)]


def piece_of(bits):
    return (bits >> 1) + 2 * (bits & 1)


def round_up(n, m):
    return -(-n // m) * m


def dot(a, b, ca=1, cb=0):
    return lax.dot_general(a, b, (((ca,), (cb,)), ((), ())), preferred_element_type=F32)


def hot_rows(place, count):
    return (jnp.arange(count, dtype=jnp.int32)[:, None] == place[None, :]).astype(BF)


def hot_columns(place, count):
    return (place[:, None] == jnp.arange(count, dtype=jnp.int32)[None, :]).astype(BF)


QB = 256
SPAN = 2


ANY = pl.BlockSpec(memory_space=pl.ANY)
WHOLE = pl.BlockSpec(memory_space=pltpu.VMEM)


def bias_of(first, second, axis, at_first, at_second):
    shape = (first.shape[0], second.shape[1])
    pos_a = lax.broadcasted_iota(jnp.int32, shape, 0) + at_first
    pos_b = lax.broadcasted_iota(jnp.int32, shape, 1) + at_second
    seen = (pos_a >= pos_b) if axis == 0 else (pos_b >= pos_a)
    return jnp.where(seen & (first == second), 0.0, NEVER)


def pack_kernel(in_ref, out_ref, *rest):
    o_ref = rest[-1]
    width = out_ref.shape[1]
    for c in range(3):
        o_ref[:, c * width : (c + 1) * width] = in_ref[c].astype(BF)
    o_ref[:, 3 * width :] = out_ref[...].astype(BF)


def pack(attn_in, attn_out, ready):
    rows, width = attn_out.shape
    return pl.pallas_call(
        pack_kernel,
        in_specs=[WHOLE] * 2 + [ANY] * len(ready),
        out_specs=WHOLE,
        out_shape=jax.ShapeDtypeStruct((rows, 4 * width), BF),
        name="pack",
    )(attn_in.transpose(1, 0, 2), attn_out, *ready)


def attend_kernel(rows_ref, w_ref, segr_ref, segc_ref, *rest):
    qkv_ref, o_ref, part_ref = rest[-3:]
    pieces, seq, width = o_ref.shape
    wide = 3 * width
    factor = jnp.asarray(HD**-0.5, BF)
    heads = [(p, c) for p in range(pieces) for c in range(0, width, HD)]
    for p in range(pieces):
        qkv_ref[p] = dot(rows_ref[...], w_ref[p, :, : 3 * width]).astype(BF)
    for b in range(seq // QB):
        lo, at, hi = max(0, b - SPAN) * QB, b * QB, (b + 1) * QB
        bias = bias_of(segc_ref[at:hi, :], segr_ref[:, lo:hi], 0, at, lo)
        scores = []
        for p, c in heads:
            q = qkv_ref[p, at:hi, c : c + HD] * factor
            scores.append(dot(q, qkv_ref[p, lo:hi, width + c : width + c + HD], 1, 1))
        probs = []
        for s in scores:
            s = s + bias
            e = jnp.exp(s - jnp.max(s, axis=1, keepdims=True))
            probs.append((e * (1.0 / jnp.sum(e, axis=1, keepdims=True))).astype(BF))
        outs = [
            dot(prob, qkv_ref[p, lo:hi, 2 * width + c : 2 * width + c + HD])
            for prob, (p, c) in zip(probs, heads, strict=True)
        ]
        for out, (p, c) in zip(outs, heads, strict=True):
            o_ref[p, at:hi, c : c + HD] = out.astype(BF)
    total = dot(o_ref[0], w_ref[0, :, wide : wide + width], 1, 1)
    for p in range(1, pieces):
        total += dot(o_ref[p], w_ref[p, :, wide : wide + width], 1, 1)
    part_ref[...] = total


def attend(rows, packed, width, seg, ready):
    seq, model = rows.shape
    pieces = packed.shape[0]
    return pl.pallas_call(
        attend_kernel,
        in_specs=[WHOLE] * 4 + [ANY] * len(ready),
        out_specs=[WHOLE] * 3,
        out_shape=[
            jax.ShapeDtypeStruct((pieces, seq, 3 * width), BF),
            jax.ShapeDtypeStruct((pieces, seq, width), BF),
            jax.ShapeDtypeStruct((seq, model), F32),
        ],
        compiler_params=pltpu.CompilerParams(vmem_limit_bytes=VMEM),
        cost_estimate=SHORT,
        name="attend",
    )(rows, packed, seg[None, :], seg[:, None], *ready)


def attend_back_kernel(branch_ref, w_ref, qkv_ref, segr_ref, segc_ref, *rest):
    d_ref, part_ref, g_ref, dk_acc, dv_acc = rest[-5:]
    pieces, seq, width = g_ref.shape
    wide = 3 * width
    scale = HD**-0.5
    factor = jnp.asarray(scale, BF)
    heads = [(p, c) for p in range(pieces) for c in range(0, width, HD)]
    for p in range(pieces):
        g_ref[p] = dot(branch_ref[...], w_ref[p, :, wide : wide + width]).astype(BF)
    dk_acc[...] = jnp.zeros_like(dk_acc)
    dv_acc[...] = jnp.zeros_like(dv_acc)
    for b in range(seq // QB):
        lo, at, hi = max(0, b - SPAN) * QB, b * QB, (b + 1) * QB
        bias = bias_of(segc_ref[lo:hi, :], segr_ref[:, at:hi], 1, lo, at)
        for group in (heads[: len(heads) // 2], heads[len(heads) // 2 :]):
            qs = [qkv_ref[p, at:hi, c : c + HD] * factor for p, c in group]
            ks = [qkv_ref[p, lo:hi, width + c : width + c + HD] for p, c in group]
            gs = [g_ref[p, at:hi, c : c + HD] for p, c in group]
            scores = [dot(k, q, 1, 1) for k, q in zip(ks, qs, strict=True)]
            d_probs = [
                dot(qkv_ref[p, lo:hi, 2 * width + c : 2 * width + c + HD], g, 1, 1)
                for (p, c), g in zip(group, gs, strict=True)
            ]
            probs, d_scores = [], []
            for s, d_prob in zip(scores, d_probs, strict=True):
                s = s + bias
                e = jnp.exp(s - jnp.max(s, axis=0, keepdims=True))
                prob = e * (1.0 / jnp.sum(e, axis=0, keepdims=True))
                centre = jnp.sum(prob * d_prob, axis=0, keepdims=True)
                d_scores.append((prob * (d_prob - centre)).astype(BF))
                probs.append(prob.astype(BF))
            dqs = [dot(d, k, 0, 0) for d, k in zip(d_scores, ks, strict=True)]
            dks = [dot(d, q) for d, q in zip(d_scores, qs, strict=True)]
            dvs = [dot(prob, g) for prob, g in zip(probs, gs, strict=True)]
            for i, (p, c) in enumerate(group):
                d_ref[p, at:hi, c : c + HD] = (dqs[i] * scale).astype(BF)
                dk_acc[p, lo:hi, c : c + HD] += dks[i]
                dv_acc[p, lo:hi, c : c + HD] += dvs[i]
    d_ref[:, :, width : 2 * width] = dk_acc[...].astype(BF)
    d_ref[:, :, 2 * width :] = dv_acc[...].astype(BF)
    total = dot(d_ref[0], w_ref[0, :, : 3 * width], 1, 1)
    for p in range(1, pieces):
        total += dot(d_ref[p], w_ref[p, :, : 3 * width], 1, 1)
    part_ref[...] = total


def attend_back(branch, packed, qkv, seg, ready):
    seq, model = branch.shape
    pieces, _, width = qkv.shape
    return pl.pallas_call(
        attend_back_kernel,
        in_specs=[WHOLE] * 5 + [ANY] * len(ready),
        out_specs=[WHOLE] * 2,
        out_shape=[
            jax.ShapeDtypeStruct((pieces, seq, width), BF),
            jax.ShapeDtypeStruct((seq, model), F32),
        ],
        scratch_shapes=[
            pltpu.VMEM((pieces, seq, width // 3), BF),
            pltpu.VMEM((pieces, seq, width // 3), F32),
            pltpu.VMEM((pieces, seq, width // 3), F32),
        ],
        compiler_params=pltpu.CompilerParams(vmem_limit_bytes=VMEM),
        cost_estimate=SHORT,
        name="attend_back",
    )(branch, packed, qkv, seg[None, :], seg[:, None], *ready)


def attn_grad_kernel(rows_ref, d_ref, branch_ref, o_ref, *rest):
    out_ref = rest[-1]
    width = d_ref.shape[2]
    out_ref[:, :width] = dot(rows_ref[...], d_ref[0], 0, 0).astype(BF)
    out_ref[:, width:] = dot(branch_ref[...], o_ref[0], 0, 0).astype(BF)


def attn_grad(rows, d_qkv, branch, attended, ready):
    model = rows.shape[1]
    seq, third = attended.shape[1:]
    one = pl.BlockSpec((1, seq, 3 * third), lambda i: (0, 0, 0))
    two = pl.BlockSpec((1, seq, third), lambda i: (0, 0, 0))
    full = pl.BlockSpec((seq, model), lambda i: (0, 0))
    return pl.pallas_call(
        attn_grad_kernel,
        grid=(1,),
        in_specs=[full, one, full, two] + [ANY] * len(ready),
        out_specs=pl.BlockSpec((model, 4 * third), lambda i: (0, 0)),
        out_shape=jax.ShapeDtypeStruct((model, 4 * third), BF),
        compiler_params=pltpu.CompilerParams(vmem_limit_bytes=VMEM),
        cost_estimate=SHORT,
        name="attn_grad",
    )(rows, d_qkv, branch, attended, *ready)


def picked(place_ref, *row_refs):
    count = row_refs[0].shape[0]
    at = lax.broadcasted_iota(jnp.int32, (place_ref.shape[0], count), 1)
    total = None
    for q, ref in enumerate(row_refs):
        part = dot((at == place_ref[...] - q * count).astype(BF), ref[...])
        total = part if total is None else total + part
    return total


def pick_norm_kernel(scale, pick, parts, base, *refs):
    first_refs, refs = refs[:parts], refs[parts:]
    if base:
        base_ref, refs = refs[0], refs[1:]
    gain_ref, sum_ref, norm_ref = refs[0], refs[-2], refs[-1]
    if pick:
        x = picked(*first_refs)
    else:
        x = first_refs[0][...]
        for ref in first_refs[1:]:
            x = x + ref[...]
    if base:
        x = base_ref[...] + x
    if scale != 1.0:
        x = x * scale
    sum_ref[...] = x
    root = lax.rsqrt(jnp.mean(x * x, axis=1, keepdims=True) + EPS_NORM)
    norm_ref[...] = (x * root * gain_ref[...]).astype(BF)


def pick_norm(first, base, gain, scale=1.0, pick=True, ready=()):
    tokens = first[0].shape[0]
    width = gain.shape[1]
    block = min(tokens, 256)
    by_rows = pl.BlockSpec((block, width), lambda i: (i, 0))
    if pick:
        first = (first[0][:, None], *first[1:])
        specs = [pl.BlockSpec((block, 1), lambda i: (i, 0))]
        specs += [pl.BlockSpec(r.shape, lambda i: (0, 0)) for r in first[1:]]
    else:
        specs = [by_rows] * len(first)
    has_base = base is not None
    return pl.pallas_call(
        partial(pick_norm_kernel, scale, pick, len(first), has_base),
        grid=(tokens // block,),
        in_specs=specs
        + [by_rows] * has_base
        + [pl.BlockSpec((1, width), lambda i: (0, 0))]
        + [ANY] * len(ready),
        out_specs=[by_rows, by_rows],
        out_shape=[
            jax.ShapeDtypeStruct((tokens, width), F32),
            jax.ShapeDtypeStruct((tokens, width), BF),
        ],
        compiler_params=pltpu.CompilerParams(vmem_limit_bytes=VMEM),
        cost_estimate=SHORT,
        name="pick_norm",
    )(*first, *((base,) if has_base else ()), gain, *ready)


def norm_back_kernel(scale, parts, pick, rest, split, x_ref, gain_ref, *refs):
    g_refs, refs = refs[:parts], refs[parts:]
    if rest:
        rest_ref, refs = refs[0], refs[1:]
    gain_out, one_ref, two_ref = refs[-3:]
    x = x_ref[...]
    if pick == "rows":
        g = picked(*g_refs)
    elif pick == "blocks":
        which = g_refs[0][pl.program_id(0)]
        g = g_refs[1][...].astype(F32)
        for q, ref in enumerate(g_refs[2:], 1):
            g = jnp.where(which == q, ref[...].astype(F32), g)
    else:
        g = g_refs[0][...].astype(F32)
        for ref in g_refs[1:]:
            g = g + ref[...].astype(F32)
    root = lax.rsqrt(jnp.mean(x * x, axis=1, keepdims=True) + EPS_NORM)
    scaled = x * root
    d_gain = jnp.sum(g * scaled, axis=0, keepdims=True)
    g = g * gain_ref[...]
    dx = root * (g - scaled * jnp.mean(g * scaled, axis=1, keepdims=True))
    if rest:
        dx = rest_ref[...] + dx
    if scale != 1.0:
        dx = dx * scale
    high = dx.astype(BF)
    one_ref[...] = high
    two_ref[...] = (dx - high.astype(F32)).astype(BF) if split else dx

    @pl.when(pl.program_id(0) == 0)
    def _():
        gain_out[...] = d_gain

    @pl.when(pl.program_id(0) > 0)
    def _():
        gain_out[...] += d_gain


def norm_back(x, gain, gradients, rest=None, scale=1.0, split=False, pick="", ready=()):
    tokens, width = x.shape
    block = min(tokens, 256)
    by_rows = pl.BlockSpec((block, width), lambda i: (i, 0))
    one_row = pl.BlockSpec((1, width), lambda i: (0, 0))
    has_rest = rest is not None
    whole = [pl.BlockSpec(g.shape, lambda i: (0, 0)) for g in gradients[1:]]
    if pick == "rows":
        gradients = (gradients[0][:, None], *gradients[1:])
        specs = [pl.BlockSpec((block, 1), lambda i: (i, 0)), *whole]
    elif pick == "blocks":
        specs = [pl.BlockSpec(memory_space=pltpu.SMEM), *whole]
    else:
        specs = [by_rows] * len(gradients)
    return pl.pallas_call(
        partial(norm_back_kernel, scale, len(gradients), pick, has_rest, split),
        grid=(tokens // block,),
        in_specs=[by_rows, one_row] + specs + [by_rows] * has_rest + [ANY] * len(ready),
        out_specs=[one_row, by_rows, by_rows],
        out_shape=[
            jax.ShapeDtypeStruct((1, width), F32),
            jax.ShapeDtypeStruct((tokens, width), BF),
            jax.ShapeDtypeStruct((tokens, width), BF if split else F32),
        ],
        compiler_params=pltpu.CompilerParams(vmem_limit_bytes=VMEM),
        cost_estimate=SHORT,
        name="norm_back",
    )(x, gain, *gradients, *((rest,) if has_rest else ()), *ready)


ERFC = (
    -1.26551223,
    1.00002368,
    0.37409196,
    0.09678418,
    -0.18628806,
    0.27886807,
    -1.13520398,
    1.48851587,
    -0.82215223,
    0.17087277,
)


def gelu_and_slope(x):
    t = 1.0 / (1.0 + 0.35355339059327373 * jnp.abs(x))
    poly = jnp.full_like(t, ERFC[-1])
    for c in ERFC[-2::-1]:
        poly = poly * t + c
    square = 0.5 * x * x
    half = 0.5 * t * jnp.exp(poly - square)
    below = jnp.where(x >= 0.0, 1.0 - half, half)
    return x * below, below + x * jnp.exp(-square) * 0.3989422804014327


def expert_kernel(rows_ref, *refs):
    w_refs, out_ref, active_refs, slope_refs = refs[:4], refs[4], refs[5:9], refs[9:]
    rows = rows_ref[...]
    total = None
    for w_ref, active_ref, slope_ref in zip(w_refs, active_refs, slope_refs, strict=True):
        value, slope_ref[...] = gelu_and_slope(dot(rows, w_ref[0]))
        active = value.astype(BF)
        active_ref[...] = active
        product = dot(active, w_ref[1])
        total = product if total is None else total + product
    out_ref[...] = total.astype(BF)


def expert(rows, weights):
    hidden = jax.ShapeDtypeStruct((rows.shape[0], weights[0].shape[2]), BF)
    slope = jax.ShapeDtypeStruct(hidden.shape, F32)
    out, *rest = pl.pallas_call(
        expert_kernel,
        in_specs=[WHOLE] * 5,
        out_specs=[WHOLE] * 9,
        out_shape=[jax.ShapeDtypeStruct(rows.shape, BF)] + [hidden] * 4 + [slope] * 4,
        compiler_params=pltpu.CompilerParams(vmem_limit_bytes=VMEM),
        cost_estimate=SHORT,
        name="expert",
    )(rows, *weights)
    return out, rest[:4], rest[4:]


def expert_back_kernel(grad_ref, *refs):
    w_refs, slope_refs, refs = refs[:4], refs[4:8], refs[8:]
    out_ref, d_refs = refs[-5], refs[-4:]
    grad = grad_ref[...]
    total = None
    for w_ref, slope_ref, d_ref in zip(w_refs, slope_refs, d_refs, strict=True):
        d_pre = (dot(grad, w_ref[1], 1, 1) * slope_ref[...]).astype(BF)
        d_ref[...] = d_pre
        product = dot(d_pre, w_ref[0], 1, 1)
        total = product if total is None else total + product
    out_ref[...] = total.astype(BF)


def expert_back(grad, weights, slopes, ready):
    return pl.pallas_call(
        expert_back_kernel,
        in_specs=[WHOLE] * 9 + [ANY] * len(ready),
        out_specs=[WHOLE] * 5,
        out_shape=[jax.ShapeDtypeStruct(grad.shape, BF)]
        + [jax.ShapeDtypeStruct(slope.shape, BF) for slope in slopes],
        compiler_params=pltpu.CompilerParams(vmem_limit_bytes=VMEM),
        cost_estimate=SHORT,
        name="expert_back",
    )(grad, *weights, *slopes, *ready)


def part_rows(padded):
    return max(r for r in range(32, 385, 32) if padded % r == 0)


def cast_pick_kernel(real, place_ref, x_ref, table_ref, o_ref, acc):
    j = pl.program_id(0)
    rows = x_ref.shape[0]
    at = lax.broadcasted_iota(jnp.int32, x_ref.shape, 0) + j * rows
    table_ref[...] = jnp.where(at < real, x_ref[...], 0.0).astype(BF)
    column = lax.broadcasted_iota(jnp.int32, (place_ref.shape[0], rows), 1) + j * rows
    found = dot((column == place_ref[...]).astype(BF), table_ref[...])

    @pl.when(j == 0)
    def _():
        acc[...] = found

    @pl.when(j > 0)
    def _():
        acc[...] += found

    @pl.when(j == pl.num_programs(0) - 1)
    def _():
        o_ref[...] = acc[...].astype(BF)


def cast_pick(place, x, padded):
    real, width = x.shape
    rows = part_rows(padded)
    count = place.shape[0]
    return pl.pallas_call(
        partial(cast_pick_kernel, real),
        grid=(padded // rows,),
        in_specs=[
            pl.BlockSpec((count, 1), lambda j: (0, 0)),
            pl.BlockSpec((rows, width), lambda j: (j, 0)),
        ],
        out_specs=[
            pl.BlockSpec((rows, width), lambda j: (j, 0)),
            pl.BlockSpec((count, width), lambda j: (0, 0)),
        ],
        out_shape=[
            jax.ShapeDtypeStruct((padded, width), BF),
            jax.ShapeDtypeStruct((count, width), BF),
        ],
        scratch_shapes=[pltpu.VMEM((count, width), F32)],
        compiler_params=pltpu.CompilerParams(vmem_limit_bytes=VMEM),
        cost_estimate=SHORT,
        name="cast_pick",
    )(place[:, None], x)


def turn_kernel(a_ref, b_ref, c_ref, d_ref, o_ref):
    o_ref[...] = jnp.concatenate([a_ref[...], b_ref[...], c_ref[...], d_ref[...]], axis=0).T


def turned(slices):
    padded, width = slices[0].shape
    rows = part_rows(padded)
    return pl.pallas_call(
        turn_kernel,
        grid=(padded // rows,),
        in_specs=[pl.BlockSpec((rows, width), lambda j: (j, 0))] * 4,
        out_specs=pl.BlockSpec((width, 4 * rows), lambda j: (0, j)),
        out_shape=jax.ShapeDtypeStruct((width, 4 * padded), BF),
        compiler_params=pltpu.CompilerParams(vmem_limit_bytes=VMEM),
        cost_estimate=pl.CostEstimate(flops=0, bytes_accessed=24 * padded * width, transcendentals=0),
        name="turned",
    )(*slices)


def logits_kernel(
    real, a_ref, b_ref, c_ref, d_ref, rows_ref, col_ref, *rest
):
    out_ref, peak_ref, stat_ref, peak_s, sum_s, hit_s = rest[-6:]
    j = pl.program_id(0)
    tokens = rows_ref.shape[0]
    part = a_ref.shape[0]

    @pl.when(j == 0)
    def _():
        peak_s[...] = jnp.full((8, tokens), NEVER, F32)
        sum_s[...] = jnp.zeros((8, tokens), F32)
        hit_s[...] = jnp.zeros((8, tokens), F32)

    away = col_ref[...] - j * (4 * part) - lax.broadcasted_iota(jnp.int32, (8, tokens), 0)
    peak, total, hit = peak_s[...], sum_s[...], hit_s[...]
    rows = rows_ref[...]
    tail = round_up(part * (-(-real // part)) - real, 8)
    for q, ref in enumerate((a_ref, b_ref, c_ref, d_ref)):
        logits = dot(ref[...], rows, 1, 1)
        if tail:
            at = lax.broadcasted_iota(jnp.int32, (tail, tokens), 0) + (j + 1) * part - tail
            end = jnp.where(at < real, logits[part - tail :], NEVER)
            logits = jnp.concatenate([logits[: part - tail], end], axis=0)
        tiles = logits.reshape(part // 8, 8, tokens)
        new = jnp.maximum(peak, jnp.max(tiles, axis=0))
        powers = jnp.exp(tiles - new[None])
        out_ref[q * part : (q + 1) * part, :] = powers.reshape(part, tokens)
        peak_ref[q * 8 : (q + 1) * 8, :] = new
        total = total * jnp.exp(peak - new) + jnp.sum(powers, axis=0)
        for i in range(part // 8):
            hit = hit + jnp.where(away == q * part + 8 * i, tiles[i], 0.0)
        peak = new
    peak_s[...], sum_s[...], hit_s[...] = peak, total, hit

    @pl.when(j == pl.num_programs(0) - 1)
    def _():
        top = jnp.max(peak, axis=0, keepdims=True)
        stat_ref[0:1, :] = top
        stat_ref[1:2, :] = jnp.sum(total * jnp.exp(peak - top), axis=0, keepdims=True)
        stat_ref[2:3, :] = jnp.sum(hit, axis=0, keepdims=True)
        stat_ref[3:8, :] = jnp.zeros((5, tokens), F32)


def head_logits(slices, rows, col, real, ready=()):
    padded, width = slices[0].shape
    tokens = rows.shape[0]
    part = part_rows(padded)
    steps = padded // part
    return pl.pallas_call(
        partial(logits_kernel, real),
        grid=(steps,),
        in_specs=[pl.BlockSpec((part, width), lambda j: (j, 0))] * 4
        + [
            pl.BlockSpec((tokens, width), lambda j: (0, 0)),
            pl.BlockSpec((1, tokens), lambda j: (0, 0)),
        ]
        + [ANY] * len(ready),
        out_specs=[
            pl.BlockSpec((4 * part, tokens), lambda j: (j, 0)),
            pl.BlockSpec((32, tokens), lambda j: (j, 0)),
            pl.BlockSpec((8, tokens), lambda j: (0, 0)),
        ],
        out_shape=[
            jax.ShapeDtypeStruct((4 * padded, tokens), F32),
            jax.ShapeDtypeStruct((32 * steps, tokens), F32),
            jax.ShapeDtypeStruct((8, tokens), F32),
        ],
        scratch_shapes=[pltpu.VMEM((8, tokens), F32)] * 3,
        compiler_params=pltpu.CompilerParams(vmem_limit_bytes=VMEM),
        cost_estimate=pl.CostEstimate(flops=16 * padded * tokens * width, bytes_accessed=16 * padded * tokens, transcendentals=0),
        name="head_logits",
    )(*slices, rows, col, *ready)


def head_back_kernel(table_ref, power_ref, peak_ref, col_ref, side_ref, *rest):
    d_ref, out_ref, acc = rest[-3:]
    j = pl.program_id(0)
    block, tokens = power_ref.shape
    part = block // 4
    away = col_ref[...] - j * block - lax.broadcasted_iota(jnp.int32, (8, tokens), 0)
    log_total, weight = side_ref[0:1, :], side_ref[1:2, :]
    pieces = []
    for q in range(4):
        factor = jnp.exp(peak_ref[q * 8 : (q + 1) * 8, :] - log_total) * weight
        for i in range(part // 8):
            at = q * part + 8 * i
            less = jnp.where(away == at, weight, 0.0)
            pieces.append(power_ref[at : at + 8, :] * factor - less)
    d = jnp.concatenate(pieces, axis=0).astype(BF)
    d_ref[...] = d
    product = dot(table_ref[...], d)

    @pl.when(j == 0)
    def _():
        acc[...] = product

    @pl.when(j > 0)
    def _():
        acc[...] += product

    @pl.when(j == pl.num_programs(0) - 1)
    def _():
        out_ref[...] = acc[...].T.astype(out_ref.dtype)


def head_back(table_t, powers, peaks, at, col, side, ready=()):
    width, vocab = table_t.shape
    tokens = col.shape[1]
    steps = peaks.shape[0] // 32
    block = vocab // steps
    return pl.pallas_call(
        head_back_kernel,
        grid=(steps,),
        in_specs=[
            pl.BlockSpec((width, block), lambda j: (0, j)),
            pl.BlockSpec((block, tokens), lambda j: (j, at)),
            pl.BlockSpec((32, tokens), lambda j: (j, at)),
            pl.BlockSpec((1, tokens), lambda j: (0, 0)),
            pl.BlockSpec((8, tokens), lambda j: (0, 0)),
        ]
        + [ANY] * len(ready),
        out_specs=[
            pl.BlockSpec((block, tokens), lambda j: (j, 0)),
            pl.BlockSpec((tokens, width), lambda j: (0, 0)),
        ],
        out_shape=[
            jax.ShapeDtypeStruct((vocab, tokens), BF),
            jax.ShapeDtypeStruct((tokens, width), BF),
        ],
        scratch_shapes=[pltpu.VMEM((width, tokens), F32)],
        compiler_params=pltpu.CompilerParams(vmem_limit_bytes=VMEM),
        cost_estimate=pl.CostEstimate(flops=4 * vocab * tokens * width, bytes_accessed=6 * vocab * tokens, transcendentals=0),
        name="head_back",
    )(table_t, powers, peaks, col, side, *ready)


def table_grad_kernel(count, *refs):
    d_refs, row_refs, out_refs = refs[: 2 * count], refs[2 * count : 3 * count], refs[-2:]
    total = None
    for k in range(count):
        both = jnp.concatenate([d_refs[2 * k][...], d_refs[2 * k + 1][...]], axis=0)
        product = dot(both, row_refs[k][...])
        total = product if total is None else total + product
    part = out_refs[0].shape[0]
    for q in range(2):
        out_refs[q][...] = total[q * part : (q + 1) * part].astype(out_refs[q].dtype)


def table_grad(ds, rows, padded, which, ready):
    width = rows[0].shape[1]
    part = part_rows(padded)

    def spec(tokens, q):
        return pl.BlockSpec((part, tokens), lambda j: (4 * j + q, 0))

    return pl.pallas_call(
        partial(table_grad_kernel, len(ds)),
        grid=(padded // part,),
        in_specs=[spec(d.shape[1], q) for d in ds for q in which]
        + [pl.BlockSpec(r.shape, lambda j: (0, 0)) for r in rows]
        + [ANY] * len(ready),
        out_specs=[pl.BlockSpec((part, width), lambda j: (j, 0))] * 2,
        out_shape=[jax.ShapeDtypeStruct((padded, width), t) for t in (F32, BF)],
        compiler_params=pltpu.CompilerParams(vmem_limit_bytes=VMEM),
        cost_estimate=pl.CostEstimate(
            flops=4 * padded * width * sum(d.shape[1] for d in ds),
            bytes_accessed=8 * padded * width,
            transcendentals=0,
        ),
        name="table_grad",
    )(*[d for d in ds for _ in which], *rows, *ready)


def finish_kernel(real, base_ref, place_ref, rows_ref, out_ref, square_ref):
    rows = base_ref.shape[0]
    first = pl.program_id(0) * rows
    at = lax.broadcasted_iota(jnp.int32, (rows, place_ref.shape[1]), 0) + first
    spread = dot((at == place_ref[...]).astype(BF), rows_ref[...])
    g = base_ref[...] + spread
    out_ref[...] = g
    inside = lax.broadcasted_iota(jnp.int32, g.shape, 0) + first < real
    g = jnp.where(inside, g, 0.0)
    squares = jnp.sum(g * g, axis=0, keepdims=True)

    @pl.when(pl.program_id(0) == 0)
    def _():
        square_ref[...] = squares

    @pl.when(pl.program_id(0) > 0)
    def _():
        square_ref[...] += squares


def finish(base, place, rows, real):
    padded, width = base.shape
    part = part_rows(padded)
    block = pl.BlockSpec((part, width), lambda j: (j, 0))
    return pl.pallas_call(
        partial(finish_kernel, real),
        grid=(padded // part,),
        in_specs=[
            block,
            pl.BlockSpec((1, place.shape[0]), lambda j: (0, 0)),
            pl.BlockSpec(rows.shape, lambda j: (0, 0)),
        ],
        out_specs=[block, pl.BlockSpec((1, width), lambda j: (0, 0))],
        out_shape=[
            jax.ShapeDtypeStruct((real, width), F32),
            jax.ShapeDtypeStruct((1, width), F32),
        ],
        compiler_params=pltpu.CompilerParams(vmem_limit_bytes=VMEM),
        cost_estimate=SHORT,
        name="finish",
    )(base, place[None, :], rows)


def adam_step(weight, first_moment, second_moment, gradient, step_rate, weight_decay):
    first_moment = BETA_ONE * first_moment + (1.0 - BETA_ONE) * gradient
    second_moment = BETA_TWO * second_moment + (1.0 - BETA_TWO) * gradient * gradient
    update = (
        first_moment
        / (1.0 - BETA_ONE**STEP)
        / (jnp.sqrt(second_moment / (1.0 - BETA_TWO**STEP)) + ADAM_EPS)
    )
    return (weight - step_rate * (update + weight_decay * weight), first_moment, second_moment)


def combine_stats(left, right):
    peak = jnp.maximum(left[0], right[0])
    total = left[1] * jnp.exp(left[0] - peak) + right[1] * jnp.exp(right[0] - peak)
    return jnp.stack([peak, total, left[2] + right[2]])


def on_device(
    token_ids,
    target_ids,
    doc_segments,
    hash_experts,
    embed_table,
    embed_first,
    embed_second,
    attn_in,
    attn_in_first,
    attn_in_second,
    attn_out,
    attn_out_first,
    attn_out_second,
    expert_in,
    expert_in_first,
    expert_in_second,
    expert_out,
    expert_out_first,
    expert_out_second,
    norm_gains,
    gains_first,
    gains_second,
):
    n_expert = lax.axis_size("expert")
    n_hidden = lax.axis_size("hidden")
    assert n_hidden == 4 and token_ids.shape[0] == 1
    e_index = lax.axis_index("expert")
    h_index = lax.axis_index("hidden")
    tok_count = token_ids.shape[1]
    vocab_rows, model_width = embed_table.shape
    embed_scale = model_width**0.5
    ids = token_ids[0]
    targets = target_ids[0]
    segment = doc_segments[0]
    token_at = jnp.arange(tok_count, dtype=jnp.int32)

    padded = round_up(vocab_rows, 32)
    own_rows = attn_in.shape[0]
    head_width = attn_in.shape[2]

    slots = round_up(5 * tok_count // (4 * n_expert * n_hidden), 8)
    shard = ids // vocab_rows
    shard_e, shard_h = shard // n_hidden, shard % n_hidden
    same_id = ids[:, None] == ids[None, :]
    first_at = jnp.min(jnp.where(same_id, token_at[None, :], tok_count), axis=1)
    is_first = first_at == token_at
    rank = jnp.sum(
        (
            (shard[:, None] == shard[None, :])
            & is_first[None, :]
            & (token_at[None, :] < first_at[:, None])
        ).astype(jnp.int32),
        axis=1,
    )
    overflow = jnp.max(rank) >= slots
    place_own = jnp.where(
        (shard_h == h_index) & (rank < slots), shard_e * slots + rank, -1
    )
    wanted = jnp.max(
        jnp.where(
            jnp.arange(n_expert * slots, dtype=jnp.int32)[:, None] == place_own[None, :],
            (ids % vocab_rows)[None, :],
            -1,
        ),
        axis=1,
    )
    own_gains = norm_gains.astype(BF).astype(F32).T.reshape(1, 3 * own_rows)
    own_gains = jnp.pad(own_gains, ((0, 0), (0, round_up(3 * own_rows, 128) - 3 * own_rows)))
    asked = jnp.concatenate(
        [
            wanted.reshape(n_expert, slots).astype(F32),
            jnp.broadcast_to(overflow.astype(F32), (n_expert, 128 - slots)),
            jnp.broadcast_to(own_gains, (n_expert, own_gains.shape[1])),
        ],
        axis=1,
    )

    asked = lax.all_to_all(asked, "expert", split_axis=0, concat_axis=0, tiled=True)
    any_overflow = jnp.max(asked[:, slots:128]) > 0
    asked_rows = asked[:, :slots].astype(jnp.int32).reshape(n_expert * slots)
    gain_full = asked[:, 128 : 128 + 3 * own_rows].reshape(n_expert, 3, own_rows)
    gain_full = gain_full.transpose(1, 0, 2).reshape(3, model_width)

    capacity = 3 * tok_count // (2 * n_expert)
    quarter = capacity // n_hidden
    expert_ids = hash_experts[ids]
    onehot = (expert_ids[:, None] == jnp.arange(n_expert, dtype=jnp.int32)).astype(jnp.int32)
    before = jnp.cumsum(onehot, axis=0) - onehot
    slot_rank = jnp.sum(before * onehot, axis=1)
    kept = slot_rank < capacity
    slot_h = slot_rank // quarter
    slot_in = expert_ids * quarter + slot_rank % quarter
    rows_dev = n_expert * quarter
    fill_place = jnp.where(kept & (slot_h == h_index), slot_in, -1)
    pick_place = jnp.where(kept, piece_of(slot_h ^ h_index) * rows_dev + slot_in, -1)

    asked_rows = jnp.where(any_overflow, -1, asked_rows)
    table_own, answer = cast_pick(asked_rows, embed_table, padded)
    packed = pack(attn_in, attn_out, (asked_rows,))
    packed = jnp.stack([packed, flip(packed, "hidden", 2)])
    packed = lax.all_gather(packed, "expert", axis=1, tiled=True)
    weights_own = jnp.stack([expert_in[0], expert_out[0]]).astype(BF)

    n_all = n_expert * n_hidden
    own_shard = e_index * n_hidden + h_index
    everyone = [(j, (j + 1) % n_all) for j in range(n_all)]

    answer = lax.all_to_all(
        answer.reshape(n_expert, slots, model_width),
        "expert",
        split_axis=0,
        concat_axis=0,
        tiled=True,
    )
    answers = hidden_gather(answer.reshape(n_expert * slots, model_width))
    place_all = piece_of(shard_h ^ h_index) * (n_expert * slots) + shard_e * slots + rank

    def look_up_step(k, carry):
        table_far, found = carry
        here = (own_shard - k + n_all) % n_all
        place = jnp.where(shard == here, ids % vocab_rows, -1)
        row = dot(hot_columns(place, padded), table_far).astype(BF)
        row = jnp.pad(row, ((0, 4 * n_expert * slots - tok_count), (0, 0)))
        parts = row.reshape(4, n_expert * slots, model_width)
        found = [jnp.where(k == 0, 0, found[q]) + parts[q] for q in range(4)]
        return lax.ppermute(table_far, ("expert", "hidden"), everyone), found

    answers = lax.fori_loop(
        0, jnp.where(any_overflow, n_all, 0), look_up_step, (table_own, answers)
    )[1]
    place_all = jnp.where(any_overflow, token_at, place_all)
    embedded, normed_one = pick_norm(
        (place_all, *answers), None, gain_full[0:1], embed_scale, ready=(fill_place, pick_place[:, None])
    )

    qkv, attended, attn_part = attend(normed_one, packed, head_width, segment, ())
    after_attn, normed_two = pick_norm(
        (attn_part, flip(attn_part, "hidden", 1)),
        embedded,
        gain_full[1:2],
        pick=False,
    )

    fill_hot = hot_rows(fill_place, rows_dev)

    def to_expert(rows_in, after=None):
        block = dot(fill_hot, rows_in).astype(BF)
        if after is not None:
            block = behind(block, after)
        return lax.all_to_all(block, "expert", split_axis=0, concat_axis=0, tiled=True)

    def from_expert(rows_in, after=None):
        block = lax.all_to_all(rows_in, "expert", split_axis=0, concat_axis=0, tiled=True)
        return hidden_gather(block.reshape(rows_dev, model_width), after)

    received = to_expert(normed_two)
    weights_y, _ = far_flip(weights_own, "hidden", 2, received[0, 0])
    expert_w = [
        weights_own,
        weights_y,
        flip(weights_own, "hidden", 1),
        flip(weights_y, "hidden", 1),
    ]
    expert_result, active, slope = expert(received, expert_w)
    after_moe, final_rows = pick_norm(
        (pick_place, *from_expert(expert_result)),
        after_attn,
        gain_full[2:3],
    )

    slice_x, _ = far_flip(table_own, "expert", 1, final_rows[0, 0])
    slices = [table_own, slice_x, flip(table_own, "hidden", 1), flip(slice_x, "hidden", 1)]
    table_t = turned(slices)
    part = part_rows(padded)

    half, fourth = tok_count // 2, tok_count // 4
    own_at = (h_index & 1) * half + (h_index >> 1) * fourth
    other_at = (h_index & 1) * half + (1 - (h_index >> 1)) * fourth
    n_far = n_expert // 2

    def own_order(x):
        return jnp.concatenate(
            [
                lax.dynamic_slice_in_dim(x, own_at, fourth, x.ndim - 1),
                lax.dynamic_slice_in_dim(x, other_at, fourth, x.ndim - 1),
            ],
            axis=-1,
        )

    counts = jnp.sum((segment[:, None] == segment[None, :]).astype(F32), axis=1)
    weights = 1.0 / counts / (n_expert * DOCS_ROW)
    about = own_order(jnp.stack([targets.astype(F32), weights]))
    about_all = [about] + [flip(about, "expert", 2 * k) for k in range(1, n_far)]
    own_part = lax.dynamic_slice_in_dim(final_rows, own_at, fourth, 0)
    other_part = lax.dynamic_slice_in_dim(final_rows, other_at, fourth, 0)
    far_rows = [flip(own_part, "expert", 2 * k) for k in range(1, n_far)]

    columns = []
    for k in range(n_far):
        target = about_all[k][0].astype(jnp.int32)
        block_of = target // vocab_rows
        away_e = (block_of // n_hidden) ^ e_index
        away_h = (block_of % n_hidden) ^ h_index
        mine = (away_e < 2) & (away_h < 2)
        row_of = target % vocab_rows
        column = (row_of // part) * (4 * part) + (away_e + 2 * away_h) * part + row_of % part
        columns.append(jnp.where(mine, column, -1)[None, :])
    head_rows, onward = [jnp.concatenate([own_part, other_part])], []
    powers, stats = [], []
    for k, far in enumerate(far_rows, 1):
        onward.append(behind(far, table_t[0, 0].astype(F32)) if k > 1 else far)
        head_rows.append(jnp.concatenate([onward[-1], flip(onward[-1], "hidden", 2)]))
    for k in range(0, n_far, 2):
        one, two, stat = head_logits(
            slices,
            jnp.concatenate(head_rows[k : k + 2]),
            jnp.concatenate(columns[k : k + 2], axis=1),
            vocab_rows,
            () if k else (table_t, *onward[1:]),
        )
        powers.append((one, two))
        stats += [stat[:3, :half], stat[:3, half:]]
    stat = jnp.stack(stats, axis=1)
    across = flip(stat, "hidden", 2)
    stat = combine_stats(stat, jnp.concatenate([across[..., fourth:], across[..., :fourth]], axis=2))
    far_stats = [flip(stat, "expert", 2 * k) for k in range(1, n_far)]
    for k in range(1, n_far):
        far = jnp.stack([far_stats[k - 1][:, j ^ k] for j in range(n_far)], axis=1)
        stat = combine_stats(stat, far)
    log_total = stat[0] + jnp.log(stat[1])
    loss_part = jnp.sum((log_total[0] - stat[2, 0]) * about[1])

    groups = [[0], [1]] + [[k, k + 1] for k in range(2, n_far, 2)]
    group_rows = [jnp.concatenate([head_rows[k] for k in group]) for group in groups]
    d_logits, d_parts, on_y = [None] * len(groups), [None] * n_far, []
    for i in range(len(groups) - 1, -1, -1):
        group = groups[i]
        wide_weights = jnp.concatenate([about_all[k][1] for k in group])
        wide_totals = jnp.concatenate([log_total[k] for k in group])
        side = jnp.stack([wide_totals, wide_weights] + [jnp.zeros_like(wide_totals)] * 6)
        d_logits[i], product = head_back(
            table_t,
            *powers[group[0] // 2],
            group[0] % 2,
            jnp.concatenate([columns[k] for k in group], axis=1),
            side,
            on_y[-3:-2] if i == 0 else (),
        )
        for g in reversed(range(len(group))):
            k, one = group[g], product[g * half : (g + 1) * half]
            gathered = one[:fourth].astype(F32) + flip(one[fourth:], "hidden", 2).astype(F32)
            if k:
                on_y.append(gathered.astype(BF))
                gathered = flip(on_y[-1], "expert", 2 * k).astype(F32)
            d_parts[k] = gathered
    d_quarter = sum(d_parts)
    d_quarter = d_quarter.astype(BF)
    d_four = hidden_gather(d_quarter)
    quarter_h = jnp.array([0, 2, 1, 3], jnp.int32)

    d_gain_three, d_result, d_after_moe = norm_back(
        after_moe,
        gain_full[2:3],
        (piece_of(quarter_h ^ h_index), *d_four),
        pick="blocks",
    )
    d_across = table_grad(d_logits, group_rows, padded, (1, 3), (d_result,))
    across_x = (d_across[0] + flip(d_across[1], "hidden", 1).astype(F32)).astype(BF)
    grad_in = to_expert(d_result, across_x[0, 0].astype(F32))
    d_received, *d_pre = expert_back(grad_in, expert_w, slope, ())
    d_w = [
        (dot(received, d_pre[p], 0, 0), dot(active[p], grad_in, 0, 0)) for p in range(4)
    ]
    d_same = table_grad(d_logits, group_rows, padded, (0, 2), (d_received,))

    base_x, both_x = far_flip(across_x, "expert", 1)
    d_base = d_same[0] + flip(d_same[1], "hidden", 1).astype(F32) + base_x.astype(F32)

    w_near = flip(d_w[3], "hidden", 1), flip(jnp.stack(d_w[2]), "hidden", 1)
    w_sent = jnp.stack([d_w[1][i] + w_near[0][i] for i in range(2)]).astype(BF)
    d_gain_two, d_branch, d_after_attn = norm_back(
        after_attn,
        gain_full[1:2],
        (pick_place, *from_expert(d_received, d_same[0][0, 0])),
        d_after_moe,
        pick="rows",
        ready=(w_sent,),
    )

    d_qkv, d_norm_part = attend_back(d_branch, packed, qkv, segment, (both_x,))
    d_gain_one, d_high, d_low = norm_back(
        embedded,
        gain_full[0:1],
        [d_norm_part, flip(d_norm_part, "hidden", 1)],
        d_after_attn,
        scale=embed_scale,
        split=True,
    )

    attn_sent = attn_grad(normed_one, d_qkv, d_branch, attended, (d_high,))

    row_hot = hot_rows(place_own, n_expert * slots)
    d_rows = dot(row_hot, d_high) + dot(row_hot, d_low)
    d_gains = jnp.concatenate([d_gain_one, d_gain_two, d_gain_three])
    d_gains = d_gains.reshape(3, n_expert, own_rows).transpose(1, 0, 2).reshape(n_expert, 1, -1)
    gains_high = lax.reduce_precision(d_gains, 8, 7)
    gains_two = jnp.concatenate([gains_high, d_gains - gains_high], axis=1).astype(BF)
    gains_two = jnp.pad(gains_two, ((0, 0), (0, 14), (0, model_width - gains_two.shape[2])))
    attn_got = lax.all_to_all(
        attn_sent.reshape(n_expert, own_rows, 4 * head_width),
        "expert",
        split_axis=0,
        concat_axis=0,
        tiled=True,
    )
    sent = jnp.concatenate(
        [d_rows.astype(BF).reshape(n_expert, slots, model_width), gains_two], axis=1
    )
    got = lax.all_to_all(sent, "expert", split_axis=0, concat_axis=0, tiled=True)
    got_rows = got[:, :slots].reshape(n_expert * slots, model_width)

    def scatter_step(k, carry):
        d_far, ids_far, total = carry
        here = ids_far // vocab_rows == own_shard
        local = jnp.where(here, ids_far % vocab_rows, 0)
        d_sum = d_far[0].astype(F32) + d_far[1].astype(F32)
        total = total.at[local].add(jnp.where(here[:, None], d_sum, 0.0))
        ring = [(j, (j + 1) % n_expert) for j in range(n_expert)]
        return lax.ppermute(d_far, "expert", ring), lax.ppermute(ids_far, "expert", ring), total

    d_base = lax.fori_loop(
        0,
        jnp.where(any_overflow, n_expert, 0),
        scatter_step,
        ((d_high, d_low), ids, d_base),
    )[2]
    g_table, table_squares = finish(d_base, asked_rows, got_rows, vocab_rows)
    g_attn = jnp.sum(attn_got.astype(F32), axis=0)
    g_attn_in = g_attn[:, : 3 * head_width].reshape(own_rows, 3, head_width)
    g_attn_out = g_attn[:, 3 * head_width :]
    g_gains = jnp.sum(got[:, slots : slots + 2, : 3 * own_rows].astype(F32), axis=(0, 1))
    g_gains = g_gains.reshape(3, own_rows).T
    w_far, _ = far_flip(w_sent, "hidden", 2, table_squares[0, 0])
    g_expert = jnp.stack(d_w[0]) + w_near[1] + w_far.astype(F32)
    g_expert_in = g_expert[0][None]
    g_expert_out = g_expert[1][None]

    squares = (
        jnp.sum(table_squares)
        + jnp.sum(g_attn * g_attn)
        + jnp.sum(g_expert * g_expert)
        + jnp.sum(g_gains * g_gains) / n_hidden
    )
    both_sums = jnp.stack([squares, loss_part * (2.0 / n_hidden)])
    both_sums = jnp.broadcast_to(jnp.pad(both_sums, (0, 126))[None], (n_expert, 128))
    both_sums = lax.all_to_all(both_sums, "expert", split_axis=0, concat_axis=0, tiled=True)
    both_sums = lax.all_gather(jnp.sum(both_sums, axis=0), "hidden", axis=0)
    both_sums = jnp.sum(both_sums, axis=0)
    clip_norm = jnp.sqrt(both_sums[0])
    loss_value = both_sums[1]
    clip_scale = jnp.minimum(1.0, CLIP_AT / clip_norm)
    table_up = adam_step(
        embed_table, embed_first, embed_second, g_table * clip_scale, RATE_MATRIX, DECAY
    )
    attn_in_up = adam_step(
        attn_in, attn_in_first, attn_in_second, g_attn_in * clip_scale, RATE_MATRIX, DECAY
    )
    attn_out_up = adam_step(
        attn_out, attn_out_first, attn_out_second, g_attn_out * clip_scale, RATE_MATRIX, DECAY
    )
    expert_in_up = adam_step(
        expert_in,
        expert_in_first,
        expert_in_second,
        g_expert_in * clip_scale,
        RATE_MATRIX,
        DECAY,
    )
    expert_out_up = adam_step(
        expert_out,
        expert_out_first,
        expert_out_second,
        g_expert_out * clip_scale,
        RATE_MATRIX,
        DECAY,
    )
    gains_up = adam_step(
        norm_gains, gains_first, gains_second, g_gains * clip_scale, RATE_GAIN, 0.0
    )
    return (
        loss_value,
        clip_norm,
        *table_up,
        *attn_in_up,
        *attn_out_up,
        *expert_in_up,
        *expert_out_up,
        *gains_up,
    )


def solution(mesh):
    rows = P("expert", None)
    table = P(("expert", "hidden"), None)
    wide = P("expert", None, "hidden")
    flat = P("expert", "hidden")
    tall = P("expert", "hidden", None)
    groups = (table, wide, flat, wide, tall, rows)
    each = tuple(spec for spec in groups for _ in range(3))
    return jax.shard_map(
        on_device,
        mesh=mesh,
        in_specs=(rows, rows, rows, P(), *each),
        out_specs=(P(), P(), *each),
        check_vma=False,
    )
```

```python
from functools import partial

import jax
import jax.numpy as jnp
from jax import lax
from jax.experimental import pallas as pl
from jax.experimental.pallas import tpu as pltpu
from jax.sharding import PartitionSpec as P

HD = 64
DOCS_ROW = 8
STEP = 7


EPS_NORM = 1e-06
BETA_ONE = 0.9
BETA_TWO = 0.95
ADAM_EPS = 1e-08
RATE_MATRIX = 0.05
RATE_GAIN = 0.3
DECAY = 0.1
CLIP_AT = 0.005
NEVER = -1e30
BF = jnp.bfloat16
F32 = jnp.float32
VMEM = 56 * 1024 * 1024
SHORT = pl.CostEstimate(flops=1024, bytes_accessed=1024, transcendentals=0)


def flip(x, axis, k):
    return lax.ppermute(x, axis, [(j, j ^ k) for j in range(lax.axis_size(axis))])


def behind(x, after):
    return jnp.where(after == after, x, 0)


def far_flip(x, axis, k, after=None):
    pairs = [[j, j ^ k] for j in range(lax.axis_size(axis)) if not j & k]
    both = lax.all_gather(x, axis, axis_index_groups=pairs)
    upper = (lax.axis_index(axis) // k) % 2
    if after is not None:
        upper = behind(upper, after)
    return lax.dynamic_index_in_dim(both, 1 - upper, 0, keepdims=False), both


def hidden_gather(x, after=None):
    far = flip(x, "hidden", 2)
    if after is not None:
        far = behind(far, after)
    return [x, far, flip(x, "hidden", 1), flip(far, "hidden", 1)]


def piece_of(bits):
    return (bits >> 1) + 2 * (bits & 1)


def round_up(n, m):
    return -(-n // m) * m


def dot(a, b, ca=1, cb=0):
    return lax.dot_general(a, b, (((ca,), (cb,)), ((), ())), preferred_element_type=F32)


def hot_rows(place, count):
    return (jnp.arange(count, dtype=jnp.int32)[:, None] == place[None, :]).astype(BF)


def hot_columns(place, count):
    return (place[:, None] == jnp.arange(count, dtype=jnp.int32)[None, :]).astype(BF)


QB = 256
SPAN = 2


ANY = pl.BlockSpec(memory_space=pl.ANY)
WHOLE = pl.BlockSpec(memory_space=pltpu.VMEM)


def bias_of(first, second, axis, at_first, at_second):
    shape = (first.shape[0], second.shape[1])
    pos_a = lax.broadcasted_iota(jnp.int32, shape, 0) + at_first
    pos_b = lax.broadcasted_iota(jnp.int32, shape, 1) + at_second
    seen = (pos_a >= pos_b) if axis == 0 else (pos_b >= pos_a)
    return jnp.where(seen & (first == second), 0.0, NEVER)


def pack_kernel(in_ref, out_ref, *rest):
    o_ref = rest[-1]
    width = out_ref.shape[1]
    for c in range(3):
        o_ref[:, c * width : (c + 1) * width] = in_ref[c].astype(BF)
    o_ref[:, 3 * width :] = out_ref[...].astype(BF)


def pack(attn_in, attn_out, ready):
    rows, width = attn_out.shape
    return pl.pallas_call(
        pack_kernel,
        in_specs=[WHOLE] * 2 + [ANY] * len(ready),
        out_specs=WHOLE,
        out_shape=jax.ShapeDtypeStruct((rows, 4 * width), BF),
        name="pack",
    )(attn_in.transpose(1, 0, 2), attn_out, *ready)


def attend_kernel(rows_ref, w_ref, segr_ref, segc_ref, *rest):
    qkv_ref, o_ref, part_ref = rest[-3:]
    pieces, seq, width = o_ref.shape
    wide = 3 * width
    factor = jnp.asarray(HD**-0.5, BF)
    heads = [(p, c) for p in range(pieces) for c in range(0, width, HD)]
    for p in range(pieces):
        qkv_ref[p] = dot(rows_ref[...], w_ref[p, :, : 3 * width]).astype(BF)
    for b in range(seq // QB):
        lo, at, hi = max(0, b - SPAN) * QB, b * QB, (b + 1) * QB
        bias = bias_of(segc_ref[at:hi, :], segr_ref[:, lo:hi], 0, at, lo)
        scores = []
        for p, c in heads:
            q = qkv_ref[p, at:hi, c : c + HD] * factor
            scores.append(dot(q, qkv_ref[p, lo:hi, width + c : width + c + HD], 1, 1))
        probs = []
        for s in scores:
            s = s + bias
            e = jnp.exp(s - jnp.max(s, axis=1, keepdims=True))
            probs.append((e * (1.0 / jnp.sum(e, axis=1, keepdims=True))).astype(BF))
        outs = [
            dot(prob, qkv_ref[p, lo:hi, 2 * width + c : 2 * width + c + HD])
            for prob, (p, c) in zip(probs, heads, strict=True)
        ]
        for out, (p, c) in zip(outs, heads, strict=True):
            o_ref[p, at:hi, c : c + HD] = out.astype(BF)
    total = dot(o_ref[0], w_ref[0, :, wide : wide + width], 1, 1)
    for p in range(1, pieces):
        total += dot(o_ref[p], w_ref[p, :, wide : wide + width], 1, 1)
    part_ref[...] = total


def attend(rows, packed, width, seg, ready):
    seq, model = rows.shape
    pieces = packed.shape[0]
    return pl.pallas_call(
        attend_kernel,
        in_specs=[WHOLE] * 4 + [ANY] * len(ready),
        out_specs=[WHOLE] * 3,
        out_shape=[
            jax.ShapeDtypeStruct((pieces, seq, 3 * width), BF),
            jax.ShapeDtypeStruct((pieces, seq, width), BF),
            jax.ShapeDtypeStruct((seq, model), F32),
        ],
        compiler_params=pltpu.CompilerParams(vmem_limit_bytes=VMEM),
        cost_estimate=SHORT,
        name="attend",
    )(rows, packed, seg[None, :], seg[:, None], *ready)


def attend_back_kernel(branch_ref, w_ref, qkv_ref, segr_ref, segc_ref, *rest):
    d_ref, part_ref, g_ref, dk_acc, dv_acc = rest[-5:]
    pieces, seq, width = g_ref.shape
    wide = 3 * width
    scale = HD**-0.5
    factor = jnp.asarray(scale, BF)
    heads = [(p, c) for p in range(pieces) for c in range(0, width, HD)]
    for p in range(pieces):
        g_ref[p] = dot(branch_ref[...], w_ref[p, :, wide : wide + width]).astype(BF)
    dk_acc[...] = jnp.zeros_like(dk_acc)
    dv_acc[...] = jnp.zeros_like(dv_acc)
    for b in range(seq // QB):
        lo, at, hi = max(0, b - SPAN) * QB, b * QB, (b + 1) * QB
        bias = bias_of(segc_ref[lo:hi, :], segr_ref[:, at:hi], 1, lo, at)
        for group in (heads[: len(heads) // 2], heads[len(heads) // 2 :]):
            qs = [qkv_ref[p, at:hi, c : c + HD] * factor for p, c in group]
            ks = [qkv_ref[p, lo:hi, width + c : width + c + HD] for p, c in group]
            gs = [g_ref[p, at:hi, c : c + HD] for p, c in group]
            scores = [dot(k, q, 1, 1) for k, q in zip(ks, qs, strict=True)]
            d_probs = [
                dot(qkv_ref[p, lo:hi, 2 * width + c : 2 * width + c + HD], g, 1, 1)
                for (p, c), g in zip(group, gs, strict=True)
            ]
            probs, d_scores = [], []
            for s, d_prob in zip(scores, d_probs, strict=True):
                s = s + bias
                e = jnp.exp(s - jnp.max(s, axis=0, keepdims=True))
                prob = e * (1.0 / jnp.sum(e, axis=0, keepdims=True))
                centre = jnp.sum(prob * d_prob, axis=0, keepdims=True)
                d_scores.append((prob * (d_prob - centre)).astype(BF))
                probs.append(prob.astype(BF))
            dqs = [dot(d, k, 0, 0) for d, k in zip(d_scores, ks, strict=True)]
            dks = [dot(d, q) for d, q in zip(d_scores, qs, strict=True)]
            dvs = [dot(prob, g) for prob, g in zip(probs, gs, strict=True)]
            for i, (p, c) in enumerate(group):
                d_ref[p, at:hi, c : c + HD] = (dqs[i] * scale).astype(BF)
                dk_acc[p, lo:hi, c : c + HD] += dks[i]
                dv_acc[p, lo:hi, c : c + HD] += dvs[i]
    d_ref[:, :, width : 2 * width] = dk_acc[...].astype(BF)
    d_ref[:, :, 2 * width :] = dv_acc[...].astype(BF)
    total = dot(d_ref[0], w_ref[0, :, : 3 * width], 1, 1)
    for p in range(1, pieces):
        total += dot(d_ref[p], w_ref[p, :, : 3 * width], 1, 1)
    part_ref[...] = total


def attend_back(branch, packed, qkv, seg, ready):
    seq, model = branch.shape
    pieces, _, width = qkv.shape
    return pl.pallas_call(
        attend_back_kernel,
        in_specs=[WHOLE] * 5 + [ANY] * len(ready),
        out_specs=[WHOLE] * 2,
        out_shape=[
            jax.ShapeDtypeStruct((pieces, seq, width), BF),
            jax.ShapeDtypeStruct((seq, model), F32),
        ],
        scratch_shapes=[
            pltpu.VMEM((pieces, seq, width // 3), BF),
            pltpu.VMEM((pieces, seq, width // 3), F32),
            pltpu.VMEM((pieces, seq, width // 3), F32),
        ],
        compiler_params=pltpu.CompilerParams(vmem_limit_bytes=VMEM),
        cost_estimate=SHORT,
        name="attend_back",
    )(branch, packed, qkv, seg[None, :], seg[:, None], *ready)


def attn_grad_kernel(rows_ref, d_ref, branch_ref, o_ref, *rest):
    out_ref = rest[-1]
    width = d_ref.shape[2]
    out_ref[:, :width] = dot(rows_ref[...], d_ref[0], 0, 0).astype(BF)
    out_ref[:, width:] = dot(branch_ref[...], o_ref[0], 0, 0).astype(BF)


def attn_grad(rows, d_qkv, branch, attended, ready):
    model = rows.shape[1]
    seq, third = attended.shape[1:]
    one = pl.BlockSpec((1, seq, 3 * third), lambda i: (0, 0, 0))
    two = pl.BlockSpec((1, seq, third), lambda i: (0, 0, 0))
    full = pl.BlockSpec((seq, model), lambda i: (0, 0))
    return pl.pallas_call(
        attn_grad_kernel,
        grid=(1,),
        in_specs=[full, one, full, two] + [ANY] * len(ready),
        out_specs=pl.BlockSpec((model, 4 * third), lambda i: (0, 0)),
        out_shape=jax.ShapeDtypeStruct((model, 4 * third), BF),
        compiler_params=pltpu.CompilerParams(vmem_limit_bytes=VMEM),
        cost_estimate=SHORT,
        name="attn_grad",
    )(rows, d_qkv, branch, attended, *ready)


def picked(place_ref, *row_refs):
    count = row_refs[0].shape[0]
    at = lax.broadcasted_iota(jnp.int32, (place_ref.shape[0], count), 1)
    total = None
    for q, ref in enumerate(row_refs):
        part = dot((at == place_ref[...] - q * count).astype(BF), ref[...])
        total = part if total is None else total + part
    return total


def pick_norm_kernel(scale, pick, parts, base, *refs):
    first_refs, refs = refs[:parts], refs[parts:]
    if base:
        base_ref, refs = refs[0], refs[1:]
    gain_ref, sum_ref, norm_ref = refs[0], refs[-2], refs[-1]
    if pick:
        x = picked(*first_refs)
    else:
        x = first_refs[0][...]
        for ref in first_refs[1:]:
            x = x + ref[...]
    if base:
        x = base_ref[...] + x
    if scale != 1.0:
        x = x * scale
    sum_ref[...] = x
    root = lax.rsqrt(jnp.mean(x * x, axis=1, keepdims=True) + EPS_NORM)
    norm_ref[...] = (x * root * gain_ref[...]).astype(BF)


def pick_norm(first, base, gain, scale=1.0, pick=True, ready=()):
    tokens = first[0].shape[0]
    width = gain.shape[1]
    block = min(tokens, 256)
    by_rows = pl.BlockSpec((block, width), lambda i: (i, 0))
    if pick:
        first = (first[0][:, None], *first[1:])
        specs = [pl.BlockSpec((block, 1), lambda i: (i, 0))]
        specs += [pl.BlockSpec(r.shape, lambda i: (0, 0)) for r in first[1:]]
    else:
        specs = [by_rows] * len(first)
    has_base = base is not None
    return pl.pallas_call(
        partial(pick_norm_kernel, scale, pick, len(first), has_base),
        grid=(tokens // block,),
        in_specs=specs
        + [by_rows] * has_base
        + [pl.BlockSpec((1, width), lambda i: (0, 0))]
        + [ANY] * len(ready),
        out_specs=[by_rows, by_rows],
        out_shape=[
            jax.ShapeDtypeStruct((tokens, width), F32),
            jax.ShapeDtypeStruct((tokens, width), BF),
        ],
        compiler_params=pltpu.CompilerParams(vmem_limit_bytes=VMEM),
        cost_estimate=SHORT,
        name="pick_norm",
    )(*first, *((base,) if has_base else ()), gain, *ready)


def norm_back_kernel(scale, parts, pick, rest, split, x_ref, gain_ref, *refs):
    g_refs, refs = refs[:parts], refs[parts:]
    if rest:
        rest_ref, refs = refs[0], refs[1:]
    gain_out, one_ref, two_ref = refs[-3:]
    x = x_ref[...]
    if pick == "rows":
        g = picked(*g_refs)
    elif pick == "blocks":
        which = g_refs[0][pl.program_id(0)]
        g = g_refs[1][...].astype(F32)
        for q, ref in enumerate(g_refs[2:], 1):
            g = jnp.where(which == q, ref[...].astype(F32), g)
    else:
        g = g_refs[0][...].astype(F32)
        for ref in g_refs[1:]:
            g = g + ref[...].astype(F32)
    root = lax.rsqrt(jnp.mean(x * x, axis=1, keepdims=True) + EPS_NORM)
    scaled = x * root
    d_gain = jnp.sum(g * scaled, axis=0, keepdims=True)
    g = g * gain_ref[...]
    dx = root * (g - scaled * jnp.mean(g * scaled, axis=1, keepdims=True))
    if rest:
        dx = rest_ref[...] + dx
    if scale != 1.0:
        dx = dx * scale
    high = dx.astype(BF)
    one_ref[...] = high
    two_ref[...] = (dx - high.astype(F32)).astype(BF) if split else dx

    @pl.when(pl.program_id(0) == 0)
    def _():
        gain_out[...] = d_gain

    @pl.when(pl.program_id(0) > 0)
    def _():
        gain_out[...] += d_gain


def norm_back(x, gain, gradients, rest=None, scale=1.0, split=False, pick="", ready=()):
    tokens, width = x.shape
    block = min(tokens, 256)
    by_rows = pl.BlockSpec((block, width), lambda i: (i, 0))
    one_row = pl.BlockSpec((1, width), lambda i: (0, 0))
    has_rest = rest is not None
    whole = [pl.BlockSpec(g.shape, lambda i: (0, 0)) for g in gradients[1:]]
    if pick == "rows":
        gradients = (gradients[0][:, None], *gradients[1:])
        specs = [pl.BlockSpec((block, 1), lambda i: (i, 0)), *whole]
    elif pick == "blocks":
        specs = [pl.BlockSpec(memory_space=pltpu.SMEM), *whole]
    else:
        specs = [by_rows] * len(gradients)
    return pl.pallas_call(
        partial(norm_back_kernel, scale, len(gradients), pick, has_rest, split),
        grid=(tokens // block,),
        in_specs=[by_rows, one_row] + specs + [by_rows] * has_rest + [ANY] * len(ready),
        out_specs=[one_row, by_rows, by_rows],
        out_shape=[
            jax.ShapeDtypeStruct((1, width), F32),
            jax.ShapeDtypeStruct((tokens, width), BF),
            jax.ShapeDtypeStruct((tokens, width), BF if split else F32),
        ],
        compiler_params=pltpu.CompilerParams(vmem_limit_bytes=VMEM),
        cost_estimate=SHORT,
        name="norm_back",
    )(x, gain, *gradients, *((rest,) if has_rest else ()), *ready)


def gathered_rows_kernel(place_ref, high_ref, low_ref, out_ref):
    at = lax.broadcasted_iota(jnp.int32, (out_ref.shape[0], place_ref.shape[1]), 0)
    hot = (at == place_ref[...]).astype(BF)
    out_ref[...] = (dot(hot, high_ref[...]) + dot(hot, low_ref[...])).astype(BF)


def gathered_rows(place, high, low, count):
    return pl.pallas_call(
        gathered_rows_kernel,
        in_specs=[WHOLE] * 3,
        out_specs=WHOLE,
        out_shape=jax.ShapeDtypeStruct((count, high.shape[1]), BF),
        compiler_params=pltpu.CompilerParams(vmem_limit_bytes=VMEM),
        name="gathered_rows",
    )(place[None, :], high, low)


ERFC = (
    -1.26551223,
    1.00002368,
    0.37409196,
    0.09678418,
    -0.18628806,
    0.27886807,
    -1.13520398,
    1.48851587,
    -0.82215223,
    0.17087277,
)


def gelu_and_slope(x):
    t = 1.0 / (1.0 + 0.35355339059327373 * jnp.abs(x))
    poly = jnp.full_like(t, ERFC[-1])
    for c in ERFC[-2::-1]:
        poly = poly * t + c
    square = 0.5 * x * x
    half = 0.5 * t * jnp.exp(poly - square)
    below = jnp.where(x >= 0.0, 1.0 - half, half)
    return x * below, below + x * jnp.exp(-square) * 0.3989422804014327


def expert_kernel(rows_ref, *refs):
    w_refs, out_ref, active_refs, slope_refs = refs[:4], refs[4], refs[5:9], refs[9:]
    rows = rows_ref[...]
    total = None
    for w_ref, active_ref, slope_ref in zip(w_refs, active_refs, slope_refs, strict=True):
        value, slope_ref[...] = gelu_and_slope(dot(rows, w_ref[0]))
        active = value.astype(BF)
        active_ref[...] = active
        product = dot(active, w_ref[1])
        total = product if total is None else total + product
    out_ref[...] = total.astype(BF)


def expert(rows, weights):
    hidden = jax.ShapeDtypeStruct((rows.shape[0], weights[0].shape[2]), BF)
    slope = jax.ShapeDtypeStruct(hidden.shape, F32)
    out, *rest = pl.pallas_call(
        expert_kernel,
        in_specs=[WHOLE] * 5,
        out_specs=[WHOLE] * 9,
        out_shape=[jax.ShapeDtypeStruct(rows.shape, BF)] + [hidden] * 4 + [slope] * 4,
        compiler_params=pltpu.CompilerParams(vmem_limit_bytes=VMEM),
        cost_estimate=SHORT,
        name="expert",
    )(rows, *weights)
    return out, rest[:4], rest[4:]


def expert_back_kernel(grad_ref, *refs):
    w_refs, slope_refs, refs = refs[:4], refs[4:8], refs[8:]
    out_ref, d_refs = refs[-5], refs[-4:]
    grad = grad_ref[...]
    total = None
    for w_ref, slope_ref, d_ref in zip(w_refs, slope_refs, d_refs, strict=True):
        d_pre = (dot(grad, w_ref[1], 1, 1) * slope_ref[...]).astype(BF)
        d_ref[...] = d_pre
        product = dot(d_pre, w_ref[0], 1, 1)
        total = product if total is None else total + product
    out_ref[...] = total.astype(BF)


def expert_back(grad, weights, slopes, ready):
    return pl.pallas_call(
        expert_back_kernel,
        in_specs=[WHOLE] * 9 + [ANY] * len(ready),
        out_specs=[WHOLE] * 5,
        out_shape=[jax.ShapeDtypeStruct(grad.shape, BF)]
        + [jax.ShapeDtypeStruct(slope.shape, BF) for slope in slopes],
        compiler_params=pltpu.CompilerParams(vmem_limit_bytes=VMEM),
        cost_estimate=SHORT,
        name="expert_back",
    )(grad, *weights, *slopes, *ready)


def part_rows(padded):
    return max(r for r in range(32, 385, 32) if padded % r == 0)


def cast_pick_kernel(real, place_ref, x_ref, table_ref, o_ref, acc):
    j = pl.program_id(0)
    rows = x_ref.shape[0]
    at = lax.broadcasted_iota(jnp.int32, x_ref.shape, 0) + j * rows
    table_ref[...] = jnp.where(at < real, x_ref[...], 0.0).astype(BF)
    column = lax.broadcasted_iota(jnp.int32, (place_ref.shape[0], rows), 1) + j * rows
    found = dot((column == place_ref[...]).astype(BF), table_ref[...])

    @pl.when(j == 0)
    def _():
        acc[...] = found

    @pl.when(j > 0)
    def _():
        acc[...] += found

    @pl.when(j == pl.num_programs(0) - 1)
    def _():
        o_ref[...] = acc[...].astype(BF)


def cast_pick(place, x, padded):
    real, width = x.shape
    rows = part_rows(padded)
    count = place.shape[0]
    return pl.pallas_call(
        partial(cast_pick_kernel, real),
        grid=(padded // rows,),
        in_specs=[
            pl.BlockSpec((count, 1), lambda j: (0, 0)),
            pl.BlockSpec((rows, width), lambda j: (j, 0)),
        ],
        out_specs=[
            pl.BlockSpec((rows, width), lambda j: (j, 0)),
            pl.BlockSpec((count, width), lambda j: (0, 0)),
        ],
        out_shape=[
            jax.ShapeDtypeStruct((padded, width), BF),
            jax.ShapeDtypeStruct((count, width), BF),
        ],
        scratch_shapes=[pltpu.VMEM((count, width), F32)],
        compiler_params=pltpu.CompilerParams(vmem_limit_bytes=VMEM),
        cost_estimate=SHORT,
        name="cast_pick",
    )(place[:, None], x)


def turn_kernel(a_ref, b_ref, c_ref, d_ref, o_ref):
    o_ref[...] = jnp.concatenate([a_ref[...], b_ref[...], c_ref[...], d_ref[...]], axis=0).T


def turned(slices):
    padded, width = slices[0].shape
    rows = part_rows(padded)
    return pl.pallas_call(
        turn_kernel,
        grid=(padded // rows,),
        in_specs=[pl.BlockSpec((rows, width), lambda j: (j, 0))] * 4,
        out_specs=pl.BlockSpec((width, 4 * rows), lambda j: (0, j)),
        out_shape=jax.ShapeDtypeStruct((width, 4 * padded), BF),
        compiler_params=pltpu.CompilerParams(vmem_limit_bytes=VMEM),
        cost_estimate=pl.CostEstimate(flops=0, bytes_accessed=24 * padded * width, transcendentals=0),
        name="turned",
    )(*slices)


def logits_kernel(
    real, a_ref, b_ref, c_ref, d_ref, rows_ref, col_ref, *rest
):
    out_ref, peak_ref, stat_ref, peak_s, sum_s, hit_s = rest[-6:]
    j = pl.program_id(0)
    tokens = rows_ref.shape[0]
    part = a_ref.shape[0]

    @pl.when(j == 0)
    def _():
        peak_s[...] = jnp.full((8, tokens), NEVER, F32)
        sum_s[...] = jnp.zeros((8, tokens), F32)
        hit_s[...] = jnp.zeros((8, tokens), F32)

    away = col_ref[...] - j * (4 * part) - lax.broadcasted_iota(jnp.int32, (8, tokens), 0)
    peak, total, hit = peak_s[...], sum_s[...], hit_s[...]
    rows = rows_ref[...]
    tail = round_up(part * (-(-real // part)) - real, 8)
    for q, ref in enumerate((a_ref, b_ref, c_ref, d_ref)):
        logits = dot(ref[...], rows, 1, 1)
        if tail:
            at = lax.broadcasted_iota(jnp.int32, (tail, tokens), 0) + (j + 1) * part - tail
            end = jnp.where(at < real, logits[part - tail :], NEVER)
            logits = jnp.concatenate([logits[: part - tail], end], axis=0)
        tiles = logits.reshape(part // 8, 8, tokens)
        new = jnp.maximum(peak, jnp.max(tiles, axis=0))
        powers = jnp.exp(tiles - new[None])
        out_ref[q * part : (q + 1) * part, :] = powers.reshape(part, tokens)
        peak_ref[q * 8 : (q + 1) * 8, :] = new
        total = total * jnp.exp(peak - new) + jnp.sum(powers, axis=0)
        for i in range(part // 8):
            hit = hit + jnp.where(away == q * part + 8 * i, tiles[i], 0.0)
        peak = new
    peak_s[...], sum_s[...], hit_s[...] = peak, total, hit

    @pl.when(j == pl.num_programs(0) - 1)
    def _():
        top = jnp.max(peak, axis=0, keepdims=True)
        stat_ref[0:1, :] = top
        stat_ref[1:2, :] = jnp.sum(total * jnp.exp(peak - top), axis=0, keepdims=True)
        stat_ref[2:3, :] = jnp.sum(hit, axis=0, keepdims=True)
        stat_ref[3:8, :] = jnp.zeros((5, tokens), F32)


def head_logits(slices, rows, col, real, ready=()):
    padded, width = slices[0].shape
    tokens = rows.shape[0]
    part = part_rows(padded)
    steps = padded // part
    return pl.pallas_call(
        partial(logits_kernel, real),
        grid=(steps,),
        in_specs=[pl.BlockSpec((part, width), lambda j: (j, 0))] * 4
        + [
            pl.BlockSpec((tokens, width), lambda j: (0, 0)),
            pl.BlockSpec((1, tokens), lambda j: (0, 0)),
        ]
        + [ANY] * len(ready),
        out_specs=[
            pl.BlockSpec((4 * part, tokens), lambda j: (j, 0)),
            pl.BlockSpec((32, tokens), lambda j: (j, 0)),
            pl.BlockSpec((8, tokens), lambda j: (0, 0)),
        ],
        out_shape=[
            jax.ShapeDtypeStruct((4 * padded, tokens), F32),
            jax.ShapeDtypeStruct((32 * steps, tokens), F32),
            jax.ShapeDtypeStruct((8, tokens), F32),
        ],
        scratch_shapes=[pltpu.VMEM((8, tokens), F32)] * 3,
        compiler_params=pltpu.CompilerParams(vmem_limit_bytes=VMEM),
        cost_estimate=pl.CostEstimate(flops=16 * padded * tokens * width, bytes_accessed=16 * padded * tokens, transcendentals=0),
        name="head_logits",
    )(*slices, rows, col, *ready)


def head_back_kernel(table_ref, power_ref, peak_ref, col_ref, side_ref, *rest):
    d_ref, out_ref, acc = rest[-3:]
    j = pl.program_id(0)
    block, tokens = power_ref.shape
    part = block // 4
    away = col_ref[...] - j * block - lax.broadcasted_iota(jnp.int32, (8, tokens), 0)
    log_total, weight = side_ref[0:1, :], side_ref[1:2, :]
    pieces = []
    for q in range(4):
        factor = jnp.exp(peak_ref[q * 8 : (q + 1) * 8, :] - log_total) * weight
        for i in range(part // 8):
            at = q * part + 8 * i
            less = jnp.where(away == at, weight, 0.0)
            pieces.append(power_ref[at : at + 8, :] * factor - less)
    d = jnp.concatenate(pieces, axis=0).astype(BF)
    d_ref[...] = d
    product = dot(table_ref[...], d)

    @pl.when(j == 0)
    def _():
        acc[...] = product

    @pl.when(j > 0)
    def _():
        acc[...] += product

    @pl.when(j == pl.num_programs(0) - 1)
    def _():
        out_ref[...] = acc[...].T.astype(out_ref.dtype)


def head_back(table_t, powers, peaks, at, col, side, ready=()):
    width, vocab = table_t.shape
    tokens = col.shape[1]
    steps = peaks.shape[0] // 32
    block = vocab // steps
    return pl.pallas_call(
        head_back_kernel,
        grid=(steps,),
        in_specs=[
            pl.BlockSpec((width, block), lambda j: (0, j)),
            pl.BlockSpec((block, tokens), lambda j: (j, at)),
            pl.BlockSpec((32, tokens), lambda j: (j, at)),
            pl.BlockSpec((1, tokens), lambda j: (0, 0)),
            pl.BlockSpec((8, tokens), lambda j: (0, 0)),
        ]
        + [ANY] * len(ready),
        out_specs=[
            pl.BlockSpec((block, tokens), lambda j: (j, 0)),
            pl.BlockSpec((tokens, width), lambda j: (0, 0)),
        ],
        out_shape=[
            jax.ShapeDtypeStruct((vocab, tokens), BF),
            jax.ShapeDtypeStruct((tokens, width), BF),
        ],
        scratch_shapes=[pltpu.VMEM((width, tokens), F32)],
        compiler_params=pltpu.CompilerParams(vmem_limit_bytes=VMEM),
        cost_estimate=pl.CostEstimate(flops=4 * vocab * tokens * width, bytes_accessed=6 * vocab * tokens, transcendentals=0),
        name="head_back",
    )(table_t, powers, peaks, col, side, *ready)


def table_grad_kernel(count, *refs):
    d_refs, row_refs, out_refs = refs[: 2 * count], refs[2 * count : 3 * count], refs[-2:]
    total = None
    for k in range(count):
        both = jnp.concatenate([d_refs[2 * k][...], d_refs[2 * k + 1][...]], axis=0)
        product = dot(both, row_refs[k][...])
        total = product if total is None else total + product
    part = out_refs[0].shape[0]
    for q in range(2):
        out_refs[q][...] = total[q * part : (q + 1) * part].astype(out_refs[q].dtype)


def table_grad(ds, rows, padded, which, ready):
    width = rows[0].shape[1]
    part = part_rows(padded)

    def spec(tokens, q):
        return pl.BlockSpec((part, tokens), lambda j: (4 * j + q, 0))

    return pl.pallas_call(
        partial(table_grad_kernel, len(ds)),
        grid=(padded // part,),
        in_specs=[spec(d.shape[1], q) for d in ds for q in which]
        + [pl.BlockSpec(r.shape, lambda j: (0, 0)) for r in rows]
        + [ANY] * len(ready),
        out_specs=[pl.BlockSpec((part, width), lambda j: (j, 0))] * 2,
        out_shape=[jax.ShapeDtypeStruct((padded, width), t) for t in (F32, BF)],
        compiler_params=pltpu.CompilerParams(vmem_limit_bytes=VMEM),
        cost_estimate=pl.CostEstimate(
            flops=4 * padded * width * sum(d.shape[1] for d in ds),
            bytes_accessed=8 * padded * width,
            transcendentals=0,
        ),
        name="table_grad",
    )(*[d for d in ds for _ in which], *rows, *ready)


def finish_kernel(real, base_ref, place_ref, rows_ref, out_ref, square_ref):
    rows = base_ref.shape[0]
    first = pl.program_id(0) * rows
    at = lax.broadcasted_iota(jnp.int32, (rows, place_ref.shape[1]), 0) + first
    spread = dot((at == place_ref[...]).astype(BF), rows_ref[...])
    g = base_ref[...] + spread
    out_ref[...] = g
    inside = lax.broadcasted_iota(jnp.int32, g.shape, 0) + first < real
    g = jnp.where(inside, g, 0.0)
    squares = jnp.sum(g * g, axis=0, keepdims=True)

    @pl.when(pl.program_id(0) == 0)
    def _():
        square_ref[...] = squares

    @pl.when(pl.program_id(0) > 0)
    def _():
        square_ref[...] += squares


def finish(base, place, rows, real):
    padded, width = base.shape
    part = part_rows(padded)
    block = pl.BlockSpec((part, width), lambda j: (j, 0))
    return pl.pallas_call(
        partial(finish_kernel, real),
        grid=(padded // part,),
        in_specs=[
            block,
            pl.BlockSpec((1, place.shape[0]), lambda j: (0, 0)),
            pl.BlockSpec(rows.shape, lambda j: (0, 0)),
        ],
        out_specs=[block, pl.BlockSpec((1, width), lambda j: (0, 0))],
        out_shape=[
            jax.ShapeDtypeStruct((real, width), F32),
            jax.ShapeDtypeStruct((1, width), F32),
        ],
        compiler_params=pltpu.CompilerParams(vmem_limit_bytes=VMEM),
        cost_estimate=SHORT,
        name="finish",
    )(base, place[None, :], rows)


def adam_step(weight, first_moment, second_moment, gradient, step_rate, weight_decay):
    first_moment = BETA_ONE * first_moment + (1.0 - BETA_ONE) * gradient
    second_moment = BETA_TWO * second_moment + (1.0 - BETA_TWO) * gradient * gradient
    update = (
        first_moment
        / (1.0 - BETA_ONE**STEP)
        / (jnp.sqrt(second_moment / (1.0 - BETA_TWO**STEP)) + ADAM_EPS)
    )
    return (weight - step_rate * (update + weight_decay * weight), first_moment, second_moment)


def combine_stats(left, right):
    peak = jnp.maximum(left[0], right[0])
    total = left[1] * jnp.exp(left[0] - peak) + right[1] * jnp.exp(right[0] - peak)
    return jnp.stack([peak, total, left[2] + right[2]])


def on_device(
    token_ids,
    target_ids,
    doc_segments,
    hash_experts,
    embed_table,
    embed_first,
    embed_second,
    attn_in,
    attn_in_first,
    attn_in_second,
    attn_out,
    attn_out_first,
    attn_out_second,
    expert_in,
    expert_in_first,
    expert_in_second,
    expert_out,
    expert_out_first,
    expert_out_second,
    norm_gains,
    gains_first,
    gains_second,
):
    n_expert = lax.axis_size("expert")
    n_hidden = lax.axis_size("hidden")
    assert n_hidden == 4 and token_ids.shape[0] == 1
    e_index = lax.axis_index("expert")
    h_index = lax.axis_index("hidden")
    tok_count = token_ids.shape[1]
    vocab_rows, model_width = embed_table.shape
    embed_scale = model_width**0.5
    ids = token_ids[0]
    targets = target_ids[0]
    segment = doc_segments[0]
    token_at = jnp.arange(tok_count, dtype=jnp.int32)

    padded = round_up(vocab_rows, 32)
    own_rows = attn_in.shape[0]
    head_width = attn_in.shape[2]

    slots = round_up(5 * tok_count // (4 * n_expert * n_hidden), 8)
    shard = ids // vocab_rows
    shard_e, shard_h = shard // n_hidden, shard % n_hidden
    same_id = ids[:, None] == ids[None, :]
    first_at = jnp.min(jnp.where(same_id, token_at[None, :], tok_count), axis=1)
    is_first = first_at == token_at
    rank = jnp.sum(
        (
            (shard[:, None] == shard[None, :])
            & is_first[None, :]
            & (token_at[None, :] < first_at[:, None])
        ).astype(jnp.int32),
        axis=1,
    )
    overflow = jnp.max(rank) >= slots
    place_own = jnp.where(
        (shard_h == h_index) & (rank < slots), shard_e * slots + rank, -1
    )
    wanted = jnp.max(
        jnp.where(
            jnp.arange(n_expert * slots, dtype=jnp.int32)[:, None] == place_own[None, :],
            (ids % vocab_rows)[None, :],
            -1,
        ),
        axis=1,
    )
    own_gains = norm_gains.astype(BF).astype(F32).T.reshape(1, 3 * own_rows)
    own_gains = jnp.pad(own_gains, ((0, 0), (0, round_up(3 * own_rows, 128) - 3 * own_rows)))
    asked = jnp.concatenate(
        [
            wanted.reshape(n_expert, slots).astype(F32),
            jnp.broadcast_to(overflow.astype(F32), (n_expert, 128 - slots)),
            jnp.broadcast_to(own_gains, (n_expert, own_gains.shape[1])),
        ],
        axis=1,
    )

    asked = lax.all_to_all(asked, "expert", split_axis=0, concat_axis=0, tiled=True)
    any_overflow = jnp.max(asked[:, slots:128]) > 0
    asked_rows = asked[:, :slots].astype(jnp.int32).reshape(n_expert * slots)
    gain_full = asked[:, 128 : 128 + 3 * own_rows].reshape(n_expert, 3, own_rows)
    gain_full = gain_full.transpose(1, 0, 2).reshape(3, model_width)

    capacity = 3 * tok_count // (2 * n_expert)
    quarter = capacity // n_hidden
    expert_ids = hash_experts[ids]
    onehot = (expert_ids[:, None] == jnp.arange(n_expert, dtype=jnp.int32)).astype(jnp.int32)
    before = jnp.cumsum(onehot, axis=0) - onehot
    slot_rank = jnp.sum(before * onehot, axis=1)
    kept = slot_rank < capacity
    slot_h = slot_rank // quarter
    slot_in = expert_ids * quarter + slot_rank % quarter
    rows_dev = n_expert * quarter
    fill_place = jnp.where(kept & (slot_h == h_index), slot_in, -1)
    pick_place = jnp.where(kept, piece_of(slot_h ^ h_index) * rows_dev + slot_in, -1)

    asked_rows = jnp.where(any_overflow, -1, asked_rows)
    table_own, answer = cast_pick(asked_rows, embed_table, padded)
    packed = pack(attn_in, attn_out, (asked_rows,))
    packed = jnp.stack([packed, flip(packed, "hidden", 2)])
    packed = lax.all_gather(packed, "expert", axis=1, tiled=True)
    weights_own = jnp.stack([expert_in[0], expert_out[0]]).astype(BF)

    n_all = n_expert * n_hidden
    own_shard = e_index * n_hidden + h_index
    everyone = [(j, (j + 1) % n_all) for j in range(n_all)]

    answer = lax.all_to_all(
        answer.reshape(n_expert, slots, model_width),
        "expert",
        split_axis=0,
        concat_axis=0,
        tiled=True,
    )
    answers = hidden_gather(answer.reshape(n_expert * slots, model_width))
    place_all = piece_of(shard_h ^ h_index) * (n_expert * slots) + shard_e * slots + rank

    def look_up_step(k, carry):
        table_far, found = carry
        here = (own_shard - k + n_all) % n_all
        place = jnp.where(shard == here, ids % vocab_rows, -1)
        row = dot(hot_columns(place, padded), table_far).astype(BF)
        row = jnp.pad(row, ((0, 4 * n_expert * slots - tok_count), (0, 0)))
        parts = row.reshape(4, n_expert * slots, model_width)
        found = [jnp.where(k == 0, 0, found[q]) + parts[q] for q in range(4)]
        return lax.ppermute(table_far, ("expert", "hidden"), everyone), found

    answers = lax.fori_loop(
        0, jnp.where(any_overflow, n_all, 0), look_up_step, (table_own, answers)
    )[1]
    place_all = jnp.where(any_overflow, token_at, place_all)
    embedded, normed_one = pick_norm(
        (place_all, *answers), None, gain_full[0:1], embed_scale, ready=(fill_place, pick_place[:, None])
    )

    qkv, attended, attn_part = attend(normed_one, packed, head_width, segment, ())
    after_attn, normed_two = pick_norm(
        (attn_part, flip(attn_part, "hidden", 1)),
        embedded,
        gain_full[1:2],
        pick=False,
    )

    fill_hot = hot_rows(fill_place, rows_dev)

    def to_expert(rows_in, after=None):
        block = dot(fill_hot, rows_in).astype(BF)
        if after is not None:
            block = behind(block, after)
        return lax.all_to_all(block, "expert", split_axis=0, concat_axis=0, tiled=True)

    def from_expert(rows_in, after=None):
        block = lax.all_to_all(rows_in, "expert", split_axis=0, concat_axis=0, tiled=True)
        return hidden_gather(block.reshape(rows_dev, model_width), after)

    received = to_expert(normed_two)
    weights_y, _ = far_flip(weights_own, "hidden", 2, received[0, 0])
    expert_w = [
        weights_own,
        weights_y,
        flip(weights_own, "hidden", 1),
        flip(weights_y, "hidden", 1),
    ]
    expert_result, active, slope = expert(received, expert_w)
    after_moe, final_rows = pick_norm(
        (pick_place, *from_expert(expert_result)),
        after_attn,
        gain_full[2:3],
    )

    slice_x, _ = far_flip(table_own, "expert", 1, final_rows[0, 0])
    slices = [table_own, slice_x, flip(table_own, "hidden", 1), flip(slice_x, "hidden", 1)]
    table_t = turned(slices)
    part = part_rows(padded)

    half, fourth = tok_count // 2, tok_count // 4
    own_at = (h_index & 1) * half + (h_index >> 1) * fourth
    other_at = (h_index & 1) * half + (1 - (h_index >> 1)) * fourth
    n_far = n_expert // 2

    def own_order(x):
        return jnp.concatenate(
            [
                lax.dynamic_slice_in_dim(x, own_at, fourth, x.ndim - 1),
                lax.dynamic_slice_in_dim(x, other_at, fourth, x.ndim - 1),
            ],
            axis=-1,
        )

    counts = jnp.sum((segment[:, None] == segment[None, :]).astype(F32), axis=1)
    weights = 1.0 / counts / (n_expert * DOCS_ROW)
    about = own_order(jnp.stack([targets.astype(F32), weights]))
    about_all = [about] + [flip(about, "expert", 2 * k) for k in range(1, n_far)]
    own_part = lax.dynamic_slice_in_dim(final_rows, own_at, fourth, 0)
    other_part = lax.dynamic_slice_in_dim(final_rows, other_at, fourth, 0)
    far_rows = [flip(own_part, "expert", 2 * k) for k in range(1, n_far)]

    columns = []
    for k in range(n_far):
        target = about_all[k][0].astype(jnp.int32)
        block_of = target // vocab_rows
        away_e = (block_of // n_hidden) ^ e_index
        away_h = (block_of % n_hidden) ^ h_index
        mine = (away_e < 2) & (away_h < 2)
        row_of = target % vocab_rows
        column = (row_of // part) * (4 * part) + (away_e + 2 * away_h) * part + row_of % part
        columns.append(jnp.where(mine, column, -1)[None, :])
    head_rows, onward = [jnp.concatenate([own_part, other_part])], []
    powers, stats = [], []
    for k, far in enumerate(far_rows, 1):
        onward.append(behind(far, table_t[0, 0].astype(F32)) if k > 1 else far)
        head_rows.append(jnp.concatenate([onward[-1], flip(onward[-1], "hidden", 2)]))
    for k in range(0, n_far, 2):
        one, two, stat = head_logits(
            slices,
            jnp.concatenate(head_rows[k : k + 2]),
            jnp.concatenate(columns[k : k + 2], axis=1),
            vocab_rows,
            () if k else (table_t, *onward[1:]),
        )
        powers.append((one, two))
        stats += [stat[:3, :half], stat[:3, half:]]
    stat = jnp.stack(stats, axis=1)
    across = flip(stat, "hidden", 2)
    stat = combine_stats(stat, jnp.concatenate([across[..., fourth:], across[..., :fourth]], axis=2))
    far_stats = [flip(stat, "expert", 2 * k) for k in range(1, n_far)]
    for k in range(1, n_far):
        far = jnp.stack([far_stats[k - 1][:, j ^ k] for j in range(n_far)], axis=1)
        stat = combine_stats(stat, far)
    log_total = stat[0] + jnp.log(stat[1])
    loss_part = jnp.sum((log_total[0] - stat[2, 0]) * about[1])

    groups = [[0], [1]] + [[k, k + 1] for k in range(2, n_far, 2)]
    group_rows = [jnp.concatenate([head_rows[k] for k in group]) for group in groups]
    d_logits, d_parts, on_y = [None] * len(groups), [None] * n_far, []
    for i in range(len(groups) - 1, -1, -1):
        group = groups[i]
        wide_weights = jnp.concatenate([about_all[k][1] for k in group])
        wide_totals = jnp.concatenate([log_total[k] for k in group])
        side = jnp.stack([wide_totals, wide_weights] + [jnp.zeros_like(wide_totals)] * 6)
        d_logits[i], product = head_back(
            table_t,
            *powers[group[0] // 2],
            group[0] % 2,
            jnp.concatenate([columns[k] for k in group], axis=1),
            side,
            on_y[-3:-2] if i == 0 else (),
        )
        for g in reversed(range(len(group))):
            k, one = group[g], product[g * half : (g + 1) * half]
            gathered = one[:fourth].astype(F32) + flip(one[fourth:], "hidden", 2).astype(F32)
            if k:
                on_y.append(gathered.astype(BF))
                gathered = flip(on_y[-1], "expert", 2 * k).astype(F32)
            d_parts[k] = gathered
    d_quarter = sum(d_parts)
    d_quarter = d_quarter.astype(BF)
    d_four = hidden_gather(d_quarter)
    quarter_h = jnp.array([0, 2, 1, 3], jnp.int32)

    d_gain_three, d_result, d_after_moe = norm_back(
        after_moe,
        gain_full[2:3],
        (piece_of(quarter_h ^ h_index), *d_four),
        pick="blocks",
    )
    d_across = table_grad(d_logits, group_rows, padded, (1, 3), (d_result,))
    across_x = (d_across[0] + flip(d_across[1], "hidden", 1).astype(F32)).astype(BF)
    grad_in = to_expert(d_result, across_x[0, 0].astype(F32))
    d_received, *d_pre = expert_back(grad_in, expert_w, slope, ())
    d_w = [
        (dot(received, d_pre[p], 0, 0), dot(active[p], grad_in, 0, 0)) for p in range(4)
    ]
    d_same = table_grad(d_logits, group_rows, padded, (0, 2), (d_received,))

    base_x, both_x = far_flip(across_x, "expert", 1)
    d_base = d_same[0] + flip(d_same[1], "hidden", 1).astype(F32) + base_x.astype(F32)

    w_near = flip(d_w[3], "hidden", 1), flip(jnp.stack(d_w[2]), "hidden", 1)
    w_sent = jnp.stack([d_w[1][i] + w_near[0][i] for i in range(2)]).astype(BF)
    d_gain_two, d_branch, d_after_attn = norm_back(
        after_attn,
        gain_full[1:2],
        (pick_place, *from_expert(d_received, d_same[0][0, 0])),
        d_after_moe,
        pick="rows",
        ready=(w_sent,),
    )

    d_qkv, d_norm_part = attend_back(d_branch, packed, qkv, segment, (both_x,))
    d_gain_one, d_high, d_low = norm_back(
        embedded,
        gain_full[0:1],
        [d_norm_part, flip(d_norm_part, "hidden", 1)],
        d_after_attn,
        scale=embed_scale,
        split=True,
    )

    attn_sent = attn_grad(normed_one, d_qkv, d_branch, attended, (d_high,))

    d_rows = gathered_rows(place_own, d_high, d_low, n_expert * slots)
    d_gains = jnp.concatenate([d_gain_one, d_gain_two, d_gain_three])
    d_gains = d_gains.reshape(3, n_expert, own_rows).transpose(1, 0, 2).reshape(n_expert, 1, -1)
    gains_high = lax.reduce_precision(d_gains, 8, 7)
    gains_two = jnp.concatenate([gains_high, d_gains - gains_high], axis=1).astype(BF)
    gains_two = jnp.pad(gains_two, ((0, 0), (0, 14), (0, model_width - gains_two.shape[2])))
    attn_got = lax.all_to_all(
        attn_sent.reshape(n_expert, own_rows, 4 * head_width),
        "expert",
        split_axis=0,
        concat_axis=0,
        tiled=True,
    )
    sent = jnp.concatenate(
        [d_rows.reshape(n_expert, slots, model_width), gains_two], axis=1
    )
    got = lax.all_to_all(sent, "expert", split_axis=0, concat_axis=0, tiled=True)
    got_rows = got[:, :slots].reshape(n_expert * slots, model_width)

    def scatter_step(k, carry):
        d_far, ids_far, total = carry
        here = ids_far // vocab_rows == own_shard
        local = jnp.where(here, ids_far % vocab_rows, 0)
        d_sum = d_far[0].astype(F32) + d_far[1].astype(F32)
        total = total.at[local].add(jnp.where(here[:, None], d_sum, 0.0))
        ring = [(j, (j + 1) % n_expert) for j in range(n_expert)]
        return lax.ppermute(d_far, "expert", ring), lax.ppermute(ids_far, "expert", ring), total

    d_base = lax.fori_loop(
        0,
        jnp.where(any_overflow, n_expert, 0),
        scatter_step,
        ((d_high, d_low), ids, d_base),
    )[2]
    g_table, table_squares = finish(d_base, asked_rows, got_rows, vocab_rows)
    g_attn = jnp.sum(attn_got.astype(F32), axis=0)
    g_attn_in = g_attn[:, : 3 * head_width].reshape(own_rows, 3, head_width)
    g_attn_out = g_attn[:, 3 * head_width :]
    g_gains = jnp.sum(got[:, slots : slots + 2, : 3 * own_rows].astype(F32), axis=(0, 1))
    g_gains = g_gains.reshape(3, own_rows).T
    w_far, _ = far_flip(w_sent, "hidden", 2, table_squares[0, 0])
    g_expert = jnp.stack(d_w[0]) + w_near[1] + w_far.astype(F32)
    g_expert_in = g_expert[0][None]
    g_expert_out = g_expert[1][None]

    squares = (
        jnp.sum(table_squares)
        + jnp.sum(g_attn * g_attn)
        + jnp.sum(g_expert * g_expert)
        + jnp.sum(g_gains * g_gains) / n_hidden
    )
    both_sums = jnp.stack([squares, loss_part * (2.0 / n_hidden)])
    both_sums = jnp.broadcast_to(jnp.pad(both_sums, (0, 126))[None], (n_expert, 128))
    both_sums = lax.all_to_all(both_sums, "expert", split_axis=0, concat_axis=0, tiled=True)
    both_sums = lax.all_gather(jnp.sum(both_sums, axis=0), "hidden", axis=0)
    both_sums = jnp.sum(both_sums, axis=0)
    clip_norm = jnp.sqrt(both_sums[0])
    loss_value = both_sums[1]
    clip_scale = jnp.minimum(1.0, CLIP_AT / clip_norm)
    table_up = adam_step(
        embed_table, embed_first, embed_second, g_table * clip_scale, RATE_MATRIX, DECAY
    )
    attn_in_up = adam_step(
        attn_in, attn_in_first, attn_in_second, g_attn_in * clip_scale, RATE_MATRIX, DECAY
    )
    attn_out_up = adam_step(
        attn_out, attn_out_first, attn_out_second, g_attn_out * clip_scale, RATE_MATRIX, DECAY
    )
    expert_in_up = adam_step(
        expert_in,
        expert_in_first,
        expert_in_second,
        g_expert_in * clip_scale,
        RATE_MATRIX,
        DECAY,
    )
    expert_out_up = adam_step(
        expert_out,
        expert_out_first,
        expert_out_second,
        g_expert_out * clip_scale,
        RATE_MATRIX,
        DECAY,
    )
    gains_up = adam_step(
        norm_gains, gains_first, gains_second, g_gains * clip_scale, RATE_GAIN, 0.0
    )
    return (
        loss_value,
        clip_norm,
        *table_up,
        *attn_in_up,
        *attn_out_up,
        *expert_in_up,
        *expert_out_up,
        *gains_up,
    )


def solution(mesh):
    rows = P("expert", None)
    table = P(("expert", "hidden"), None)
    wide = P("expert", None, "hidden")
    flat = P("expert", "hidden")
    tall = P("expert", "hidden", None)
    groups = (table, wide, flat, wide, tall, rows)
    each = tuple(spec for spec in groups for _ in range(3))
    return jax.shard_map(
        on_device,
        mesh=mesh,
        in_specs=(rows, rows, rows, P(), *each),
        out_specs=(P(), P(), *each),
        check_vma=False,
    )
```
